32 devices in a mesh: fsdp: 2 (over x), blk: 16 (over z, y, core).
Axes of the slice: x: 2, y: 2, z: 4, core: 2. Of those that a mesh axis runs over, the one named last changes fastest.
Arguments:
- question_activations: bfloat16 [64, 64, 768], P(('fsdp', 'blk')), may hold values from -6 to 6
- passage_activations: bfloat16 [64, 768, 768], P(('fsdp', 'blk')), may hold values from -6 to 6
- question_unpadded_counts: int32 [64], P(('fsdp', 'blk')), may hold values from 8 to 64, as said below
- passage_unpadded_counts: int32 [64], P(('fsdp', 'blk')), may hold values from 96 to 768, as said below
- correct_passage_index: int32 [64], P(('fsdp', 'blk')), may hold values from 0 to 63, each once
- query_weights: float32 [64], P(('fsdp', 'blk')), may hold values from 0.5 to 8.4
- softness_factor: float32 [1], replicated, may hold values from 0.1 to 0.2
- combined_projection_matrix: bfloat16 [768, 2304], P('fsdp'), may hold values from -0.21875 to 0.21875
- mixing_result_matrix: bfloat16 [768, 768], P('fsdp'), may hold values from -0.875 to 0.875
- gating_matrix: bfloat16 [768, 3072], P('fsdp'), may hold values from -0.21875 to 0.21875
- widening_matrix: bfloat16 [768, 3072], P('fsdp'), may hold values from -0.21875 to 0.21875
- narrowing_matrix: bfloat16 [3072, 768], P('fsdp'), may hold values from -0.109375 to 0.109375
- initial_layernorm_scale: bfloat16 [768], P('fsdp'), may hold values from 0.5 to 1.5
- initial_layernorm_shift: bfloat16 [768], P('fsdp'), may hold values from -0.59765625 to 0.59765625
- later_layernorm_scale: bfloat16 [768], P('fsdp'), may hold values from 0.5 to 1.5
- later_layernorm_shift: bfloat16 [768], P('fsdp'), may hold values from -0.59765625 to 0.59765625
Outputs:
- loss: float32 [1], replicated
- grad_queries: float32 [64, 64, 768], P(('fsdp', 'blk'))
- grad_documents: float32 [64, 768, 768], P(('fsdp', 'blk'))
- grad_qkv: float32 [768, 2304], P('fsdp')
- grad_out: float32 [768, 768], P('fsdp')
- grad_gate: float32 [768, 3072], P('fsdp')
- grad_up: float32 [768, 3072], P('fsdp')
- grad_down: float32 [3072, 768], P('fsdp')
- grad_norm1_gain: float32 [768], P('fsdp')
- grad_norm1_bias: float32 [768], P('fsdp')
- grad_norm2_gain: float32 [768], P('fsdp')
- grad_norm2_bias: float32 [768], P('fsdp')
The draws below stay inside these ranges and needn't reach their ends.
Inputs may be any that keep to these rules, and one draw needn't show every extreme that they name: `question_unpadded_counts`: some query has exactly 64 tokens and some exactly 8. `passage_unpadded_counts`: some document has exactly 768 tokens and some exactly 96. `correct_passage_index`: each document index appears once.
All inputs are finite; a program needn't handle non-finite values.
Results may differ from the reference program's by a relative error of at most 0.028.
Values may be sent and summed in bfloat16 or wider, within the bound.
No kernel may reach another device: no remote copies, remote signals or barrier semaphores. Data moves between devices by JAX's collectives and lax.ppermute only.
A program may use at most 320 MiB of HBM per device.

```python
import jax
import jax.numpy as jnp
from jax import lax

D = 768
HEADS = 12
HEAD_DIM = 64
FF = 3072
QLEN = 64
DOC_LEN = 768
PAIRS = 64


def spread_lengths(key, members, longest, shortest):
    first_key, second_key = jax.random.split(key)
    values = jax.random.randint(first_key, (members,), shortest, longest + 1)
    chosen = jax.random.permutation(second_key, members)
    values = values.at[chosen[0]].set(longest)
    values = values.at[chosen[1]].set(shortest)
    return values.astype(jnp.int32)


def draw_question_unpadded_counts(key, part):
    key = jax.random.fold_in(key, 5)
    return spread_lengths(key, PAIRS, QLEN, max(QLEN // 8, 1))


def draw_passage_unpadded_counts(key, part):
    key = jax.random.fold_in(key, 9)
    return spread_lengths(key, PAIRS, DOC_LEN, max(DOC_LEN // 8, 1))


def rising_weights(key, members, ratio, wobble):
    position = jnp.arange(members, dtype=jnp.float32) / max(members - 1, 1)
    jitter = jax.random.uniform(key, (members,), jnp.float32, 1.0 - wobble, 1.0 + wobble)
    return (ratio ** position * jitter).astype(jnp.float32)


def draw_query_weights(key, part):
    key = jax.random.fold_in(key, 13)
    return rising_weights(key, PAIRS, 4.0, 0.25)


def levels(own_key, extent, cuts, low, largest):
    factor_of, own = 1.0, jax.random.fold_in(own_key, 6)
    for dim, parts in cuts:
        steps = jnp.exp(jax.random.uniform(jax.random.fold_in(own, dim), (parts,), jnp.float32, low / len(cuts), largest / len(cuts)))
        factor_of = factor_of * jnp.repeat(steps, extent[dim] // parts).reshape([-1 if axis == dim else 1 for axis in range(len(extent))])
    return factor_of


def scatter_about(stream_key, shape, deviation, limit, cuts=(), kind=jnp.bfloat16):
    entries = deviation * jax.random.normal(stream_key, shape, jnp.float32)
    if cuts:
        entries = entries * levels(stream_key, shape, cuts, -0.22, 0.18)
    return jnp.clip(entries, -limit, limit).astype(kind)


def setup_inputs(seed: int = 0) -> dict:
    arg_keys = jax.random.split(jax.random.key(seed), 17)
    return {
        "question_activations": scatter_about(arg_keys[0], (PAIRS, QLEN, D), 1.0, 6.0, ((0, 32),)),
        "passage_activations": scatter_about(arg_keys[1], (PAIRS, DOC_LEN, D), 1.0, 6.0, ((0, 32),)),
        "question_unpadded_counts": draw_question_unpadded_counts(jax.random.fold_in(arg_keys[16], 71), 0),
        "passage_unpadded_counts": draw_passage_unpadded_counts(jax.random.fold_in(arg_keys[16], 71), 0),
        "correct_passage_index": jax.random.permutation(arg_keys[4], PAIRS).astype(jnp.int32),
        "query_weights": draw_query_weights(jax.random.fold_in(arg_keys[16], 71), 0),
        "softness_factor": jnp.clip(jax.random.uniform(arg_keys[6], (1,), jnp.float32, 0.1, 0.2), 0.1, 0.2),
        "combined_projection_matrix": scatter_about(arg_keys[7], (D, 3 * D), D ** -0.5, 0.21875, ((0, 2),)),
        "mixing_result_matrix": scatter_about(arg_keys[8], (D, D), (D // 16) ** -0.5, 0.875, ((0, 2),)),
        "gating_matrix": scatter_about(arg_keys[9], (D, FF), D ** -0.5, 0.21875, ((0, 2),)),
        "widening_matrix": scatter_about(arg_keys[10], (D, FF), D ** -0.5, 0.21875, ((0, 2),)),
        "narrowing_matrix": scatter_about(arg_keys[11], (FF, D), FF ** -0.5, 0.109375, ((0, 2),)),
        "initial_layernorm_scale": jnp.clip(1.0 + 0.1 * jax.random.normal(arg_keys[12], (D,), jnp.float32), 0.5, 1.5).astype(jnp.bfloat16),
        "initial_layernorm_shift": scatter_about(arg_keys[13], (D,), 0.1, 0.59765625, ((0, 2),)),
        "later_layernorm_scale": jnp.clip(1.0 + 0.1 * jax.random.normal(arg_keys[14], (D,), jnp.float32), 0.5, 1.5).astype(jnp.bfloat16),
        "later_layernorm_shift": scatter_about(arg_keys[15], (D,), 0.1, 0.59765625, ((0, 2),)),
    }


@jax.custom_vjp
def low(v):
    return lax.optimization_barrier(v.astype(jnp.bfloat16)).astype(jnp.float32)

@jax.custom_vjp
def low_back(v):
    return v

def low_keep(v):
    return (low(v), None)

def low_pass(kept, grad):
    return (grad,)

def back_keep(v):
    return (v, None)

def back_low(kept, grad):
    return (low(grad),)
low.defvjp(low_keep, low_pass)
low_back.defvjp(back_keep, back_low)
EPS_NORM = 1e-05
EPS_UNIT = 1e-06
MASKED = -1e+30
HIGHEST = lax.Precision.HIGHEST

def matmul(left, right):
    return jnp.dot(left, right, precision=HIGHEST, preferred_element_type=jnp.float32)

def rotary(tensor, length):
    halfway = tensor.shape[-1] // 2
    frequency = 1000.0 ** (-(jnp.arange(halfway, dtype=jnp.float32) * 2.0 / tensor.shape[-1]))
    angles = jnp.arange(length, dtype=jnp.float32)[:, None] * frequency[None, :]
    cosine_table = jnp.cos(angles)[:, None, :]
    sine_table = jnp.sin(angles)[:, None, :]
    front_half = tensor[..., :halfway]
    back_half = tensor[..., halfway:]
    return jnp.concatenate([front_half * cosine_table - back_half * sine_table, back_half * cosine_table + front_half * sine_table], axis=-1)

def layer_norm(summed, norm_gain, norm_bias):
    centered = summed - lax.optimization_barrier(jnp.mean(summed, axis=-1, keepdims=True))
    variance = lax.optimization_barrier(jnp.mean(centered * centered, axis=-1, keepdims=True))
    return centered * lax.rsqrt(variance + EPS_NORM) * norm_gain + norm_bias

def encode(tokens, valid_len, weights):
    combined_projection_matrix, mixing_result_matrix, gating_matrix, widening_matrix, narrowing_matrix, gain_one, bias_one, gain_two, bias_two = weights
    length = tokens.shape[0]
    merged_qkv = low_back(matmul(tokens, combined_projection_matrix))
    query_rot = low(rotary(merged_qkv[:, :D].reshape(length, HEADS, HEAD_DIM), length))
    key_rot = low(rotary(merged_qkv[:, D:2 * D].reshape(length, HEADS, HEAD_DIM), length))
    value_heads = low(merged_qkv[:, 2 * D:].reshape(length, HEADS, HEAD_DIM))
    scores = low_back(jnp.einsum('qhd,khd->hqk', query_rot, key_rot, precision=HIGHEST) * HEAD_DIM ** (-0.5))
    valid_keys = jnp.arange(length) < valid_len
    scores = jnp.where(valid_keys[None, None, :], scores, MASKED)
    attn_probs = low(jax.nn.softmax(scores, axis=-1))
    attended = low(low_back(jnp.einsum('hqk,khd->qhd', attn_probs, value_heads, precision=HIGHEST))).reshape(length, D)
    normed_one = layer_norm(tokens + low_back(matmul(attended, mixing_result_matrix)), gain_one, bias_one)
    normed_low = low(normed_one)
    gate_proj = low_back(matmul(normed_low, gating_matrix))
    up_proj = low_back(matmul(normed_low, widening_matrix))
    hidden = low(jax.nn.silu(gate_proj) * up_proj)
    normed_two = layer_norm(normed_one + low_back(matmul(hidden, narrowing_matrix)), gain_two, bias_two)
    keep_rows = valid_keys.astype(tokens.dtype)
    pooled = lax.optimization_barrier(jnp.sum(normed_two * keep_rows[:, None], axis=0)) / valid_len.astype(tokens.dtype)
    return low(pooled * lax.rsqrt(jnp.sum(pooled * pooled) + EPS_UNIT))

def reference(question_activations, passage_activations, question_unpadded_counts, passage_unpadded_counts, correct_passage_index, query_weights, softness_factor, combined_projection_matrix, mixing_result_matrix, gating_matrix, widening_matrix, narrowing_matrix, initial_layernorm_scale, initial_layernorm_shift, later_layernorm_scale, later_layernorm_shift):
    floats = tuple((holder.astype(jnp.float32) for holder in (question_activations, passage_activations, combined_projection_matrix, mixing_result_matrix, gating_matrix, widening_matrix, narrowing_matrix, initial_layernorm_scale, initial_layernorm_shift, later_layernorm_scale, later_layernorm_shift)))
    average_divisor = softness_factor[0]
    term_weights = query_weights.astype(jnp.float32)

    def forward(query_tok, doc_tok, *weights):
        encoder = jax.checkpoint(lambda packed: encode(packed[0], packed[1], weights))
        query_units = lax.map(encoder, (query_tok, question_unpadded_counts))
        doc_units = lax.map(encoder, (doc_tok, passage_unpadded_counts))
        similarity = matmul(query_units, doc_units.T) / average_divisor
        log_norm = jax.nn.logsumexp(similarity, axis=1)
        matched = jnp.take_along_axis(similarity, correct_passage_index[:, None], axis=1)[:, 0]
        return jnp.mean(term_weights * (log_norm - matched))
    loss_value, pullback = jax.vjp(forward, *floats)
    gradients = pullback(jnp.ones_like(loss_value))
    return (loss_value.reshape(1), gradients[0], gradients[1], gradients[2], gradients[3], gradients[4], gradients[5], gradients[6], gradients[7], gradients[8], gradients[9], gradients[10])
```

```python
import functools

import jax
import jax.numpy as jnp
import numpy as np
from jax import lax
from jax.experimental import pallas as pl
from jax.experimental.pallas import tpu as pltpu
from jax.sharding import PartitionSpec as P

HEAD = 64
BLOCK = 128
TILE = 256
EPS_NORM = 1e-05
EPS_UNIT = 1e-06
MASKED = -1e30
F32 = jnp.float32
BF16 = jnp.bfloat16
VMEM_LIMIT = 60 * 1024 * 1024
OFF0, OFF1, OFFQ, LEN0, LEN1, QLEN0, QLEN1, CNT0, CNT1, TILES, CORE, SIDE, ROW = range(13)


def dot(left, right, contract=((1,), (0,))):
    return lax.dot_general(left, right, (contract, ((), ())), preferred_element_type=F32)


def cost(flops, moved, exps=0):
    return pl.CostEstimate(flops=int(flops), bytes_accessed=int(moved), transcendentals=int(exps))


def params(**more):
    return pltpu.CompilerParams(vmem_limit_bytes=VMEM_LIMIT, **more)


def rotary_tables(doc_len, query_len):
    frequency = 1000.0 ** (-(np.arange(HEAD // 2, dtype=np.float32) * 2.0 / HEAD))
    positions = np.concatenate([np.arange(doc_len), np.arange(query_len), np.arange(query_len)])
    angles = positions.astype(np.float32)[:, None] * frequency.astype(np.float32)[None, :]
    cosine, sine = np.cos(angles), np.sin(angles)
    return (
        np.concatenate([cosine] * 4, axis=1).astype(np.float32),
        np.concatenate([-sine, sine, -sine, sine], axis=1).astype(np.float32),
    )


def swap_halves(pair):
    lane = lax.broadcasted_iota(jnp.int32, pair.shape, 1)
    return jnp.where(lane % HEAD < HEAD // 2, pltpu.roll(pair, 96, 1), pltpu.roll(pair, 32, 1))


def live(step, meta):
    return jnp.minimum(step, meta[TILES] - 1)


def tiled(columns, at=0):
    return pl.BlockSpec((TILE, columns), lambda i, m, *_: (live(i, m), at))


def while_live(kernel):
    @functools.wraps(kernel)
    def run(meta, *refs):
        @pl.when(pl.program_id(0) < meta[TILES])
        def _():
            kernel(meta, *refs)

    return run


def resident(shape):
    return pl.BlockSpec(shape, lambda *_: (0,) * len(shape), pipeline_mode=pl.Buffered(1))


@while_live
def qkv_kernel(meta, table_block, x_ref, w_ref, cos_ref, sin_ref, out_ref):
    tile = pl.program_id(0)
    x = x_ref[...]
    width = x.shape[1]
    for part in range(3):
        acc = dot(x, w_ref[:, part * width : (part + 1) * width])
        if part == 2:
            out_ref[:, 2 * width :] = acc.astype(BF16)
            continue
        scale = HEAD**-0.5 if part == 0 else 1.0
        for sub in range(TILE // BLOCK):
            rows = slice(sub * BLOCK, (sub + 1) * BLOCK)
            table = pl.ds(table_block[tile * (TILE // BLOCK) + sub] * BLOCK, BLOCK)
            cosine, sine = cos_ref[table, :] * scale, sin_ref[table, :] * scale
            for group in range(width // 128):
                pair = acc[rows, group * 128 : (group + 1) * 128]
                turned = pair * cosine + swap_halves(pair) * sine
                at = part * width + group * 128
                out_ref[rows, at : at + 128] = turned.astype(BF16)


def project(meta, table_block, x, weight, tables):
    rows, width = x.shape
    grid_spec = pltpu.PrefetchScalarGridSpec(
        num_scalar_prefetch=2,
        grid=(rows // TILE,),
        in_specs=[
            tiled(width),
            resident(weight.shape),
            resident(tables[0].shape),
            resident(tables[1].shape),
        ],
        out_specs=tiled(3 * width),
    )
    return pl.pallas_call(
        qkv_kernel,
        grid_spec=grid_spec,
        out_shape=jax.ShapeDtypeStruct((rows, 3 * width), BF16),
        compiler_params=params(),
        cost_estimate=cost(2 * rows * width * 3 * width, 8 * rows * width),
        name="qkv",
    )(meta, table_block, x, weight, *tables)


def split_pair(pair):
    lane = lax.broadcasted_iota(jnp.int32, pair.shape, 1)
    zero = jnp.zeros_like(pair)
    return jnp.concatenate(
        [jnp.where(lane < HEAD, pair, zero), jnp.where(lane < HEAD, zero, pair)], axis=0
    )


def mask_keys(scores, last, valid):
    rows = lax.broadcasted_iota(jnp.int32, (BLOCK, scores.shape[1]), 0)
    tail = jnp.where(rows < valid, scores[last * BLOCK :, :], MASKED)
    if last == 0:
        return tail
    return jnp.concatenate([scores[: last * BLOCK, :], tail], axis=0)


def query_mask(meta, scores):
    half = scores.shape[0] // 2
    key = lax.broadcasted_iota(jnp.int32, scores.shape, 0)
    row = lax.broadcasted_iota(jnp.int32, scores.shape, 1) % (2 * half)
    length = jnp.where(key < half, meta[QLEN0], meta[QLEN1])
    keep = ((key < half) == (row < half)) & (key % half < length)
    return jnp.where(keep, scores, MASKED)


def stack_heads(pair_wide):
    half = pair_wide.shape[1] // 2
    return jnp.concatenate([pair_wide[:, :half], pair_wide[:, half:]], axis=0)


def attend_kernel(meta, q_ref, k_ref, v_ref, out_ref, lse_ref):
    def tile_of(start, size, keys, values, masked):
        rows = pl.ds(start, size)
        queries = split_pair(q_ref[rows, :])
        scores = masked(dot(keys, queries, ((1,), (1,))))
        highest = jnp.max(scores, axis=0, keepdims=True)
        exponent = jnp.exp(scores - highest)
        total = jnp.sum(exponent, axis=0, keepdims=True)
        probs = (exponent * (1.0 / total)).astype(BF16)
        out_ref[rows, :] = dot(stack_heads(probs), values, ((0,), (0,))).astype(BF16)
        log_norm = highest + jnp.log(total)
        lse_ref[0, 0:1, rows] = log_norm[:, :size]
        lse_ref[0, 1:2, rows] = log_norm[:, size:]

    @pl.loop(0, 2)
    def _(doc):
        start = pl.multiple_of(meta[OFF0 + doc], BLOCK)
        for blocks in range(1, 7):

            @pl.when(meta[CNT0 + doc] == blocks)
            def _():
                keys = k_ref[pl.ds(start, blocks * BLOCK), :]
                values = split_pair(v_ref[pl.ds(start, blocks * BLOCK), :])
                valid = meta[LEN0 + doc] - (blocks - 1) * BLOCK

                @pl.loop(0, (blocks + 1) // 2)
                def _(step):
                    tile_of(
                        pl.multiple_of(start + step * TILE, BLOCK),
                        TILE,
                        keys,
                        values,
                        lambda scores: mask_keys(scores, blocks - 1, valid),
                    )

    first = pl.multiple_of(meta[OFFQ], BLOCK)
    rows = pl.ds(first, BLOCK)
    tile_of(first, BLOCK, k_ref[rows, :], split_pair(v_ref[rows, :]), functools.partial(query_mask, meta))
    out_ref[pl.ds(first + BLOCK, BLOCK), :] = jnp.zeros((BLOCK, 128), BF16)


def attend(meta, qkv):
    rows, width = qkv.shape[0], qkv.shape[1] // 3
    pairs = width // 128

    def column(part):
        return pl.BlockSpec((rows, 128), lambda h, *_: (0, part * pairs + h))

    grid_spec = pltpu.PrefetchScalarGridSpec(
        num_scalar_prefetch=1,
        grid=(pairs,),
        in_specs=[column(0), column(1), column(2)],
        out_specs=[column(0), pl.BlockSpec((1, 8, rows), lambda h, *_: (h, 0, 0))],
    )
    return pl.pallas_call(
        attend_kernel,
        grid_spec=grid_spec,
        out_shape=[
            jax.ShapeDtypeStruct((rows, width), BF16),
            jax.ShapeDtypeStruct((pairs, 8, rows), F32),
        ],
        compiler_params=params(),
        cost_estimate=cost(8 * rows * 500 * width, 8 * rows * width, rows * 6000),
        name="attend",
    )(meta, qkv, qkv, qkv)


def normalize(summed):
    centered = summed - jnp.mean(summed, axis=-1, keepdims=True)
    recip = lax.rsqrt(jnp.mean(centered * centered, axis=-1, keepdims=True) + EPS_NORM)
    return centered * recip, recip


@while_live
def forward_kernel(
    meta, counts, att_ref, x_ref, wo_ref, wg_ref, wu_ref, wd_ref, gain_ref, bias_ref,
    low_ref, z1_ref, r1_ref, silu_ref, slope_ref, hidden_ref, z2_ref, r2_ref, sums_ref,
):
    tile = pl.program_id(0)
    z1, r1 = normalize(x_ref[...].astype(F32) + dot(att_ref[...], wo_ref[...]))
    z1_ref[...] = z1.astype(BF16)
    r1_ref[...] = r1
    normed = z1 * gain_ref[...] + bias_ref[...]
    low = normed.astype(BF16)
    low_ref[...] = low
    total = normed
    inner, chunk = wg_ref.shape[1], 512
    for at in range(0, inner, chunk):
        columns = slice(at, at + chunk)
        gate = dot(low, wg_ref[:, columns])
        up = dot(low, wu_ref[:, columns])
        sigmoid = 1.0 / (1.0 + jnp.exp(-gate))
        silu = gate * sigmoid
        hidden = (silu * up).astype(BF16)
        silu_ref[:, columns] = silu.astype(BF16)
        slope_ref[:, columns] = (up * (sigmoid + silu * (1.0 - sigmoid))).astype(BF16)
        hidden_ref[:, columns] = hidden
        total = total + dot(hidden, wd_ref[columns, :])
    z2, r2 = normalize(total)
    z2_ref[...] = z2.astype(BF16)
    r2_ref[...] = r2
    half = BLOCK // 2
    inside = lax.broadcasted_iota(jnp.int32, (half, z2.shape[1]), 0)
    for group in range(TILE // half):
        valid = counts[tile * (TILE // half) + group]
        kept = jnp.where(inside < valid, z2[group * half : (group + 1) * half, :], 0.0)
        sums_ref[0, group : group + 1, :] = jnp.sum(kept, axis=0, keepdims=True)


def forward(meta, counts, att, x, wo, wg, wu, wd, gain, bias):
    rows, width = x.shape
    inner = wg.shape[1]

    def array(columns, kind):
        return jax.ShapeDtypeStruct((rows, columns), kind)

    grid_spec = pltpu.PrefetchScalarGridSpec(
        num_scalar_prefetch=2,
        grid=(rows // TILE,),
        in_specs=[tiled(width), tiled(width)]
        + [resident(w.shape) for w in (wo, wg, wu, wd, gain, bias)],
        out_specs=[
            tiled(width), tiled(width), tiled(1), tiled(inner), tiled(inner), tiled(inner),
            tiled(width), tiled(1), pl.BlockSpec((1, 4, width), lambda i, m, *_: (live(i, m), 0, 0)),
        ],
    )
    return pl.pallas_call(
        forward_kernel,
        grid_spec=grid_spec,
        out_shape=[
            array(width, BF16), array(width, BF16), array(1, F32), array(inner, BF16),
            array(inner, BF16), array(inner, BF16), array(width, BF16), array(1, F32),
            jax.ShapeDtypeStruct((rows // TILE, 4, width), F32),
        ],
        compiler_params=params(),
        cost_estimate=cost(2 * rows * width * (width + 3 * inner), rows * (inner * 6 + width * 12)),
        name="forward",
    )(meta, counts, att, x, wo, wg, wu, wd, gain, bias)


@while_live
def norm_two_back_kernel(meta, counts, owner, z_ref, r_ref, scaled_ref, branch_ref, out_ref):
    tile = pl.program_id(0)
    half = BLOCK // 2
    width = z_ref.shape[1]
    inside = lax.broadcasted_iota(jnp.int32, (half, width), 0)
    for group in range(TILE // half):
        at = tile * (TILE // half) + group
        rows = slice(group * half, (group + 1) * half)
        scaled = scaled_ref[pl.ds(owner[at], 1), :]
        z = z_ref[rows, :].astype(F32)
        plain = jnp.mean(scaled, axis=-1, keepdims=True)
        cross = jnp.mean(scaled * z, axis=-1, keepdims=True)
        grad = r_ref[rows, :] * (scaled - plain - z * cross)
        grad = jnp.where(inside < counts[at], grad, 0.0)
        branch_ref[rows, :] = grad.astype(BF16)
        out_ref[rows, :] = grad


def norm_two_back(meta, counts, owner, z, recip, scaled):
    rows, width = z.shape

    grid_spec = pltpu.PrefetchScalarGridSpec(
        num_scalar_prefetch=3,
        grid=(rows // TILE,),
        in_specs=[tiled(width), tiled(1), resident(scaled.shape)],
        out_specs=[tiled(width), tiled(width)],
    )
    return pl.pallas_call(
        norm_two_back_kernel,
        grid_spec=grid_spec,
        out_shape=[jax.ShapeDtypeStruct((rows, width), BF16), jax.ShapeDtypeStruct((rows, width), F32)],
        compiler_params=params(),
        cost_estimate=cost(10 * rows * width, rows * width * 8),
        name="norm_two_back",
    )(meta, counts, owner, z, recip, scaled)


@while_live
def ffn_back_kernel(
    meta, branch_ref, low_ref, hid0, hid1, silu0, silu1, slope0, slope1,
    wd0, wd1, wg0, wg1, wu0, wu1, first_in, first_out, keep_ref, send_ref, acc_g, acc_u, acc_d,
):
    tile = pl.program_id(0)
    span = wd0.shape[0]

    @pl.when(tile == 0)
    def _():
        acc_g[...] = jnp.zeros_like(acc_g)
        acc_u[...] = jnp.zeros_like(acc_u)
        acc_d[...] = jnp.zeros_like(acc_d)

    branch = branch_ref[...]
    low_t = low_ref[...].T
    branch_t = branch.T
    first = first_in[...]
    for half, (hid, silu, slope, wd, wg, wu) in enumerate(
        ((hid0, silu0, slope0, wd0, wg0, wu0), (hid1, silu1, slope1, wd1, wg1, wu1))
    ):
        columns = slice(half * span, (half + 1) * span)
        grad_hidden = dot(branch, wd[...], ((1,), (1,)))
        grad_gate = (grad_hidden * slope[...].astype(F32)).astype(BF16)
        grad_up = (grad_hidden * silu[...].astype(F32)).astype(BF16)
        first = first + dot(grad_gate, wg[...], ((1,), (1,))) + dot(grad_up, wu[...], ((1,), (1,)))
        acc_g[:, columns] += dot(low_t, grad_gate)
        acc_u[:, columns] += dot(low_t, grad_up)
        acc_d[:, columns] += dot(branch_t, hid[...])
    first_out[...] = first

    @pl.when(tile == meta[TILES] - 1)
    def _():
        rows, quarter = acc_g.shape[0] // 4, acc_g.shape[0] // 4
        side, row, core = meta[SIDE], meta[ROW], meta[CORE]
        for other_core, out in ((0, keep_ref), (1, send_ref)):
            columns = pl.ds(pl.multiple_of((core ^ other_core) * span, span), span)
            inner = pl.ds(
                pl.multiple_of((core ^ other_core) * (span // 2), span // 2), span // 2
            )
            for other_side in range(2):
                for other_row in range(2):
                    at = (side ^ other_side) * 2 + (row ^ other_row)
                    lines = pl.ds(pl.multiple_of(at * quarter, quarter), quarter)
                    out[other_side, other_row, 0] = acc_g[lines, columns].astype(BF16)
                    out[other_side, other_row, 1] = acc_u[lines, columns].astype(BF16)
                    left = pl.multiple_of(
                        (side ^ other_side) * span + (core ^ other_core) * (span // 2), span // 2
                    )
                    for part in range(2):
                        lines = pl.ds(
                            pl.multiple_of((row ^ other_row) * 2 * quarter + part * quarter, quarter),
                            quarter,
                        )
                        out[
                            other_side, other_row, 2, :, part * (span // 2) : (part + 1) * (span // 2)
                        ] = acc_d[lines, pl.ds(left, span // 2)].astype(BF16)


def ffn_back(meta, chunk, branch, low, hidden, silu, slope, wd, wg, wu, first):
    rows, width = low.shape
    inner = hidden.shape[1]
    span = 512
    halves = (chunk, chunk + inner // (2 * span))

    def fixed(shape, index):
        return pl.BlockSpec(shape, lambda i, *_: index, pipeline_mode=pl.Buffered(1))

    grid_spec = pltpu.PrefetchScalarGridSpec(
        num_scalar_prefetch=1,
        grid=(rows // TILE,),
        in_specs=[tiled(width), tiled(width)]
        + [tiled(span, at) for _ in range(3) for at in halves]
        + [fixed((span, width), (at, 0)) for at in halves]
        + [fixed((width, span), (0, at)) for _ in range(2) for at in halves]
        + [tiled(width)],
        out_specs=[tiled(width)]
        + [pl.BlockSpec((2, 2, 3, width // 4, span), lambda i, *_: (0, 0, 0, 0, 0))] * 2,
        scratch_shapes=[pltpu.VMEM((width, 2 * span), F32)] * 3,
    )
    piece = jax.ShapeDtypeStruct((2, 2, 3, width // 4, span), BF16)
    return pl.pallas_call(
        ffn_back_kernel,
        grid_spec=grid_spec,
        out_shape=[jax.ShapeDtypeStruct((rows, width), F32), piece, piece],
        input_output_aliases={15: 0},
        compiler_params=params(),
        cost_estimate=cost(12 * rows * width * 2 * span, rows * width * 16),
        name="ffn_back",
    )(
        meta, branch, low, hidden, hidden, silu, silu, slope, slope, wd, wd, wg, wg, wu, wu, first
    )


def out_pieces(meta, acc, keep_ref, send_ref):
    quarter, half = acc.shape[0] // 4, acc.shape[1] // 2
    side, row, core = meta[SIDE], meta[ROW], meta[CORE]
    for other_core, out in ((0, keep_ref), (1, send_ref)):
        columns = pl.ds(pl.multiple_of((core ^ other_core) * half, half), half)
        for other_side in range(2):
            for other_row in range(2):
                at = (side ^ other_side) * 2 + (row ^ other_row)
                lines = pl.ds(pl.multiple_of(at * quarter, quarter), quarter)
                out[other_side, other_row] = acc[lines, columns].astype(BF16)


@while_live
def norm_one_back_kernel(
    meta, first_ref, z_ref, r_ref, att_ref, gain_ref, wo_ref,
    sum_ref, att_grad_ref, gain_out, keep_ref, send_ref, acc,
):
    tile = pl.program_id(0)

    @pl.when(tile == 0)
    def _():
        acc[...] = jnp.zeros_like(acc)
        gain_out[...] = jnp.zeros_like(gain_out)

    first = first_ref[...]
    z = z_ref[...].astype(F32)
    scaled = first * gain_ref[...]
    plain = jnp.mean(scaled, axis=-1, keepdims=True)
    cross = jnp.mean(scaled * z, axis=-1, keepdims=True)
    grad = r_ref[...] * (scaled - plain - z * cross)
    sum_ref[...] = grad
    low = grad.astype(BF16)
    att_grad_ref[...] = dot(low, wo_ref[...], ((1,), (1,))).astype(BF16)
    acc[...] += dot(att_ref[...].T, low)
    gain_out[0:1, :] += jnp.sum(first * z, axis=0, keepdims=True)
    gain_out[1:2, :] += jnp.sum(first, axis=0, keepdims=True)

    @pl.when(tile == meta[TILES] - 1)
    def _():
        out_pieces(meta, acc, keep_ref, send_ref)


def norm_one_back(meta, first, z, recip, att, gain, wo):
    rows, width = z.shape

    block = (2, 2, width // 4, width // 2)
    piece = jax.ShapeDtypeStruct(block, BF16)
    grid_spec = pltpu.PrefetchScalarGridSpec(
        num_scalar_prefetch=1,
        grid=(rows // TILE,),
        in_specs=[tiled(width), tiled(width), tiled(1), tiled(width)]
        + [resident(gain.shape), resident(wo.shape)],
        out_specs=[
            tiled(width), tiled(width), pl.BlockSpec((8, width), lambda i, *_: (0, 0)),
            pl.BlockSpec(block, lambda i, *_: (0, 0, 0, 0)),
            pl.BlockSpec(block, lambda i, *_: (0, 0, 0, 0)),
        ],
        scratch_shapes=[pltpu.VMEM((width, width), F32)],
    )
    return pl.pallas_call(
        norm_one_back_kernel,
        grid_spec=grid_spec,
        out_shape=[
            jax.ShapeDtypeStruct((rows, width), F32), jax.ShapeDtypeStruct((rows, width), BF16),
            jax.ShapeDtypeStruct((8, width), F32), piece, piece,
        ],
        compiler_params=params(),
        cost_estimate=cost(4 * rows * width * width, rows * width * 14),
        name="norm_one_back",
    )(meta, first, z, recip, att, gain, wo)


def attend_back_kernel(meta, table_block, q_ref, k_ref, v_ref, g_ref, lse_ref, cos_ref, sin_ref, out_ref, key_acc, value_acc):
    def turn_back(grad, table):
        cosine, sine = cos_ref[table, :], sin_ref[table, :]
        return (grad * cosine - swap_halves(grad) * sine).astype(BF16)

    def tile_of(start, size, keys, values, keys_split, limit, masked):
        rows = pl.ds(start, size)
        queries, grads = split_pair(q_ref[rows, :]), split_pair(g_ref[rows, :])
        log_norm = jnp.concatenate([lse_ref[0, 0:1, rows], lse_ref[0, 1:2, rows]], axis=1)
        if limit is not None:
            column = lax.broadcasted_iota(jnp.int32, log_norm.shape, 1) % size
            log_norm = jnp.where(column < limit, log_norm, -MASKED)
        scores = masked(dot(keys, queries, ((1,), (1,))))
        probs = jnp.exp(scores - log_norm)
        grad_probs = dot(values, grads, ((1,), (1,)))
        inner = jnp.sum(probs * grad_probs, axis=0, keepdims=True)
        grad_scores = (probs * (grad_probs - inner)).astype(BF16)
        grad_query = dot(stack_heads(grad_scores), keys_split, ((0,), (0,))) * HEAD**-0.5
        return grad_query, dot(grad_scores, queries), dot(probs.astype(BF16), grads)

    @pl.loop(0, 2)
    def _(doc):
        start = pl.multiple_of(meta[OFF0 + doc], BLOCK)
        for blocks in range(1, 7):

            @pl.when(meta[CNT0 + doc] == blocks)
            def _():
                size = blocks * BLOCK
                whole = pl.ds(start, size)
                keys, values = k_ref[whole, :], v_ref[whole, :]
                keys_split = split_pair(keys)
                valid = meta[LEN0 + doc] - (blocks - 1) * BLOCK
                key_acc[:size, :] = jnp.zeros((size, 128), F32)
                value_acc[:size, :] = jnp.zeros((size, 128), F32)

                @pl.loop(0, (blocks + 1) // 2)
                def _(step):
                    at = pl.multiple_of(start + step * TILE, BLOCK)
                    grad_query, grad_key, grad_value = tile_of(
                        at, TILE, keys, values, keys_split, size - step * TILE,
                        lambda scores: mask_keys(scores, blocks - 1, valid),
                    )
                    key_acc[:size, :] += grad_key
                    value_acc[:size, :] += grad_value
                    for sub in range(2):
                        table = pl.ds((step * 2 + sub) * BLOCK, BLOCK)
                        out_ref[pl.ds(at + sub * BLOCK, BLOCK), 0:128] = turn_back(
                            grad_query[sub * BLOCK : (sub + 1) * BLOCK, :], table
                        )

                out_ref[whole, 128:256] = turn_back(key_acc[:size, :], pl.ds(0, size))
                out_ref[whole, 256:384] = value_acc[:size, :].astype(BF16)

    first = pl.multiple_of(meta[OFFQ], BLOCK)
    rows = pl.ds(first, BLOCK)
    keys = k_ref[rows, :]
    grad_query, grad_key, grad_value = tile_of(
        first, BLOCK, keys, v_ref[rows, :], split_pair(keys), None, functools.partial(query_mask, meta)
    )
    table = pl.ds(cos_ref.shape[0] - BLOCK, BLOCK)
    out_ref[rows, 0:128] = turn_back(grad_query, table)
    out_ref[rows, 128:256] = turn_back(grad_key, table)
    out_ref[rows, 256:384] = grad_value.astype(BF16)
    out_ref[pl.ds(first + BLOCK, BLOCK), :] = jnp.zeros((BLOCK, 384), BF16)


def attend_back(meta, table_block, group, members, qkv, grad, lse, tables):
    rows, width = grad.shape
    pairs = width // 128

    def column(part, columns=128):
        return pl.BlockSpec((rows, columns), lambda h, *_: (0, part * pairs + group * members + h))

    grid_spec = pltpu.PrefetchScalarGridSpec(
        num_scalar_prefetch=2,
        grid=(members,),
        in_specs=[
            column(0), column(1), column(2), column(0),
            pl.BlockSpec((1, 8, rows), lambda h, *_: (group * members + h, 0, 0)),
            resident(tables[0].shape), resident(tables[1].shape),
        ],
        out_specs=pl.BlockSpec((rows, 384), lambda h, *_: (0, h)),
        scratch_shapes=[pltpu.VMEM((6 * BLOCK, 128), F32)] * 2,
    )
    return pl.pallas_call(
        attend_back_kernel,
        grid_spec=grid_spec,
        out_shape=jax.ShapeDtypeStruct((rows, 384 * members), BF16),
        compiler_params=params(),
        cost_estimate=cost(20 * rows * 500 * 128 * members, 10 * rows * 128 * members, rows * 1000 * members),
        name="attend_back",
    )(meta, table_block, qkv, qkv, qkv, grad, lse, *tables)


@while_live
def qkv_grad_kernel(meta, x_ref, g_ref, keep_ref, send_ref, acc):
    tile = pl.program_id(0)

    @pl.when(tile == 0)
    def _():
        acc[...] = jnp.zeros_like(acc)

    acc[...] += dot(x_ref[...].T, g_ref[...])

    @pl.when(tile == meta[TILES] - 1)
    def _():
        out_pieces(meta, acc, keep_ref, send_ref)


def qkv_grad(meta, x, grad):
    rows, width = x.shape
    columns = grad.shape[1]
    block = (2, 2, width // 4, columns // 2)
    piece = jax.ShapeDtypeStruct(block, BF16)
    grid_spec = pltpu.PrefetchScalarGridSpec(
        num_scalar_prefetch=1,
        grid=(rows // TILE,),
        in_specs=[
            tiled(width),
            tiled(columns),
        ],
        out_specs=[pl.BlockSpec(block, lambda i, *_: (0, 0, 0, 0))] * 2,
        scratch_shapes=[pltpu.VMEM((width, columns), F32)],
    )
    return pl.pallas_call(
        qkv_grad_kernel,
        grid_spec=grid_spec,
        out_shape=[piece, piece],
        compiler_params=params(),
        cost_estimate=cost(2 * rows * width * columns, rows * (width + columns) * 2),
        name="qkv_grad",
    )(meta, x, grad)


def token_grad_kernel(members, meta, *refs):
    groups = 6 // members
    sums = refs[0:2]
    grads = [refs[2 + 2 * g : 4 + 2 * g] for g in range(groups)]
    weights = refs[2 + 2 * groups : 2 + 2 * groups + 18]
    docs_ref, queries_ref = refs[-2:]
    step = pl.program_id(0)
    doc, tile = step // 3, step % 3
    length = jnp.where(step < 6, meta[LEN0 + jnp.minimum(doc, 1)] - tile * TILE, TILE)

    def value():
        total = jnp.concatenate([sums[0][...], sums[1][...]], axis=0)
        for group in range(groups):
            grad = jnp.concatenate([grads[group][0][...], grads[group][1][...]], axis=0)
            chosen = []
            for member in range(members):
                pair = group * members + member
                chosen += [weights[3 * pair + part][...] for part in range(3)]
            total = total + dot(grad, jnp.concatenate(chosen, axis=1), ((1,), (1,)))
        return total

    @pl.when((step < 6) & (length > 0))
    def _():
        total = value()
        inside = lax.broadcasted_iota(jnp.int32, total.shape, 0)
        docs_ref[0] = jnp.where(inside < length, total, 0.0)

    @pl.when((step < 6) & (length <= 0))
    def _():
        docs_ref[...] = jnp.zeros_like(docs_ref)

    @pl.when(step == 6)
    def _():
        total = value()[:BLOCK, :]
        inside = lax.broadcasted_iota(jnp.int32, (BLOCK // 2, total.shape[1]), 0)
        for which in range(2):
            half = total[which * (BLOCK // 2) : (which + 1) * (BLOCK // 2), :]
            queries_ref[which] = jnp.where(inside < meta[QLEN0 + which], half, 0.0)


def token_grad(meta, sums, grads, weight, members):
    rows, width = sums.shape
    pairs = width // 128

    def block_of(step, meta, second):
        doc, tile = step // 3, step % 3
        last = jnp.where(doc == 0, meta[CNT0], meta[CNT1]) - 1
        in_doc = jnp.minimum(tile * 2 + second, last)
        base = jnp.where(doc == 0, meta[OFF0], meta[OFF1]) // BLOCK
        return jnp.where(step < 6, base + in_doc, meta[OFFQ] // BLOCK)

    def halves(columns):
        return [
            pl.BlockSpec((BLOCK, columns), lambda i, meta, s=s: (block_of(i, meta, s), 0)) for s in range(2)
        ]

    grid_spec = pltpu.PrefetchScalarGridSpec(
        num_scalar_prefetch=1,
        grid=(7,),
        in_specs=halves(width)
        + sum((halves(grad.shape[1]) for grad in grads), [])
        + [
            pl.BlockSpec(
                (width, 128), lambda i, meta, at=part * pairs + pair: (0, at), pipeline_mode=pl.Buffered(1)
            )
            for pair in range(pairs)
            for part in range(3)
        ],
        out_specs=[
            pl.BlockSpec((1, TILE, width), lambda i, meta: (jnp.minimum(i // 3, 1), jnp.where(i < 6, i % 3, 2), 0)),
            pl.BlockSpec((2, BLOCK // 2, width), lambda i, meta: (0, 0, 0)),
        ],
    )
    return pl.pallas_call(
        functools.partial(token_grad_kernel, members),
        grid_spec=grid_spec,
        out_shape=[
            jax.ShapeDtypeStruct((2, 6 * BLOCK, width), F32),
            jax.ShapeDtypeStruct((2, BLOCK // 2, width), F32),
        ],
        compiler_params=params(),
        cost_estimate=cost(6 * rows * width * width, rows * width * 14),
        name="token_grad",
    )(meta, sums, sums, *[g for grad in grads for g in (grad, grad)], *([weight] * (3 * pairs)))


def layout(doc_counts, query_counts, rows, core, side, row):
    blocks = (doc_counts + BLOCK - 1) // BLOCK
    offq = blocks[0] + blocks[1]
    tiles = (offq + 1 + 1) // 2
    meta = jnp.stack(
        [
            jnp.int32(0), blocks[0] * BLOCK, offq * BLOCK, doc_counts[0], doc_counts[1],
            query_counts[0], query_counts[1], blocks[0], blocks[1], tiles, core, side, row,
            jnp.int32(0), jnp.int32(0), jnp.int32(0),
        ]
    ).astype(jnp.int32)
    at = jnp.arange(rows // BLOCK, dtype=jnp.int32)
    in_first, in_second = at < blocks[0], (at >= blocks[0]) & (at < offq)
    table_block = jnp.where(in_first, at, jnp.where(in_second, at - blocks[0], 6))
    half = jnp.arange(rows // (BLOCK // 2), dtype=jnp.int32)
    start = half * (BLOCK // 2)
    first, second = start < blocks[0] * BLOCK, start < offq * BLOCK
    which_query = half - 2 * offq
    counts = jnp.where(
        first,
        doc_counts[0] - start,
        jnp.where(
            second,
            doc_counts[1] - (start - blocks[0] * BLOCK),
            jnp.where(which_query == 0, query_counts[0], jnp.where(which_query == 1, query_counts[1], 0)),
        ),
    )
    owner = jnp.where(first, 0, jnp.where(second, 1, jnp.clip(2 + which_query, 2, 3)))
    return meta, table_block, jnp.clip(counts, 0, BLOCK // 2).astype(jnp.int32), owner.astype(jnp.int32)


def pack_rows(docs, queries, meta, rows):
    width = docs.shape[-1]
    tail = jnp.zeros((rows - docs.shape[1], width), docs.dtype)
    packed = jnp.concatenate([docs[0], tail], axis=0)
    packed = lax.dynamic_update_slice(packed, docs[1], (meta[OFF1], 0))
    padded = jnp.concatenate(
        [queries.reshape(BLOCK, width), jnp.zeros((BLOCK, width), docs.dtype)], axis=0
    )
    return lax.dynamic_update_slice(packed, padded, (meta[OFFQ], 0))


def loss_kernel(where, message_ref, soft_ref, loss_ref, query_grad_ref, doc_grad_ref):
    rows = message_ref.shape[0]
    devices = rows // 8
    pairs = 2 * devices
    soft = soft_ref[0:1, 0:1]
    message = message_ref[...]
    low = message.astype(BF16)
    owner = lax.broadcasted_iota(jnp.int32, (pairs, rows), 0) // 2
    entry = lax.broadcasted_iota(jnp.int32, (pairs, rows), 0) % 2
    row = lax.broadcasted_iota(jnp.int32, (pairs, rows), 1)
    relative = row // 8
    outer_size = devices // 8
    outer = (where[0] + outer_size - relative // 8) % outer_size
    absolute = (
        ((where[2] ^ ((relative // 2) % 2)) * outer_size + outer) * 2 + (where[1] ^ ((relative // 4) % 2))
    ) * 2 + (where[3] ^ (relative % 2))
    matched = owner == absolute
    pick = lambda at: (matched & (row % 8 == at)).astype(F32)
    units_q = dot((matched & (row % 8 == entry)).astype(BF16), low).astype(BF16)
    units_d = dot((matched & (row % 8 == entry + 2)).astype(BF16), low).astype(BF16)
    extra = lax.dot_general(
        pick(4), message[:, :128], (((1,), (0,)), ((), ())), precision=lax.Precision.HIGHEST,
        preferred_element_type=F32,
    )
    lane = lax.broadcasted_iota(jnp.int32, extra.shape, 1)
    member = lax.broadcasted_iota(jnp.int32, extra.shape, 0) % 2
    weight = jnp.sum(jnp.where(lane == member, extra, 0.0), axis=1, keepdims=True)
    correct = jnp.sum(jnp.where(lane == member + 2, extra, 0.0), axis=1, keepdims=True)
    similarity = dot(units_q, units_d, ((1,), (1,))) / soft
    columns = lax.broadcasted_iota(jnp.int32, similarity.shape, 1)
    target = (columns == (correct + 0.5).astype(jnp.int32)).astype(F32)
    highest = jnp.max(similarity, axis=1, keepdims=True)
    log_norm = highest + jnp.log(jnp.sum(jnp.exp(similarity - highest), axis=1, keepdims=True))
    picked = jnp.sum(target * similarity, axis=1, keepdims=True)
    loss = jnp.sum(weight * (log_norm - picked), axis=0, keepdims=True) / pairs
    loss_ref[...] = jnp.broadcast_to(loss, loss_ref.shape)
    grad = weight * (jnp.exp(similarity - log_norm) - target) / pairs
    me = (((where[2] * outer_size + where[0]) * 2 + where[1]) * 2 + where[3]) * 2
    mine_rows = lax.broadcasted_iota(jnp.int32, (8, pairs), 1) == me + lax.broadcasted_iota(
        jnp.int32, (8, pairs), 0
    )
    mine = mine_rows.astype(F32)
    highest_dot = functools.partial(
        lax.dot_general, precision=lax.Precision.HIGHEST, preferred_element_type=F32
    )
    plain, turned = (((1,), (0,)), ((), ())), (((1,), (1,)), ((), ()))
    query_rows = highest_dot(mine, grad, plain)
    doc_rows = highest_dot(mine, grad, turned)
    query_grad_ref[...] = highest_dot(query_rows, units_d.astype(F32), plain) / soft
    doc_grad_ref[...] = highest_dot(doc_rows, units_q.astype(F32), plain) / soft


def loss_and_grads(where, messages, soft):
    width = messages.shape[1]
    vmem = pl.BlockSpec(memory_space=pltpu.VMEM)
    return pl.pallas_call(
        loss_kernel,
        in_specs=[pl.BlockSpec(memory_space=pltpu.SMEM), vmem, vmem],
        out_specs=[vmem, vmem, vmem],
        out_shape=[
            jax.ShapeDtypeStruct((8, 128), F32),
            jax.ShapeDtypeStruct((8, width), F32),
            jax.ShapeDtypeStruct((8, width), F32),
        ],
        compiler_params=params(),
        name="loss",
    )(where, messages, jnp.broadcast_to(soft.reshape(1, 1), (8, 128)))


def wide_unfold_kernel(meta, p00, p01, p10, p11, *refs):
    gate_ref, up_ref, down_ref = refs[-3:]
    for other_core in range(2):
        for other_row in range(2):
            piece = ((p00, p01), (p10, p11))[other_core][other_row]

            @pl.when((pl.program_id(0) == other_core) & (pl.program_id(1) == other_row))
            def _():
                gate_ref[...] = piece[0].astype(F32)
                up_ref[...] = piece[1].astype(F32)
                span = piece.shape[2] // 2
                block = jnp.concatenate([piece[2, :, :span], piece[2, :, span:]], axis=0)
                down_ref[...] = block.astype(F32).T


def wide_unfold(meta, chunk, pieces, before, side, width, inner):
    quarter, span = pieces[0].shape[1:]
    chunks = inner // (2 * span)
    aliased = [pl.BlockSpec(memory_space=pl.ANY)] * len(before)
    grid_spec = pltpu.PrefetchScalarGridSpec(
        num_scalar_prefetch=1,
        grid=(2, 2),
        in_specs=[resident(p.shape) for p in pieces] + aliased,
        out_specs=[
            pl.BlockSpec(
                (quarter, span), lambda c, r, m: (m[ROW] ^ r, (m[CORE] ^ c) * chunks + chunk)
            )
            for _ in range(2)
        ]
        + [
            pl.BlockSpec(
                (span // 2, 2 * quarter), lambda c, r, m: (2 * chunk + (m[CORE] ^ c), m[ROW] ^ r)
            )
        ],
    )
    return pl.pallas_call(
        wide_unfold_kernel,
        grid_spec=grid_spec,
        out_shape=[
            jax.ShapeDtypeStruct((width // 2, inner), F32),
            jax.ShapeDtypeStruct((width // 2, inner), F32),
            jax.ShapeDtypeStruct((inner // 2, width), F32),
        ],
        input_output_aliases={5 + at: at for at in range(len(before))},
        compiler_params=pltpu.CompilerParams(vmem_limit_bytes=16 * 1024 * 1024),
        cost_estimate=cost(0, 6 * 4 * pieces[0].size),
        name="wide_unfold",
    )(meta, *pieces, *before)


def narrow_unfold_kernel(meta, p00, p01, p10, p11, *refs):
    out_ref = refs[-1]
    lines = out_ref.shape[1]
    for other_core in range(2):
        for other_row in range(2):
            piece = ((p00, p01), (p10, p11))[other_core][other_row]

            @pl.when((pl.program_id(0) == other_core) & (pl.program_id(1) == other_row))
            def _():
                at = pl.multiple_of(pl.program_id(2) * lines, lines)
                out_ref[...] = piece[:, pl.ds(at, lines)].astype(F32)


def narrow_unfold(meta, pieces, before, columns, lines, place):
    quarter = pieces[0].shape[0]
    parts = pieces[0].shape[1] // lines
    aliased = [pl.BlockSpec(memory_space=pl.ANY)] * len(before)
    grid_spec = pltpu.PrefetchScalarGridSpec(
        num_scalar_prefetch=1,
        grid=(2, 2, parts),
        in_specs=[resident(p.shape) for p in pieces] + aliased,
        out_specs=pl.BlockSpec(
            (quarter, lines), lambda c, r, part, m: (m[ROW] ^ r, place(part, m[CORE] ^ c))
        ),
    )
    return pl.pallas_call(
        narrow_unfold_kernel,
        grid_spec=grid_spec,
        out_shape=jax.ShapeDtypeStruct((2 * quarter, columns), F32),
        input_output_aliases={5 + at: at for at in range(len(before))},
        compiler_params=pltpu.CompilerParams(vmem_limit_bytes=16 * 1024 * 1024),
        cost_estimate=cost(0, 6 * 4 * pieces[0].size),
        name="narrow_unfold",
    )(meta, *pieces, *before)


AXES = ("fsdp", "blk")


class Links:
    def __init__(self, sides, blk):
        self.sides, self.blk, self.outer = sides, blk, blk // 4

    def swap(self, value, side=0, mask=0):
        pairs = [
            (f * self.blk + b, (f ^ side) * self.blk + (b ^ mask))
            for f in range(self.sides)
            for b in range(self.blk)
        ]
        return lax.ppermute(value, AXES, pairs)

    def core(self, value):
        return self.swap(value, mask=1)

    def row(self, value):
        return self.swap(value, mask=2)

    def side(self, value):
        return self.swap(value, side=1)

    def shift(self, value, by):
        pairs = [
            (f * self.blk + b, f * self.blk + (b + 4 * by) % self.blk)
            for f in range(self.sides)
            for b in range(self.blk)
        ]
        return lax.ppermute(value, AXES, pairs)

    def outer_masks(self):
        mask = 4
        while mask < self.blk:
            yield mask
            mask *= 2

    def gather(self, value):
        both = jnp.concatenate([value, self.core(value)], axis=0)
        plane = jnp.concatenate(
            [both, self.swap(both, 1, 0), self.swap(both, 0, 2), self.swap(both, 1, 2)], axis=0
        )
        return jnp.concatenate(
            [plane] + [self.shift(plane, by) for by in range(1, self.outer)], axis=0
        )

    def total(self, keep, send):
        add = lambda *terms: sum(term.astype(F32) for term in terms).astype(BF16)
        received = self.core(send)
        across = self.side(add(keep[1], received[1]))
        other = self.row(add(keep[0, 1], received[0, 1], across[1]))
        mine = add(keep[0, 0], received[0, 0], across[0], other)
        for mask in self.outer_masks():
            mine = add(mine, self.swap(mine, mask=mask))
        return mine

    def spread(self, mine):
        other = self.row(mine)
        return mine, other, self.core(mine), self.core(other)

    def total_small(self, value):
        value = value + self.core(value)
        value = value + self.side(value)
        value = value + self.row(value)
        for mask in self.outer_masks():
            value = value + self.swap(value, mask=mask)
        return value


def fetch(links, share, side, core):
    rows = share.shape[0]
    half = rows // 2
    got = links.side(lax.dynamic_slice_in_dim(share, core * half, half, 0))
    other = links.core(got)
    whole = jnp.concatenate([share, share], axis=0)
    base = (1 - side) * rows
    whole = lax.dynamic_update_slice_in_dim(whole, got, base + core * half, 0)
    return lax.dynamic_update_slice_in_dim(whole, other, base + (1 - core) * half, 0)


def body(
    question_activations,
    passage_activations,
    question_unpadded_counts,
    passage_unpadded_counts,
    correct_passage_index,
    query_weights,
    softness_factor,
    combined_projection_matrix,
    mixing_result_matrix,
    gating_matrix,
    widening_matrix,
    narrowing_matrix,
    initial_layernorm_scale,
    initial_layernorm_shift,
    later_layernorm_scale,
    later_layernorm_shift,
):
    doc_len, width = passage_activations.shape[1:]
    query_len = question_activations.shape[1]
    inner = gating_matrix.shape[1]
    assert passage_activations.shape[0] == 2 and doc_len == 6 * BLOCK and 2 * query_len == BLOCK
    links = Links(lax.axis_size("fsdp"), lax.axis_size("blk"))
    side, blk = lax.axis_index("fsdp"), lax.axis_index("blk")
    core, row, outer = blk % 2, (blk // 2) % 2, blk // 4
    where = jnp.stack([outer, row, side, core]).astype(jnp.int32)

    wqkv = fetch(links, combined_projection_matrix, side, core)
    wo = fetch(links, mixing_result_matrix, side, core)
    wg = fetch(links, gating_matrix, side, core)
    wu = fetch(links, widening_matrix, side, core)
    wd = fetch(links, narrowing_matrix, side, core)
    vectors = jnp.stack(
        [initial_layernorm_scale, initial_layernorm_shift, later_layernorm_scale, later_layernorm_shift]
    )
    others = links.side(vectors)
    vectors = jnp.concatenate(
        [jnp.where(side == 0, vectors, others), jnp.where(side == 0, others, vectors)], axis=1
    ).astype(F32)
    gain_one, bias_one, gain_two, bias_two = (vectors[at : at + 1] for at in range(4))

    rows = -(-(2 * doc_len + BLOCK) // TILE) * TILE
    doc_counts, query_counts = passage_unpadded_counts, question_unpadded_counts
    meta, table_block, counts, owner = layout(doc_counts, query_counts, rows, core, side, row)
    tables = tuple(jnp.asarray(table) for table in rotary_tables(doc_len, query_len))
    x = pack_rows(passage_activations, question_activations, meta, rows)

    qkv = project(meta, table_block, x, wqkv, tables)
    att, lse = attend(meta, qkv)
    low, z1, r1, silu, slope, hidden, z2, r2, sums = forward(
        meta, counts, att, x, wo, wg, wu, wd, gain_one, bias_one
    )

    groups = rows // (BLOCK // 2)
    used = (jnp.arange(groups) // (2 * TILE // BLOCK))[None, :] < meta[TILES]
    chosen = (owner[None, :] == jnp.arange(4)[:, None]) & used
    z_sums = jnp.sum(jnp.where(chosen[:, :, None], sums.reshape(1, groups, width), 0.0), axis=1)
    lengths = jnp.concatenate([doc_counts, query_counts]).astype(F32)[:, None]
    pooled = z_sums / lengths * gain_two + bias_two
    recip = lax.rsqrt(jnp.sum(pooled * pooled, axis=1, keepdims=True) + EPS_UNIT)
    unit = (pooled * recip).astype(BF16).astype(F32)
    extra = jnp.concatenate([query_weights, correct_passage_index.astype(F32)])
    extra = jnp.pad(extra[None, :], ((0, 3), (0, width - 4)))
    messages = links.gather(jnp.concatenate([unit[2:], unit[:2], extra], axis=0))
    loss, grad_q, grad_d = loss_and_grads(where, messages, softness_factor)
    grad_unit = jnp.concatenate([grad_d[:2], grad_q[:2]], axis=0)
    crossed = jnp.sum(grad_unit * pooled, axis=1, keepdims=True)
    grad_rows = (recip * grad_unit - pooled * recip**3 * crossed) / lengths
    grad_gain_two = jnp.sum(grad_rows * z_sums, axis=0)
    grad_bias_two = jnp.sum(grad_rows * lengths, axis=0)

    scaled = jnp.pad(grad_rows * gain_two, ((0, 4), (0, 0)))
    branch, first = norm_two_back(meta, counts, owner, z2, r2, scaled)
    wide = []
    for chunk in range(3):
        first, keep, send = ffn_back(meta, chunk, branch, low, hidden, silu, slope, wd, wg, wu, first)
        wide.append(links.total(keep, send))
    sum_one, grad_att, grad_norm, keep, send = norm_one_back(meta, first, z1, r1, att, gain_one, wo)
    narrow = [links.total(keep, send)]
    small = links.total_small(
        jnp.concatenate([grad_norm[:2], grad_gain_two[None], grad_bias_two[None]], axis=0)
    )
    small = lax.dynamic_slice_in_dim(small, side * (width // 2), width // 2, 1)
    grads = []
    for group in range(3):
        grads.append(attend_back(meta, table_block, group, 2, qkv, grad_att, lse, tables))
        narrow.append(links.total(*qkv_grad(meta, x, grads[-1])))
    grad_docs, grad_queries = token_grad(meta, sum_one, grads, wqkv, 2)

    grad_wide = ()
    for chunk in range(3):
        grad_wide = wide_unfold(meta, chunk, links.spread(wide[chunk]), grad_wide, side, width, inner)
    grad_out = narrow_unfold(
        meta, links.spread(narrow[0]), (), width, width // 2, lambda part, at: at
    )
    grad_qkv = ()
    for group in range(3):
        grad_qkv = (
            narrow_unfold(
                meta, links.spread(narrow[group + 1]), grad_qkv, 3 * width, 128,
                lambda part, at, group=group: part * 6 + 2 * group + at,
            ),
        )
    return (
        loss[0, :1],
        grad_queries,
        grad_docs,
        grad_qkv[0],
        grad_out,
        grad_wide[0],
        grad_wide[1],
        grad_wide[2],
        small[0],
        small[1],
        small[2],
        small[3],
    )


def solution(mesh):
    placed = (
        P(("fsdp", "blk"), None, None),
        P(("fsdp", "blk"), None, None),
        P(("fsdp", "blk")),
        P(("fsdp", "blk")),
        P(("fsdp", "blk")),
        P(("fsdp", "blk")),
        P(),
        P("fsdp", None),
        P("fsdp", None),
        P("fsdp", None),
        P("fsdp", None),
        P("fsdp", None),
        P("fsdp"),
        P("fsdp"),
        P("fsdp"),
        P("fsdp"),
    )
    return jax.shard_map(
        body,
        mesh=mesh,
        in_specs=placed,
        out_specs=(
            P(),
            P(("fsdp", "blk"), None, None),
            P(("fsdp", "blk"), None, None),
            P("fsdp", None),
            P("fsdp", None),
            P("fsdp", None),
            P("fsdp", None),
            P("fsdp", None),
            P("fsdp"),
            P("fsdp"),
            P("fsdp"),
            P("fsdp"),
        ),
        check_vma=False,
    )
```

```python
import functools

import jax
import jax.numpy as jnp
import numpy as np
from jax import lax
from jax.experimental import pallas as pl
from jax.experimental.pallas import tpu as pltpu
from jax.sharding import PartitionSpec as P

HEAD = 64
BLOCK = 128
TILE = 256
EPS_NORM = 1e-05
EPS_UNIT = 1e-06
MASKED = -1e30
F32 = jnp.float32
BF16 = jnp.bfloat16
PACE = 0.5
VMEM_LIMIT = 60 * 1024 * 1024
OFF0, OFF1, OFFQ, LEN0, LEN1, QLEN0, QLEN1, CNT0, CNT1, TILES, CORE, SIDE, ROW, SLOT, STAY = range(15)


def dot(left, right, contract=((1,), (0,))):
    return lax.dot_general(left, right, (contract, ((), ())), preferred_element_type=F32)


def cost(microseconds):
    return pl.CostEstimate(flops=int(microseconds * PACE * 1e9), bytes_accessed=0, transcendentals=0)


def params(**more):
    return pltpu.CompilerParams(vmem_limit_bytes=VMEM_LIMIT, **more)


def rotary_tables(doc_len, query_len):
    frequency = 1000.0 ** (-(np.arange(HEAD // 2, dtype=np.float32) * 2.0 / HEAD))
    positions = np.concatenate([np.arange(doc_len), np.arange(query_len), np.arange(query_len)])
    angles = positions.astype(np.float32)[:, None] * frequency.astype(np.float32)[None, :]
    cosine, sine = np.cos(angles), np.sin(angles)
    return (
        np.concatenate([cosine] * 4, axis=1).astype(np.float32),
        np.concatenate([-sine, sine, -sine, sine], axis=1).astype(np.float32),
    )


def swap_halves(pair):
    lane = lax.broadcasted_iota(jnp.int32, pair.shape, 1)
    return jnp.where(lane % HEAD < HEAD // 2, pltpu.roll(pair, 96, 1), pltpu.roll(pair, 32, 1))


def live(step, meta):
    return jnp.minimum(step, meta[TILES] - 1)


def tiled(columns, at=0):
    return pl.BlockSpec((TILE, columns), lambda i, m, *_: (live(i, m), at))


def while_live(kernel):
    @functools.wraps(kernel)
    def run(meta, *refs):
        @pl.when(pl.program_id(0) < meta[TILES])
        def _():
            kernel(meta, *refs)

    return run


def anywhere(count):
    return [pl.BlockSpec(memory_space=pl.ANY)] * count


def resident(shape):
    return pl.BlockSpec(shape, lambda *_: (0,) * len(shape), pipeline_mode=pl.Buffered(1))


def piece_copies(meta, rows, pieces, whole, sems):
    side, row, core = meta[SIDE], meta[ROW], meta[CORE]
    parts = len(pieces) - 1
    if parts == 2:
        places = [core, 1 - core]
    else:
        places = [row * 2 + core, (1 - row) * 2 + core, row * 2 + 1 - core, (1 - row) * 2 + 1 - core]
    size = rows // parts
    starts = [side * rows] + [(1 - side) * rows + place * size for place in places]
    return [
        pltpu.make_async_copy(
            piece, whole.at[pl.ds(pl.multiple_of(start, 16), piece.shape[0]), :], sems.at[at]
        )
        for at, (piece, start) in enumerate(zip(pieces, starts))
    ]


def qkv_kernel(meta, table_block, x_ref, cos_ref, sin_ref, *refs):
    pieces, (out_ref, whole_out, w_ref, sems, out_sem) = refs[:3], refs[-5:]
    tile = pl.program_id(0)
    keep = pltpu.make_async_copy(w_ref, whole_out, out_sem)

    @pl.when(tile == 0)
    def _():
        copies = piece_copies(meta, pieces[0].shape[0], pieces, w_ref, sems)
        for copy in copies:
            copy.start()
        for copy in copies:
            copy.wait()
        keep.start()

    @pl.when(tile < meta[TILES])
    def _():
        x = x_ref[...]
        width = x.shape[1]
        for part in range(3):
            acc = dot(x, w_ref[:, part * width : (part + 1) * width])
            if part == 2:
                out_ref[:, 2 * width :] = acc.astype(BF16)
                continue
            scale = HEAD**-0.5 if part == 0 else 1.0
            for sub in range(TILE // BLOCK):
                rows = slice(sub * BLOCK, (sub + 1) * BLOCK)
                table = pl.ds(table_block[tile * (TILE // BLOCK) + sub] * BLOCK, BLOCK)
                cosine, sine = cos_ref[table, :] * scale, sin_ref[table, :] * scale
                for group in range(width // 128):
                    pair = acc[rows, group * 128 : (group + 1) * 128]
                    turned = pair * cosine + swap_halves(pair) * sine
                    at = part * width + group * 128
                    out_ref[rows, at : at + 128] = turned.astype(BF16)

    @pl.when(tile == pl.num_programs(0) - 1)
    def _():
        keep.wait()


def project(meta, table_block, x, pieces, tables, after=()):
    rows, width = x.shape
    whole = (width, 3 * width)
    grid_spec = pltpu.PrefetchScalarGridSpec(
        num_scalar_prefetch=2,
        grid=(rows // TILE,),
        in_specs=[tiled(width), resident(tables[0].shape), resident(tables[1].shape)]
        + anywhere(len(pieces) + len(after)),
        out_specs=[tiled(3 * width)] + anywhere(1),
        scratch_shapes=[
            pltpu.VMEM(whole, BF16),
            pltpu.SemaphoreType.DMA((len(pieces),)),
            pltpu.SemaphoreType.DMA,
        ],
    )
    return pl.pallas_call(
        qkv_kernel,
        grid_spec=grid_spec,
        out_shape=[
            jax.ShapeDtypeStruct((rows, 3 * width), BF16),
            jax.ShapeDtypeStruct(whole, BF16),
        ],
        compiler_params=params(),
        cost_estimate=cost(11),
        name="qkv",
    )(meta, table_block, x, *tables, *pieces, *after)


def split_pair(pair):
    lane = lax.broadcasted_iota(jnp.int32, pair.shape, 1)
    zero = jnp.zeros_like(pair)
    return jnp.concatenate(
        [jnp.where(lane < HEAD, pair, zero), jnp.where(lane < HEAD, zero, pair)], axis=0
    )


def mask_keys(scores, last, valid):
    rows = lax.broadcasted_iota(jnp.int32, (BLOCK, scores.shape[1]), 0)
    tail = jnp.where(rows < valid, scores[last * BLOCK :, :], MASKED)
    if last == 0:
        return tail
    return jnp.concatenate([scores[: last * BLOCK, :], tail], axis=0)


def query_mask(meta, scores):
    half = scores.shape[0] // 2
    key = lax.broadcasted_iota(jnp.int32, scores.shape, 0)
    row = lax.broadcasted_iota(jnp.int32, scores.shape, 1) % (2 * half)
    length = jnp.where(key < half, meta[QLEN0], meta[QLEN1])
    keep = ((key < half) == (row < half)) & (key % half < length)
    return jnp.where(keep, scores, MASKED)


def stack_heads(pair_wide):
    half = pair_wide.shape[1] // 2
    return jnp.concatenate([pair_wide[:, :half], pair_wide[:, half:]], axis=0)


def attend_kernel(meta, q_ref, k_ref, v_ref, *refs):
    out_ref, lse_ref = refs[-2:]

    def tile_of(start, size, keys, values, masked):
        rows = pl.ds(start, size)
        queries = split_pair(q_ref[rows, :])
        scores = masked(dot(keys, queries, ((1,), (1,))))
        highest = jnp.max(scores, axis=0, keepdims=True)
        exponent = jnp.exp(scores - highest)
        total = jnp.sum(exponent, axis=0, keepdims=True)
        probs = (exponent * (1.0 / total)).astype(BF16)
        out_ref[rows, :] = dot(stack_heads(probs), values, ((0,), (0,))).astype(BF16)
        log_norm = highest + jnp.log(total)
        lse_ref[0, 0:1, rows] = log_norm[:, :size]
        lse_ref[0, 1:2, rows] = log_norm[:, size:]

    @pl.loop(0, 2)
    def _(doc):
        start = pl.multiple_of(meta[OFF0 + doc], BLOCK)
        for blocks in range(1, 7):

            @pl.when(meta[CNT0 + doc] == blocks)
            def _():
                keys = k_ref[pl.ds(start, blocks * BLOCK), :]
                values = split_pair(v_ref[pl.ds(start, blocks * BLOCK), :])
                valid = meta[LEN0 + doc] - (blocks - 1) * BLOCK

                @pl.loop(0, (blocks + 1) // 2)
                def _(step):
                    tile_of(
                        pl.multiple_of(start + step * TILE, BLOCK),
                        TILE,
                        keys,
                        values,
                        lambda scores: mask_keys(scores, blocks - 1, valid),
                    )

    first = pl.multiple_of(meta[OFFQ], BLOCK)
    rows = pl.ds(first, BLOCK)
    tile_of(first, BLOCK, k_ref[rows, :], split_pair(v_ref[rows, :]), functools.partial(query_mask, meta))
    out_ref[pl.ds(first + BLOCK, BLOCK), :] = jnp.zeros((BLOCK, 128), BF16)


def attend(meta, qkv, group, members, after=()):
    rows, width = qkv.shape[0], qkv.shape[1] // 3
    pairs = width // 128

    def column(part):
        return pl.BlockSpec((rows, 128), lambda h, *_: (0, part * pairs + group * members + h))

    grid_spec = pltpu.PrefetchScalarGridSpec(
        num_scalar_prefetch=1,
        grid=(members,),
        in_specs=[column(0), column(1), column(2)] + anywhere(len(after)),
        out_specs=[
            pl.BlockSpec((rows, 128), lambda h, *_: (0, h)),
            pl.BlockSpec((1, 8, rows), lambda h, *_: (h, 0, 0)),
        ],
    )
    return pl.pallas_call(
        attend_kernel,
        grid_spec=grid_spec,
        out_shape=[
            jax.ShapeDtypeStruct((rows, 128 * members), BF16),
            jax.ShapeDtypeStruct((members, 8, rows), F32),
        ],
        compiler_params=params(),
        cost_estimate=cost(13),
        name="attend",
    )(meta, qkv, qkv, qkv, *after)


def normalize(summed):
    centered = summed - jnp.mean(summed, axis=-1, keepdims=True)
    recip = lax.rsqrt(jnp.mean(centered * centered, axis=-1, keepdims=True) + EPS_NORM)
    return centered * recip, recip


def forward_kernel(
    meta, counts, att0, att1, att2, x_ref, gain_ref, bias_ref, *refs,
):
    outs, scratch = refs[-20:-7], refs[-7:]
    pieces = [refs[0:3], refs[3:8], refs[8:13], refs[13:18]]
    low_ref, z1_ref, r1_ref, silu_ref, slope_ref, hidden_ref, z2_ref, r2_ref, sums_ref = outs[:9]
    whole_outs = outs[9:]
    wholes, (sems, out_sems) = scratch[:4], scratch[5:]
    wo_ref, wg_ref, wu_ref, wd_ref = wholes
    tile = pl.program_id(0)
    copies = [
        piece_copies(meta, pieces[at][0].shape[0], pieces[at], wholes[at], sems.at[at])
        for at in range(4)
    ]
    keeps = [
        pltpu.make_async_copy(wholes[at], whole_outs[at], out_sems.at[at]) for at in range(4)
    ]

    @pl.when(tile == 0)
    def _():
        for group in copies:
            for copy in group:
                copy.start()

    def ready(which):
        @pl.when(tile == 0)
        def _():
            for at in which:
                for copy in copies[at]:
                    copy.wait()
                keeps[at].start()

    ready((0,))

    @pl.when(tile < meta[TILES])
    def _():
        att = jnp.concatenate([att0[...], att1[...], att2[...]], axis=1)
        z1, r1 = normalize(x_ref[...].astype(F32) + dot(att, wo_ref[...]))
        z1_ref[...] = z1.astype(BF16)
        r1_ref[...] = r1
        normed = z1 * gain_ref[...] + bias_ref[...]
        low_ref[...] = normed.astype(BF16)
        scratch[4][...] = normed

    ready((1, 2, 3))

    @pl.when(tile < meta[TILES])
    def _():
        low = low_ref[...]
        total = scratch[4][...]
        inner, chunk = wg_ref.shape[1], 512
        for at in range(0, inner, chunk):
            columns = slice(at, at + chunk)
            gate = dot(low, wg_ref[:, columns])
            up = dot(low, wu_ref[:, columns])
            sigmoid = 0.5 * jnp.tanh(0.5 * gate) + 0.5
            silu = gate * sigmoid
            hidden = (silu * up).astype(BF16)
            silu_ref[:, columns] = silu.astype(BF16)
            slope_ref[:, columns] = (up * (sigmoid + silu * (1.0 - sigmoid))).astype(BF16)
            hidden_ref[:, columns] = hidden
            total = total + dot(hidden, wd_ref[columns, :])
        z2, r2 = normalize(total)
        z2_ref[...] = z2.astype(BF16)
        r2_ref[...] = r2
        half = BLOCK // 2
        inside = lax.broadcasted_iota(jnp.int32, (half, z2.shape[1]), 0)
        for group in range(TILE // half):
            valid = counts[tile * (TILE // half) + group]
            kept = jnp.where(inside < valid, z2[group * half : (group + 1) * half, :], 0.0)
            sums_ref[0, group : group + 1, :] = jnp.sum(kept, axis=0, keepdims=True)

    @pl.when(tile == pl.num_programs(0) - 1)
    def _():
        for keep in keeps:
            keep.wait()


def forward(meta, counts, att, x, pieces, gain, bias, after=()):
    rows, width = x.shape
    inner = pieces[1][0].shape[1]
    wholes = [(width, width), (width, inner), (width, inner), (inner, width)]

    def array(columns, kind):
        return jax.ShapeDtypeStruct((rows, columns), kind)

    grid_spec = pltpu.PrefetchScalarGridSpec(
        num_scalar_prefetch=2,
        grid=(rows // TILE,),
        in_specs=[tiled(part.shape[1]) for part in att]
        + [tiled(width), resident(gain.shape), resident(bias.shape)]
        + anywhere(18 + len(after)),
        out_specs=[
            tiled(width), tiled(width), tiled(1), tiled(inner), tiled(inner), tiled(inner),
            tiled(width), tiled(1),
            pl.BlockSpec((1, 4, width), lambda i, m, *_: (live(i, m), 0, 0)),
        ]
        + anywhere(4),
        scratch_shapes=[pltpu.VMEM(shape, BF16) for shape in wholes]
        + [
            pltpu.VMEM((TILE, width), F32),
            pltpu.SemaphoreType.DMA((4, 5)),
            pltpu.SemaphoreType.DMA((4,)),
        ],
    )
    return pl.pallas_call(
        forward_kernel,
        grid_spec=grid_spec,
        out_shape=[
            array(width, BF16), array(width, BF16), array(1, F32), array(inner, BF16),
            array(inner, BF16), array(inner, BF16), array(width, BF16), array(1, F32),
            jax.ShapeDtypeStruct((rows // TILE, 4, width), F32),
        ]
        + [jax.ShapeDtypeStruct(shape, BF16) for shape in wholes],
        compiler_params=params(),
        cost_estimate=cost(42),
        name="forward",
    )(meta, counts, *att, x, gain, bias, *[p for group in pieces for p in group], *after)


@while_live
def norm_two_back_kernel(meta, counts, owner, z_ref, r_ref, scaled_ref, *refs):
    branch_ref, out_ref = refs[-2:]
    tile = pl.program_id(0)
    half = BLOCK // 2
    width = z_ref.shape[1]
    inside = lax.broadcasted_iota(jnp.int32, (half, width), 0)
    for group in range(TILE // half):
        at = tile * (TILE // half) + group
        rows = slice(group * half, (group + 1) * half)
        scaled = scaled_ref[pl.ds(owner[at], 1), :]
        z = z_ref[rows, :].astype(F32)
        plain = jnp.mean(scaled, axis=-1, keepdims=True)
        cross = jnp.mean(scaled * z, axis=-1, keepdims=True)
        grad = r_ref[rows, :] * (scaled - plain - z * cross)
        grad = jnp.where(inside < counts[at], grad, 0.0)
        branch_ref[rows, :] = grad.astype(BF16)
        out_ref[rows, :] = grad


def norm_two_back(meta, counts, owner, z, recip, scaled):
    rows, width = z.shape

    grid_spec = pltpu.PrefetchScalarGridSpec(
        num_scalar_prefetch=3,
        grid=(rows // TILE,),
        in_specs=[tiled(width), tiled(1), resident(scaled.shape)],
        out_specs=[tiled(width), tiled(width)],
    )
    return pl.pallas_call(
        norm_two_back_kernel,
        grid_spec=grid_spec,
        out_shape=[jax.ShapeDtypeStruct((rows, width), BF16), jax.ShapeDtypeStruct((rows, width), F32)],
        compiler_params=params(),
        cost_estimate=cost(7),
        name="norm_two_back",
    )(meta, counts, owner, z, recip, scaled)


@while_live
def ffn_back_kernel(
    meta, branch_ref, low_ref, hid0, hid1, silu0, silu1, slope0, slope1,
    wd0, wd1, wg0, wg1, wu0, wu1, first_in, *refs,
):
    first_out, keep_ref, send_ref, acc_g, acc_u, acc_d = refs[-6:]
    tile = pl.program_id(0)
    span = wd0.shape[0]

    @pl.when(tile == 0)
    def _():
        acc_g[...] = jnp.zeros_like(acc_g)
        acc_u[...] = jnp.zeros_like(acc_u)
        acc_d[...] = jnp.zeros_like(acc_d)

    branch = branch_ref[...]
    low_t = low_ref[...].T
    branch_t = branch.T
    first = first_in[...]
    for half, (hid, silu, slope, wd, wg, wu) in enumerate(
        ((hid0, silu0, slope0, wd0, wg0, wu0), (hid1, silu1, slope1, wd1, wg1, wu1))
    ):
        columns = slice(half * span, (half + 1) * span)
        grad_hidden = dot(branch, wd[...], ((1,), (1,)))
        grad_gate = (grad_hidden * slope[...].astype(F32)).astype(BF16)
        grad_up = (grad_hidden * silu[...].astype(F32)).astype(BF16)
        first = first + dot(grad_gate, wg[...], ((1,), (1,))) + dot(grad_up, wu[...], ((1,), (1,)))
        acc_g[:, columns] += dot(low_t, grad_gate)
        acc_u[:, columns] += dot(low_t, grad_up)
        acc_d[:, columns] += dot(branch_t, hid[...])
    first_out[...] = first

    @pl.when(tile == meta[TILES] - 1)
    def _():
        rows, quarter = acc_g.shape[0] // 4, acc_g.shape[0] // 4
        side, row, core = meta[SIDE], meta[ROW], meta[CORE]
        for other_core, out in ((0, keep_ref), (1, send_ref)):
            columns = pl.ds(pl.multiple_of((core ^ other_core) * span, span), span)
            inner = pl.ds(
                pl.multiple_of((core ^ other_core) * (span // 2), span // 2), span // 2
            )
            for other_side in range(2):
                for other_row in range(2):
                    at = (side ^ other_side) * 2 + (row ^ other_row)
                    lines = pl.ds(pl.multiple_of(at * quarter, quarter), quarter)
                    out[other_side, other_row, 0] = acc_g[lines, columns].astype(BF16)
                    out[other_side, other_row, 1] = acc_u[lines, columns].astype(BF16)
                    left = pl.multiple_of(
                        (side ^ other_side) * span + (core ^ other_core) * (span // 2), span // 2
                    )
                    for part in range(2):
                        lines = pl.ds(
                            pl.multiple_of((row ^ other_row) * 2 * quarter + part * quarter, quarter),
                            quarter,
                        )
                        out[
                            other_side, other_row, 2, :, part * (span // 2) : (part + 1) * (span // 2)
                        ] = acc_d[lines, pl.ds(left, span // 2)].astype(BF16)


def ffn_back(meta, chunk, branch, low, hidden, silu, slope, wd, wg, wu, first, after=()):
    rows, width = low.shape
    inner = hidden.shape[1]
    span = 512
    halves = (chunk, chunk + inner // (2 * span))

    def fixed(shape, index):
        return pl.BlockSpec(shape, lambda i, *_: index, pipeline_mode=pl.Buffered(1))

    grid_spec = pltpu.PrefetchScalarGridSpec(
        num_scalar_prefetch=1,
        grid=(rows // TILE,),
        in_specs=[tiled(width), tiled(width)]
        + [tiled(span, at) for _ in range(3) for at in halves]
        + [fixed((span, width), (at, 0)) for at in halves]
        + [fixed((width, span), (0, at)) for _ in range(2) for at in halves]
        + [tiled(width)]
        + anywhere(len(after)),
        out_specs=[tiled(width)]
        + [pl.BlockSpec((2, 2, 3, width // 4, span), lambda i, *_: (0, 0, 0, 0, 0))] * 2,
        scratch_shapes=[pltpu.VMEM((width, 2 * span), F32)] * 3,
    )
    piece = jax.ShapeDtypeStruct((2, 2, 3, width // 4, span), BF16)
    return pl.pallas_call(
        ffn_back_kernel,
        grid_spec=grid_spec,
        out_shape=[jax.ShapeDtypeStruct((rows, width), F32), piece, piece],
        input_output_aliases={15: 0},
        compiler_params=params(),
        cost_estimate=cost(23),
        name="ffn_back",
    )(
        meta, branch, low, hidden, hidden, silu, silu, slope, slope, wd, wd, wg, wg, wu, wu, first, *after
    )


def out_pieces(meta, acc, keep_ref, send_ref):
    part = acc.shape[0] // 8
    side, row, core = meta[SIDE], meta[ROW], meta[CORE]
    for other_core, out in ((0, keep_ref), (1, send_ref)):
        for other_side in range(2):
            for other_row in range(2):
                at = ((side ^ other_side) * 2 + (row ^ other_row)) * 2 + (core ^ other_core)
                lines = pl.ds(pl.multiple_of(at * part, part), part)
                out[other_side, other_row, :, : acc.shape[1]] = acc[lines, :].astype(BF16)


@while_live
def norm_one_back_kernel(
    meta, first_ref, z_ref, r_ref, att0, att1, att2, gain_ref, wo_ref, later_ref, *refs,
):
    sum_ref, att_grad_ref, gains_out, keep_ref, send_ref, acc = refs[-6:]
    tile = pl.program_id(0)

    @pl.when(tile == 0)
    def _():
        acc[...] = jnp.zeros_like(acc)
        gains_out[...] = later_ref[...]

    first = first_ref[...]
    z = z_ref[...].astype(F32)
    scaled = first * gain_ref[...]
    plain = jnp.mean(scaled, axis=-1, keepdims=True)
    cross = jnp.mean(scaled * z, axis=-1, keepdims=True)
    grad = r_ref[...] * (scaled - plain - z * cross)
    sum_ref[...] = grad
    low = grad.astype(BF16)
    att_grad_ref[...] = dot(low, wo_ref[...], ((1,), (1,))).astype(BF16)
    att = jnp.concatenate([att0[...], att1[...], att2[...]], axis=1)
    acc[...] += dot(att.T, low)
    gains_out[0:1, :] += jnp.sum(first * z, axis=0, keepdims=True)
    gains_out[1:2, :] += jnp.sum(first, axis=0, keepdims=True)

    @pl.when(tile == meta[TILES] - 1)
    def _():
        out_pieces(meta, acc, keep_ref, send_ref)


def norm_one_back(meta, first, z, recip, att, gain, wo, later, after=()):
    rows, width = z.shape
    block = (2, 2, width // 8, width)
    piece = jax.ShapeDtypeStruct(block, BF16)
    grid_spec = pltpu.PrefetchScalarGridSpec(
        num_scalar_prefetch=1,
        grid=(rows // TILE,),
        in_specs=[tiled(width), tiled(width), tiled(1)]
        + [tiled(part.shape[1]) for part in att]
        + [resident(gain.shape), resident(wo.shape), resident(later.shape)]
        + anywhere(len(after)),
        out_specs=[tiled(width), tiled(width), pl.BlockSpec((8, width), lambda i, *_: (0, 0))]
        + [pl.BlockSpec(block, lambda i, *_: (0, 0, 0, 0))] * 2,
        scratch_shapes=[pltpu.VMEM((width, width), F32)],
    )
    return pl.pallas_call(
        norm_one_back_kernel,
        grid_spec=grid_spec,
        out_shape=[
            jax.ShapeDtypeStruct((rows, width), F32), jax.ShapeDtypeStruct((rows, width), BF16),
            jax.ShapeDtypeStruct((8, width), F32), piece, piece,
        ],
        compiler_params=params(),
        cost_estimate=cost(12),
        name="norm_one_back",
    )(meta, first, z, recip, *att, gain, wo, later, *after)


def attend_back_kernel(meta, q_ref, k_ref, v_ref, g_ref, lse_ref, cos_ref, sin_ref, *refs):
    out_ref, key_acc, value_acc = refs[-3:]

    def turn_back(grad, table):
        cosine, sine = cos_ref[table, :], sin_ref[table, :]
        return (grad * cosine - swap_halves(grad) * sine).astype(BF16)

    def tile_of(start, size, keys, values, keys_split, limit, masked):
        rows = pl.ds(start, size)
        queries, grads = split_pair(q_ref[rows, :]), split_pair(g_ref[rows, :])
        log_norm = jnp.concatenate([lse_ref[0, 0:1, rows], lse_ref[0, 1:2, rows]], axis=1)
        if limit is not None:
            column = lax.broadcasted_iota(jnp.int32, log_norm.shape, 1) % size
            log_norm = jnp.where(column < limit, log_norm, -MASKED)
        scores = masked(dot(keys, queries, ((1,), (1,))))
        probs = jnp.exp(scores - log_norm)
        grad_probs = dot(values, grads, ((1,), (1,)))
        inner = jnp.sum(probs * grad_probs, axis=0, keepdims=True)
        grad_scores = (probs * (grad_probs - inner)).astype(BF16)
        grad_query = dot(stack_heads(grad_scores), keys_split, ((0,), (0,))) * HEAD**-0.5
        return grad_query, dot(grad_scores, queries), dot(probs.astype(BF16), grads)

    @pl.loop(0, 2)
    def _(doc):
        start = pl.multiple_of(meta[OFF0 + doc], BLOCK)
        for blocks in range(1, 7):

            @pl.when(meta[CNT0 + doc] == blocks)
            def _():
                size = blocks * BLOCK
                whole = pl.ds(start, size)
                keys, values = k_ref[whole, :], v_ref[whole, :]
                keys_split = split_pair(keys)
                valid = meta[LEN0 + doc] - (blocks - 1) * BLOCK
                key_acc[:size, :] = jnp.zeros((size, 128), F32)
                value_acc[:size, :] = jnp.zeros((size, 128), F32)

                @pl.loop(0, (blocks + 1) // 2)
                def _(step):
                    at = pl.multiple_of(start + step * TILE, BLOCK)
                    grad_query, grad_key, grad_value = tile_of(
                        at, TILE, keys, values, keys_split, size - step * TILE,
                        lambda scores: mask_keys(scores, blocks - 1, valid),
                    )
                    key_acc[:size, :] += grad_key
                    value_acc[:size, :] += grad_value
                    for sub in range(2):
                        table = pl.ds((step * 2 + sub) * BLOCK, BLOCK)
                        out_ref[pl.ds(at + sub * BLOCK, BLOCK), 0:128] = turn_back(
                            grad_query[sub * BLOCK : (sub + 1) * BLOCK, :], table
                        )

                out_ref[whole, 128:256] = turn_back(key_acc[:size, :], pl.ds(0, size))
                out_ref[whole, 256:384] = value_acc[:size, :].astype(BF16)

    first = pl.multiple_of(meta[OFFQ], BLOCK)
    rows = pl.ds(first, BLOCK)
    keys = k_ref[rows, :]
    grad_query, grad_key, grad_value = tile_of(
        first, BLOCK, keys, v_ref[rows, :], split_pair(keys), None, functools.partial(query_mask, meta)
    )
    table = pl.ds(cos_ref.shape[0] - BLOCK, BLOCK)
    out_ref[rows, 0:128] = turn_back(grad_query, table)
    out_ref[rows, 128:256] = turn_back(grad_key, table)
    out_ref[rows, 256:384] = grad_value.astype(BF16)
    out_ref[pl.ds(first + BLOCK, BLOCK), :] = jnp.zeros((BLOCK, 384), BF16)


def attend_back(meta, group, members, qkv, grad, lse, tables, after=()):
    rows, width = grad.shape
    pairs = width // 128

    def column(part, columns=128):
        return pl.BlockSpec((rows, columns), lambda h, *_: (0, part * pairs + group * members + h))

    grid_spec = pltpu.PrefetchScalarGridSpec(
        num_scalar_prefetch=1,
        grid=(members,),
        in_specs=[
            column(0), column(1), column(2), column(0),
            pl.BlockSpec((1, 8, rows), lambda h, *_: (lse[1] + h, 0, 0)),
            resident(tables[0].shape), resident(tables[1].shape),
        ]
        + anywhere(len(after)),
        out_specs=pl.BlockSpec((rows, 384), lambda h, *_: (0, h)),
        scratch_shapes=[pltpu.VMEM((6 * BLOCK, 128), F32)] * 2,
    )
    return pl.pallas_call(
        attend_back_kernel,
        grid_spec=grid_spec,
        out_shape=jax.ShapeDtypeStruct((rows, 384 * members), BF16),
        compiler_params=params(),
        cost_estimate=cost(11),
        name="attend_back",
    )(meta, qkv, qkv, qkv, grad, lse[0], *tables, *after)


@while_live
def qkv_grad_kernel(meta, x_ref, *refs):
    keep_ref, send_ref, acc = refs[-3:]
    columns = acc.shape[1]
    grads = refs[: columns // 384]
    tile = pl.program_id(0)

    @pl.when(tile == 0)
    def _():
        acc[...] = jnp.zeros_like(acc)

    grad = jnp.concatenate(
        [g[:, part * 128 : (part + 1) * 128] for part in range(3) for g in grads], axis=1
    )
    acc[...] += dot(x_ref[...].T, grad)

    @pl.when(tile == meta[TILES] - 1)
    def _():
        out_pieces(meta, acc, keep_ref, send_ref)
        if keep_ref.shape[3] > columns:
            extra = refs[columns // 384 : columns // 384 + 2]
            keep_ref[:, :, :, columns:] = extra[0][...]
            send_ref[:, :, :, columns:] = extra[1][...]


def qkv_grad(meta, x, grads, extra=(), after=()):
    rows, width = x.shape
    columns = sum(grad.shape[1] for grad in grads)
    block = (2, 2, width // 8, columns + sum(part.shape[3] for part in extra[:1]))
    piece = jax.ShapeDtypeStruct(block, BF16)
    grid_spec = pltpu.PrefetchScalarGridSpec(
        num_scalar_prefetch=1,
        grid=(rows // TILE,),
        in_specs=[tiled(width)]
        + [tiled(grad.shape[1]) for grad in grads]
        + [resident(part.shape) for part in extra]
        + anywhere(len(after)),
        out_specs=[pl.BlockSpec(block, lambda i, *_: (0, 0, 0, 0))] * 2,
        scratch_shapes=[pltpu.VMEM((width, columns), F32)],
    )
    return pl.pallas_call(
        qkv_grad_kernel,
        grid_spec=grid_spec,
        out_shape=[piece, piece],
        compiler_params=params(),
        cost_estimate=cost(9),
        name="qkv_grad",
    )(meta, x, *grads, *extra, *after)


def token_grad_kernel(which, meta, *refs):
    pairs = 6
    sums = refs[0:2]
    grads = [refs[2 + 2 * pair : 4 + 2 * pair] for pair in range(pairs)]
    weights = refs[2 + 2 * pairs : 2 + 5 * pairs]
    step = pl.program_id(0)

    def value():
        total = jnp.concatenate([sums[0][...], sums[1][...]], axis=0)
        grad = jnp.concatenate(
            [
                jnp.concatenate([grads[pair][0][...], grads[pair][1][...]], axis=0)
                for pair in range(pairs)
            ],
            axis=1,
        )
        weight = jnp.concatenate([weight[...] for weight in weights], axis=1)
        return total + dot(grad, weight, ((1,), (1,)))

    if which == 0:
        docs_ref = refs[-1]
        length = meta[LEN0] - step * TILE
        store = lambda value: docs_ref.__setitem__(0, value)
    else:
        docs_ref, queries_ref = refs[-2:]
        length = jnp.where(step < 3, meta[LEN1] - step * TILE, TILE)
        store = lambda value: docs_ref.__setitem__(slice(None), value.astype(BF16))

    @pl.when((step < 3) & (length > 0))
    def _():
        total = value()
        inside = lax.broadcasted_iota(jnp.int32, total.shape, 0)
        store(jnp.where(inside < length, total, 0.0))

    @pl.when((step < 3) & (length <= 0))
    def _():
        store(jnp.zeros((TILE, docs_ref.shape[-1]), F32))

    if which == 1:

        @pl.when(step == 3)
        def _():
            total = value()[:BLOCK, :]
            inside = lax.broadcasted_iota(jnp.int32, (BLOCK // 2, total.shape[1]), 0)
            for query in range(2):
                half = total[query * (BLOCK // 2) : (query + 1) * (BLOCK // 2), :]
                queries_ref[query] = jnp.where(inside < meta[QLEN0 + query], half, 0.0)


def token_grad(which, meta, sums, grads, weight, after=()):
    rows, width = sums.shape
    pairs = width // 128

    def block_of(step, meta, second):
        last = meta[CNT0 + which] - 1
        in_doc = jnp.minimum(jnp.minimum(step, 2) * 2 + second, last)
        return jnp.where(step < 3, meta[OFF0 + which] // BLOCK + in_doc, meta[OFFQ] // BLOCK)

    def halves(columns):
        return [
            pl.BlockSpec((BLOCK, columns), lambda i, meta, s=s: (block_of(i, meta, s), 0)) for s in range(2)
        ]

    if which == 0:
        out_specs = [pl.BlockSpec((1, TILE, width), lambda i, meta: (1 - meta[SLOT], i, 0))]
        out_shape = [jax.ShapeDtypeStruct((2, 6 * BLOCK, width), F32)]
    else:
        out_specs = [
            pl.BlockSpec((TILE, width), lambda i, meta: (jnp.minimum(i, 2), 0)),
            pl.BlockSpec((2, BLOCK // 2, width), lambda i, meta: (0, 0, 0)),
        ]
        out_shape = [
            jax.ShapeDtypeStruct((6 * BLOCK, width), BF16),
            jax.ShapeDtypeStruct((2, BLOCK // 2, width), F32),
        ]
    grid_spec = pltpu.PrefetchScalarGridSpec(
        num_scalar_prefetch=1,
        grid=(3 + which,),
        in_specs=halves(width)
        + sum((halves(grad.shape[1]) for grad in grads), [])
        + [
            pl.BlockSpec(
                (width, 128), lambda i, meta, at=part * pairs + pair: (0, at), pipeline_mode=pl.Buffered(1)
            )
            for pair in range(pairs)
            for part in range(3)
        ]
        + anywhere(len(after)),
        out_specs=out_specs,
    )
    return pl.pallas_call(
        functools.partial(token_grad_kernel, which),
        grid_spec=grid_spec,
        out_shape=out_shape,
        compiler_params=params(),
        cost_estimate=cost(9),
        name="token_grad",
    )(meta, sums, sums, *[g for grad in grads for g in (grad, grad)], *([weight] * (3 * pairs)), *after)


def place_moved_kernel(meta, own_ref, other_ref, *refs):
    docs_ref = refs[-1]

    @pl.when(meta[STAY] == 1)
    def _():
        docs_ref[0] = own_ref[...].astype(F32)

    @pl.when(meta[STAY] == 0)
    def _():
        docs_ref[0] = other_ref[...].astype(F32)


def place_moved(meta, docs, own, other, after=()):
    width = docs.shape[2]
    grid_spec = pltpu.PrefetchScalarGridSpec(
        num_scalar_prefetch=1,
        grid=(3,),
        in_specs=[pl.BlockSpec((TILE, width), lambda i, m: (i, 0))] * 2 + anywhere(1 + len(after)),
        out_specs=pl.BlockSpec((1, TILE, width), lambda i, m: (m[SLOT], i, 0)),
    )
    return pl.pallas_call(
        place_moved_kernel,
        grid_spec=grid_spec,
        out_shape=jax.ShapeDtypeStruct(docs.shape, F32),
        input_output_aliases={3: 0},
        compiler_params=pltpu.CompilerParams(vmem_limit_bytes=16 * 1024 * 1024),
        cost_estimate=cost(4),
        name="place_moved",
    )(meta, own, other, docs, *after)


def layout(doc_counts, query_counts, rows, core, side, row, slot, stay):
    blocks = (doc_counts + BLOCK - 1) // BLOCK
    offq = blocks[0] + blocks[1]
    tiles = (offq + 1 + 1) // 2
    meta = jnp.stack(
        [
            jnp.int32(0), blocks[0] * BLOCK, offq * BLOCK, doc_counts[0], doc_counts[1],
            query_counts[0], query_counts[1], blocks[0], blocks[1], tiles, core, side, row,
            slot, stay, jnp.int32(0),
        ]
    ).astype(jnp.int32)
    at = jnp.arange(rows // BLOCK, dtype=jnp.int32)
    in_first, in_second = at < blocks[0], (at >= blocks[0]) & (at < offq)
    table_block = jnp.where(in_first, at, jnp.where(in_second, at - blocks[0], 6))
    half = jnp.arange(rows // (BLOCK // 2), dtype=jnp.int32)
    start = half * (BLOCK // 2)
    first, second = start < blocks[0] * BLOCK, start < offq * BLOCK
    which_query = half - 2 * offq
    counts = jnp.where(
        first,
        doc_counts[0] - start,
        jnp.where(
            second,
            doc_counts[1] - (start - blocks[0] * BLOCK),
            jnp.where(which_query == 0, query_counts[0], jnp.where(which_query == 1, query_counts[1], 0)),
        ),
    )
    owner = jnp.where(first, 0, jnp.where(second, 1, jnp.clip(2 + which_query, 2, 3)))
    return meta, table_block, jnp.clip(counts, 0, BLOCK // 2).astype(jnp.int32), owner.astype(jnp.int32)


def pack_rows(first, second, queries, meta, rows):
    width = first.shape[-1]
    tail = jnp.zeros((rows - first.shape[0], width), first.dtype)
    packed = jnp.concatenate([first, tail], axis=0)
    packed = lax.dynamic_update_slice(packed, second, (meta[OFF1], 0))
    padded = jnp.concatenate(
        [queries.reshape(BLOCK, width), jnp.zeros((BLOCK, width), first.dtype)], axis=0
    )
    return lax.dynamic_update_slice(packed, padded, (meta[OFFQ], 0))


def loss_kernel(ids, message_ref, soft_ref, loss_ref, query_grad_ref, doc_grad_ref):
    rows, half = message_ref.shape[0], message_ref.shape[1] - 128
    pairs = rows // 4
    soft = soft_ref[0:1, 0:1]
    low = message_ref[:, :half]
    extra = message_ref[:, half:].astype(F32)
    row = lax.broadcasted_iota(jnp.int32, (rows, pairs), 0) % 8
    index = (extra[:, 0:1] + 0.5).astype(jnp.int32)
    found = lax.broadcasted_iota(jnp.int32, (rows, pairs), 1) == index
    of_query, of_doc = found & (row % 4 < 2), found & (row % 4 >= 2)

    def units(chosen):
        halves = [
            dot((chosen & (row // 4 == which)).astype(F32).astype(BF16), low, ((0,), (0,))) for which in range(2)
        ]
        return jnp.concatenate(halves, axis=1).astype(BF16)

    units_q, units_d = units(of_query), units(of_doc)
    exact = functools.partial(
        lax.dot_general, precision=lax.Precision.HIGHEST, preferred_element_type=F32
    )
    plain, turned, over_rows = (((1,), (0,)), ((), ())), (((1,), (1,)), ((), ())), (((0,), (0,)), ((), ()))
    extra = exact((of_query & (row < 4)).astype(F32), extra, over_rows)
    weight = extra[:, 2:3] / 16.0 + extra[:, 3:4] / 4096.0 + extra[:, 4:5] / 1048576.0
    similarity = dot(units_q, units_d, ((1,), (1,))) / soft
    columns = lax.broadcasted_iota(jnp.int32, similarity.shape, 1)
    target = (columns == (extra[:, 1:2] + 0.5).astype(jnp.int32)).astype(F32)
    highest = jnp.max(similarity, axis=1, keepdims=True)
    log_norm = highest + jnp.log(jnp.sum(jnp.exp(similarity - highest), axis=1, keepdims=True))
    picked = jnp.sum(target * similarity, axis=1, keepdims=True)
    loss = jnp.sum(weight * (log_norm - picked), axis=0, keepdims=True) / pairs
    loss_ref[...] = jnp.broadcast_to(loss, loss_ref.shape)
    grad = weight * (jnp.exp(similarity - log_norm) - target) / pairs
    line = lax.broadcasted_iota(jnp.int32, (8, pairs), 0)
    column = lax.broadcasted_iota(jnp.int32, (8, pairs), 1)
    my_queries = (column == jnp.where(line == 0, ids[0], ids[1])) & (line < 2)
    my_docs = (column == jnp.where(line == 0, ids[2], ids[3])) & (line < 2)
    query_rows = exact(my_queries.astype(F32), grad, plain)
    doc_rows = exact(my_docs.astype(F32), grad, turned)
    query_grad_ref[...] = exact(query_rows, units_d.astype(F32), plain) / soft
    doc_grad_ref[...] = exact(doc_rows, units_q.astype(F32), plain) / soft


def loss_and_grads(ids, messages, soft, width):
    vmem = pl.BlockSpec(memory_space=pltpu.VMEM)
    return pl.pallas_call(
        loss_kernel,
        in_specs=[pl.BlockSpec(memory_space=pltpu.SMEM), vmem, vmem],
        out_specs=[vmem, vmem, vmem],
        out_shape=[
            jax.ShapeDtypeStruct((8, 128), F32),
            jax.ShapeDtypeStruct((8, width), F32),
            jax.ShapeDtypeStruct((8, width), F32),
        ],
        compiler_params=params(),
        name="loss",
    )(ids, messages, jnp.broadcast_to(soft.reshape(1, 1), (8, 128)))


def wide_unfold_kernel(piece, *refs):
    gate_ref, up_ref, down_ref = refs[-3:]
    gate_ref[...] = piece[0, 0].astype(F32)
    up_ref[...] = piece[0, 1].astype(F32)
    span = piece.shape[3] // 2
    block = jnp.concatenate([piece[0, 2, :, :span], piece[0, 2, :, span:]], axis=0)
    down_ref[...] = block.astype(F32).T


def wide_unfold(chunk, pieces, before, width, inner, after=()):
    quarter, span = pieces.shape[2:]
    chunks = inner // (2 * span)
    place = pl.BlockSpec((quarter, span), lambda i: (i // 2, (i % 2) * chunks + chunk))
    return pl.pallas_call(
        wide_unfold_kernel,
        grid=(4,),
        in_specs=[pl.BlockSpec((1, *pieces.shape[1:]), lambda i: (i, 0, 0, 0))]
        + anywhere(len(before) + len(after)),
        out_specs=[
            place, place,
            pl.BlockSpec((span // 2, 2 * quarter), lambda i: (2 * chunk + i % 2, i // 2)),
        ],
        out_shape=[
            jax.ShapeDtypeStruct((width // 2, inner), F32),
            jax.ShapeDtypeStruct((width // 2, inner), F32),
            jax.ShapeDtypeStruct((inner // 2, width), F32),
        ],
        input_output_aliases={1 + at: at for at in range(len(before))},
        compiler_params=pltpu.CompilerParams(vmem_limit_bytes=16 * 1024 * 1024),
        cost_estimate=cost(3),
        name="wide_unfold",
    )(pieces, *before, *after)


def wide_unfold_parts_kernel(meta, p00, p01, p10, p11, *refs):
    gate_ref, up_ref, down_ref = refs[-3:]
    for other_core in range(2):
        for other_row in range(2):
            piece = ((p00, p01), (p10, p11))[other_core][other_row]

            @pl.when((pl.program_id(0) == other_core) & (pl.program_id(1) == other_row))
            def _():
                gate_ref[...] = piece[0].astype(F32)
                up_ref[...] = piece[1].astype(F32)
                span = piece.shape[2] // 2
                block = jnp.concatenate([piece[2, :, :span], piece[2, :, span:]], axis=0)
                down_ref[...] = block.astype(F32).T


def wide_unfold_parts(meta, chunk, pieces, before, width, inner, after=()):
    quarter, span = pieces[0].shape[1:]
    chunks = inner // (2 * span)
    aliased = [pl.BlockSpec(memory_space=pl.ANY)] * len(before)
    grid_spec = pltpu.PrefetchScalarGridSpec(
        num_scalar_prefetch=1,
        grid=(2, 2),
        in_specs=[resident(p.shape) for p in pieces] + aliased + anywhere(len(after)),
        out_specs=[
            pl.BlockSpec(
                (quarter, span), lambda c, r, m: (m[ROW] ^ r, (m[CORE] ^ c) * chunks + chunk)
            )
            for _ in range(2)
        ]
        + [
            pl.BlockSpec(
                (span // 2, 2 * quarter), lambda c, r, m: (2 * chunk + (m[CORE] ^ c), m[ROW] ^ r)
            )
        ],
    )
    return pl.pallas_call(
        wide_unfold_parts_kernel,
        grid_spec=grid_spec,
        out_shape=[
            jax.ShapeDtypeStruct((width // 2, inner), F32),
            jax.ShapeDtypeStruct((width // 2, inner), F32),
            jax.ShapeDtypeStruct((inner // 2, width), F32),
        ],
        input_output_aliases={5 + at: at for at in range(len(before))},
        compiler_params=pltpu.CompilerParams(vmem_limit_bytes=16 * 1024 * 1024),
        cost_estimate=cost(3),
        name="wide_unfold_parts",
    )(meta, *pieces, *before, *after)


AXES = ("fsdp", "blk")


class Links:
    def __init__(self, sides, blk):
        self.sides, self.blk, self.outer = sides, blk, blk // 4

    def swap(self, value, side=0, mask=0):
        pairs = [
            (f * self.blk + b, (f ^ side) * self.blk + (b ^ mask))
            for f in range(self.sides)
            for b in range(self.blk)
        ]
        return lax.ppermute(value, AXES, pairs)

    def core(self, value):
        return self.swap(value, mask=1)

    def row(self, value):
        return self.swap(value, mask=2)

    def side(self, value):
        return self.swap(value, side=1)

    def shift(self, value, by):
        pairs = [
            (f * self.blk + b, f * self.blk + (b + 4 * by) % self.blk)
            for f in range(self.sides)
            for b in range(self.blk)
        ]
        return lax.ppermute(value, AXES, pairs)

    def step(self, value, moves):
        pairs = [
            (f * self.blk + 4 * start + b, f * self.blk + 4 * end + b)
            for f in range(self.sides)
            for start, end in moves
            for b in range(4)
        ]
        return lax.ppermute(value, AXES, pairs)

    def outer_masks(self):
        mask = 4
        while mask < self.blk:
            yield mask
            mask *= 2

    def gather(self, value):
        both = jnp.concatenate([value, self.core(value)], axis=0)
        plane = jnp.concatenate(
            [both, self.swap(both, 1, 0), self.swap(both, 0, 2), self.swap(both, 1, 2)], axis=0
        )
        return jnp.concatenate(
            [plane] + [self.shift(plane, by) for by in range(1, self.outer)], axis=0
        )

    def stages(self, keep, send, row_first, by_swaps=False):
        add = lambda *terms: sum(term.astype(F32) for term in terms).astype(BF16)
        now = yield
        now = yield (send := tie(send, now))
        received = tie(self.core(send), now)
        if row_first:
            now = yield (away := add(keep[:, 1], received[:, 1]))
            across = tie(self.row(away), now)
            now = yield (away := add(keep[1, 0], received[1, 0], across[1]))
            last = self.side(away)
        else:
            now = yield (away := add(keep[1], received[1]))
            across = tie(self.side(away), now)
            now = yield (away := add(keep[0, 1], received[0, 1], across[1]))
            last = self.row(away)
        mine = add(keep[0, 0], received[0, 0], across[0], tie(last, now))
        if self.outer == 4:
            outer = lax.axis_index("blk") // 4
            now = yield mine
            mine = add(mine, tie(self.step(mine, ((0, 1), (3, 2))), now))
            now = yield mine
            mine = add(mine, tie(self.step(mine, ((1, 2), (2, 1))), now))
            now = yield mine
            result = tie(self.step(mine, ((1, 0), (2, 3))), now)
            mine = jnp.where((outer == 1) | (outer == 2), mine, result)
        else:
            for mask in self.outer_masks():
                now = yield mine
                mine = add(mine, tie(self.swap(mine, mask=mask), now))
        if by_swaps:
            now = yield mine
            other = tie(self.row(mine), now)
            yield other
            return mine, other, self.core(mine), self.core(other)
        groups = [[at + part for part in range(4)] for at in range(0, self.blk, 4)]
        flat = mine.reshape(-1, mine.shape[-1])
        gathered = lax.all_gather(flat, "blk", axis_index_groups=groups, axis=0, tiled=True)
        yield mine
        return gathered

    def stages_small(self, value):
        now = yield
        for side, mask in [(0, 1), (1, 0), (0, 2)] + [(0, mask) for mask in self.outer_masks()]:
            value = tie(value, now)
            now = yield value
            value = value + self.swap(value, side, mask)
        return value


def tie(value, now):
    return lax.optimization_barrier((value, now))[0]


class Flow:
    def __init__(self):
        self.sums, self.done = {}, {}

    def begin(self, name, stages):
        next(stages)
        self.sums[name] = stages

    def forward(self, now, *names):
        sent = []
        for name in names:
            if name in self.done:
                continue
            try:
                sent.append(self.sums[name].send(now))
            except StopIteration as end:
                self.done[name] = end.value
        return tuple(sent)

    def result(self, now, name):
        while name not in self.done:
            self.forward(now, name)
        return self.done[name]


def part_of(share, parts, at):
    size = share.shape[0] // parts
    return lax.dynamic_slice_in_dim(share, at * size, size, 0)


def body(
    question_activations,
    passage_activations,
    question_unpadded_counts,
    passage_unpadded_counts,
    correct_passage_index,
    query_weights,
    softness_factor,
    combined_projection_matrix,
    mixing_result_matrix,
    gating_matrix,
    widening_matrix,
    narrowing_matrix,
    initial_layernorm_scale,
    initial_layernorm_shift,
    later_layernorm_scale,
    later_layernorm_shift,
):
    doc_len, width = passage_activations.shape[1:]
    query_len = question_activations.shape[1]
    inner = gating_matrix.shape[1]
    assert passage_activations.shape[0] == 2 and doc_len == 6 * BLOCK and 2 * query_len == BLOCK
    links = Links(lax.axis_size("fsdp"), lax.axis_size("blk"))
    side, blk = lax.axis_index("fsdp"), lax.axis_index("blk")
    core, row = blk % 2, (blk // 2) % 2

    got_qkv = links.side(part_of(combined_projection_matrix, 2, core))
    quarter = row * 2 + core
    part_out = tie(part_of(mixing_result_matrix, 2, core), got_qkv)
    part_gate = tie(part_of(gating_matrix, 4, quarter), got_qkv)
    got_out, got_gate = links.side(part_out), links.side(part_gate)
    pieces_qkv = (combined_projection_matrix, got_qkv, links.core(got_qkv))
    vectors = jnp.stack(
        [initial_layernorm_scale, initial_layernorm_shift, later_layernorm_scale, later_layernorm_shift]
    )
    others = links.side(vectors)
    vectors = jnp.concatenate(
        [jnp.where(side == 0, vectors, others), jnp.where(side == 0, others, vectors)], axis=1
    ).astype(F32)
    gain_one, bias_one, gain_two, bias_two = (vectors[at : at + 1] for at in range(4))

    per_chip = passage_unpadded_counts.astype(jnp.int32)
    across = links.core(per_chip)
    four = jnp.where(core == 0, jnp.concatenate([per_chip, across]), jnp.concatenate([across, per_chip]))
    blocks = (four + BLOCK - 1) // BLOCK
    work = blocks * (10 + blocks)
    total = jnp.sum(work)
    loads = jnp.stack([work[0] + work[at] for at in (1, 2, 3)])
    plan = jnp.argmin(jnp.maximum(loads, total - loads)).astype(jnp.int32)
    stay = (plan == 0).astype(jnp.int32)
    slot_of = lambda which: jnp.where(which == 0, 1, jnp.where(plan == 1, 0, 1))
    slot = slot_of(core)
    sent_doc = lax.dynamic_index_in_dim(passage_activations, slot, 0, keepdims=False)
    first_doc = lax.dynamic_index_in_dim(passage_activations, 1 - slot, 0, keepdims=False)
    second_doc = jnp.where(stay == 1, sent_doc, links.core(sent_doc))
    own_counts = per_chip[1 - slot], jnp.where(stay == 1, per_chip[slot], across[slot_of(1 - core)])
    doc_counts, query_counts = jnp.stack(own_counts), question_unpadded_counts
    device = side * links.blk + blk
    ids = jnp.stack(
        [
            2 * device, 2 * device + 1, 2 * device + 1 - slot,
            jnp.where(stay == 1, 2 * device + slot, 2 * (device ^ 1) + slot_of(1 - core)),
        ]
    ).astype(jnp.int32)

    rows = -(-(2 * doc_len + BLOCK) // TILE) * TILE
    meta, table_block, counts, owner = layout(doc_counts, query_counts, rows, core, side, row, slot, stay)
    tables = tuple(jnp.asarray(table) for table in rotary_tables(doc_len, query_len))
    x = pack_rows(first_doc, second_doc, question_activations, meta, rows)

    qkv, wqkv = project(meta, table_block, x, pieces_qkv, tables, (part_out, part_gate))
    got_out, got_gate = tie((got_out, got_gate), qkv)
    part_up = tie(part_of(widening_matrix, 4, quarter), qkv)
    far_out, along_gate, got_up = links.core(got_out), links.row(got_gate), links.side(part_up)
    att0, lse0 = attend(meta, qkv, 0, 2, (got_out, got_gate, part_up))
    along_gate, got_up = tie((along_gate, got_up), lse0)
    part_down = tie(part_of(narrowing_matrix, 4, quarter), lse0)
    far_gate = links.core(got_gate), links.core(along_gate)
    along_up, got_down = links.row(got_up), links.side(part_down)
    att1, lse1 = attend(meta, qkv, 1, 2, (far_out, along_gate, got_up, part_down))
    along_up, got_down = tie((along_up, got_down), lse1)
    far_up = links.core(got_up), links.core(along_up)
    along_down = links.row(got_down)
    att2, lse2 = attend(meta, qkv, 2, 2, (*far_gate, along_up, got_down))
    along_down = tie(along_down, lse2)
    far_down = links.core(got_down), links.core(along_down)
    att, lse = (att0, att1, att2), (lse0, lse1, lse2)
    weights = [
        (mixing_result_matrix, got_out, far_out),
        (gating_matrix, got_gate, along_gate, *far_gate),
        (widening_matrix, got_up, along_up, *far_up),
        (narrowing_matrix, got_down, along_down, *far_down),
    ]
    low, z1, r1, silu, slope, hidden, z2, r2, sums, wo, wg, wu, wd = forward(
        meta, counts, att, x, weights, gain_one, bias_one
    )

    groups = rows // (BLOCK // 2)
    used = (jnp.arange(groups) // (2 * TILE // BLOCK))[None, :] < meta[TILES]
    chosen = (owner[None, :] == jnp.arange(4)[:, None]) & used
    z_sums = jnp.sum(jnp.where(chosen[:, :, None], sums.reshape(1, groups, width), 0.0), axis=1)
    lengths = jnp.concatenate([doc_counts, query_counts]).astype(F32)[:, None]
    pooled = z_sums / lengths * gain_two + bias_two
    recip = lax.rsqrt(jnp.sum(pooled * pooled, axis=1, keepdims=True) + EPS_UNIT)
    unit = (pooled * recip).astype(BF16).astype(F32)
    high = jnp.floor(query_weights * 16.0)
    rest = (query_weights * 16.0 - high) * 256.0
    middle = jnp.floor(rest)
    lowest = jnp.floor((rest - middle) * 256.0)
    extra = jnp.stack(
        [ids.astype(BF16)]
        + [jnp.pad(part.astype(BF16), (0, 2)) for part in (correct_passage_index, high, middle, lowest)],
        axis=1,
    )
    extra = jnp.pad(extra, ((0, 0), (0, 123)))
    unit = jnp.concatenate([unit[2:], unit[:2]], axis=0).astype(BF16)
    message = jnp.concatenate(
        [
            jnp.concatenate([unit[:, : width // 2], extra], axis=1),
            jnp.concatenate([unit[:, width // 2 :], extra], axis=1),
        ],
        axis=0,
    )
    messages = links.gather(message)
    loss, grad_q, grad_d = loss_and_grads(ids, messages, softness_factor, width)
    grad_unit = jnp.concatenate([grad_d[:2], grad_q[:2]], axis=0)
    crossed = jnp.sum(grad_unit * pooled, axis=1, keepdims=True)
    grad_rows = (recip * grad_unit - pooled * recip**3 * crossed) / lengths
    grad_gain_two = jnp.sum(grad_rows * z_sums, axis=0)
    grad_bias_two = jnp.sum(grad_rows * lengths, axis=0)

    scaled = jnp.pad(grad_rows * gain_two, ((0, 4), (0, 0)))
    branch, first = norm_two_back(meta, counts, owner, z2, r2, scaled)
    flow = Flow()

    def wide(chunk, first, after):
        first, keep, send = ffn_back(
            meta, chunk, branch, low, hidden, silu, slope, wd, wg, wu, first, after
        )
        flow.begin("w%d" % chunk, links.stages(keep, send, chunk == 2, chunk == 2))
        return first, keep

    def score(pair, after):
        grads.append(
            attend_back(meta, pair, 1, qkv, grad_att, (lse[pair // 2], pair % 2), tables, after)
        )
        return grads[-1]

    def narrow(group, pairs, extra, after):
        keep, send = qkv_grad(meta, x, [grads[pair] for pair in pairs], extra, after)
        flow.begin("q%d" % group, links.stages(keep, send, group == 0))
        return keep

    grads = []
    first, now = wide(0, first, ())
    first, now = wide(1, first, flow.forward(now, "w0"))
    first, now = wide(2, first, flow.forward(now, "w0", "w1"))
    later = jnp.pad(jnp.stack([grad_gain_two, grad_bias_two]), ((2, 4), (0, 0)))
    sum_one, grad_att, now, *mixing = norm_one_back(
        meta, first, z1, r1, att, gain_one, wo, later, flow.forward(now, "w0", "w1", "w2")
    )
    flow.begin("s", links.stages_small(now))
    now = score(0, flow.forward(now, "w0", "w2", "s"))
    now = score(1, flow.forward(now, "w0", "s"))
    now = score(2, flow.forward(now, "w0", "w1", "s"))
    now = score(3, flow.forward(now, "w0", "w2"))
    now = narrow(0, range(4), mixing, flow.forward(now, "w1", "s"))
    now = score(4, flow.forward(now, "w1", "w2", "q0"))
    now = score(5, flow.forward(now, "w0", "w1", "w2", "q0", "s"))
    unfold = lambda chunk, before, after: wide_unfold(
        chunk, flow.result(now, "w%d" % chunk).reshape(4, 3, width // 4, -1), before, width, inner, after
    )
    grad_wide = unfold(0, (), ())
    now = narrow(1, range(4, 6), (), (*flow.forward(now, "w1", "w2", "s"), grad_wide[0]))
    (grad_docs,) = token_grad(0, meta, sum_one, grads, wqkv, flow.forward(now, "w2", "q0", "q1", "s"))
    moved, grad_queries = token_grad(
        1, meta, sum_one, grads, wqkv, (grad_docs, *flow.forward(grad_docs, "q0", "q1"))
    )
    other_moved, now = links.core(moved), moved
    flow.forward(now, "w1")
    grad_wide = unfold(1, grad_wide, flow.forward(now, "w2", "q0", "q1"))
    now = grad_wide[0]
    after = flow.forward(now, "w2", "q0", "q1")
    now = grad_docs = place_moved(meta, grad_docs, moved, other_moved, after)
    after = flow.forward(now, "w2", "q0", "q1")
    grad_wide = wide_unfold_parts(meta, 2, flow.result(grad_docs, "w2"), grad_wide, width, inner, after)
    while len(flow.done) < 6:
        flow.forward(grad_wide[0], "q0", "q1", "s")
    first_part, second_part = flow.done["q0"], flow.done["q1"]
    joint = first_part.shape[1] - width
    grad_qkv = jnp.concatenate(
        [
            part.astype(F32)
            for parts in zip(jnp.split(first_part[:, :joint], 3, axis=1), jnp.split(second_part, 3, axis=1))
            for part in parts
        ],
        axis=1,
    )
    grad_out = first_part[:, joint:].astype(F32)
    small = lax.dynamic_slice_in_dim(flow.done["s"], side * (width // 2), width // 2, 1)
    return (
        loss[0, :1],
        grad_queries,
        grad_docs,
        grad_qkv,
        grad_out,
        grad_wide[0],
        grad_wide[1],
        grad_wide[2],
        small[0],
        small[1],
        small[2],
        small[3],
    )


def solution(mesh):
    placed = (
        P(("fsdp", "blk"), None, None),
        P(("fsdp", "blk"), None, None),
        P(("fsdp", "blk")),
        P(("fsdp", "blk")),
        P(("fsdp", "blk")),
        P(("fsdp", "blk")),
        P(),
        P("fsdp", None),
        P("fsdp", None),
        P("fsdp", None),
        P("fsdp", None),
        P("fsdp", None),
        P("fsdp"),
        P("fsdp"),
        P("fsdp"),
        P("fsdp"),
    )
    return jax.shard_map(
        body,
        mesh=mesh,
        in_specs=placed,
        out_specs=(
            P(),
            P(("fsdp", "blk"), None, None),
            P(("fsdp", "blk"), None, None),
            P("fsdp", None),
            P("fsdp", None),
            P("fsdp", None),
            P("fsdp", None),
            P("fsdp", None),
            P("fsdp"),
            P("fsdp"),
            P("fsdp"),
            P("fsdp"),
        ),
        check_vma=False,
    )
```

```python
import functools

import jax
import jax.numpy as jnp
import numpy as np
from jax import lax
from jax.experimental import pallas as pl
from jax.experimental.pallas import tpu as pltpu
from jax.sharding import PartitionSpec as P

HEAD = 64
BLOCK = 128
TILE = 256
EPS_NORM = 1e-05
EPS_UNIT = 1e-06
MASKED = -1e30
F32 = jnp.float32
BF16 = jnp.bfloat16
PACE = 0.5
SPAN = 512
VMEM_LIMIT = 60 * 1024 * 1024
OFF0, OFF1, OFFQ, LEN0, LEN1, QLEN0, QLEN1, CNT0, CNT1, TILES, CORE, SIDE, ROW, SLOT, STAY = range(15)


def dot(left, right, contract=((1,), (0,))):
    return lax.dot_general(left, right, (contract, ((), ())), preferred_element_type=F32)


def cost(microseconds):
    return pl.CostEstimate(flops=int(microseconds * PACE * 1e9), bytes_accessed=0, transcendentals=0)


def params(**more):
    return pltpu.CompilerParams(vmem_limit_bytes=VMEM_LIMIT, **more)


def rotary_tables(doc_len, query_len):
    frequency = 1000.0 ** (-(np.arange(HEAD // 2, dtype=np.float32) * 2.0 / HEAD))
    positions = np.concatenate([np.arange(doc_len), np.arange(query_len), np.arange(query_len)])
    angles = positions.astype(np.float32)[:, None] * frequency.astype(np.float32)[None, :]
    cosine, sine = np.cos(angles), np.sin(angles)
    return (
        np.concatenate([cosine] * 4, axis=1).astype(np.float32),
        np.concatenate([-sine, sine, -sine, sine], axis=1).astype(np.float32),
    )


def swap_halves(pair):
    lane = lax.broadcasted_iota(jnp.int32, pair.shape, 1)
    return jnp.where(lane % HEAD < HEAD // 2, pltpu.roll(pair, 96, 1), pltpu.roll(pair, 32, 1))


def live(step, meta):
    return jnp.minimum(step, meta[TILES] - 1)


def tiled(columns, at=0):
    return pl.BlockSpec((TILE, columns), lambda i, m, *_: (live(i, m), at))


def while_live(kernel):
    @functools.wraps(kernel)
    def run(meta, *refs):
        @pl.when(pl.program_id(0) < meta[TILES])
        def _():
            kernel(meta, *refs)

    return run


def anywhere(count):
    return [pl.BlockSpec(memory_space=pl.ANY)] * count


def resident(shape):
    return pl.BlockSpec(shape, lambda *_: (0,) * len(shape), pipeline_mode=pl.Buffered(1))


def piece_copies(meta, rows, pieces, whole, sems):
    side, row, core = meta[SIDE], meta[ROW], meta[CORE]
    parts = len(pieces) - 1
    if parts == 2:
        places = [core, 1 - core]
    else:
        places = [row * 2 + core, (1 - row) * 2 + core, row * 2 + 1 - core, (1 - row) * 2 + 1 - core]
    size = rows // parts
    starts = [side * rows] + [(1 - side) * rows + place * size for place in places]
    return [
        pltpu.make_async_copy(
            piece, whole.at[pl.ds(pl.multiple_of(start, 16), piece.shape[0]), :], sems.at[at]
        )
        for at, (piece, start) in enumerate(zip(pieces, starts))
    ]


def qkv_kernel(meta, table_block, x_ref, cos_ref, sin_ref, *refs):
    pieces, (out_ref, turned_out, w_ref, turned, sems, out_sem) = refs[:3], refs[-6:]
    tile = pl.program_id(0)
    keep = pltpu.make_async_copy(turned, turned_out, out_sem)

    @pl.when(tile == 0)
    def _():
        copies = piece_copies(meta, pieces[0].shape[0], pieces, w_ref, sems)
        for copy in copies:
            copy.start()
        for copy in copies:
            copy.wait()

    @pl.when(tile == 1)
    def _():
        width = x_ref.shape[1]
        for pair in range(width // 128):
            for part in range(3):
                at, to = part * width + pair * 128, (pair * 3 + part) * 128
                turned[to : to + 128, :] = w_ref[:, at : at + 128].T
        keep.start()

    @pl.when(tile < meta[TILES])
    def _():
        x = x_ref[...]
        width = x.shape[1]

        def turn(part, acc):
            scale = HEAD**-0.5 if part == 0 else 1.0
            for sub in range(TILE // BLOCK):
                rows = slice(sub * BLOCK, (sub + 1) * BLOCK)
                table = pl.ds(table_block[tile * (TILE // BLOCK) + sub] * BLOCK, BLOCK)
                cosine, sine = cos_ref[table, :] * scale, sin_ref[table, :] * scale
                for group in range(width // 128):
                    pair = acc[rows, group * 128 : (group + 1) * 128]
                    turned_pair = pair * cosine + swap_halves(pair) * sine
                    at = part * width + group * 128
                    out_ref[rows, at : at + 128] = turned_pair.astype(BF16)

        queries = dot(x, w_ref[:, :width])
        keys = dot(x, w_ref[:, width : 2 * width])
        turn(0, queries)
        values = dot(x, w_ref[:, 2 * width :])
        turn(1, keys)
        out_ref[:, 2 * width :] = values.astype(BF16)

    @pl.when(tile == pl.num_programs(0) - 1)
    def _():
        keep.wait()


def project(meta, table_block, x, pieces, tables, after=()):
    rows, width = x.shape
    whole = (width, 3 * width)
    grid_spec = pltpu.PrefetchScalarGridSpec(
        num_scalar_prefetch=2,
        grid=(rows // TILE,),
        in_specs=[tiled(width), resident(tables[0].shape), resident(tables[1].shape)]
        + anywhere(len(pieces) + len(after)),
        out_specs=[tiled(3 * width)] + anywhere(1),
        scratch_shapes=[
            pltpu.VMEM(whole, BF16),
            pltpu.VMEM(whole[::-1], BF16),
            pltpu.SemaphoreType.DMA((len(pieces),)),
            pltpu.SemaphoreType.DMA,
        ],
    )
    return pl.pallas_call(
        qkv_kernel,
        grid_spec=grid_spec,
        out_shape=[
            jax.ShapeDtypeStruct((rows, 3 * width), BF16),
            jax.ShapeDtypeStruct(whole[::-1], BF16),
        ],
        compiler_params=params(),
        cost_estimate=cost(11),
        name="qkv",
    )(meta, table_block, x, *tables, *pieces, *after)


def split_pair(pair):
    lane = lax.broadcasted_iota(jnp.int32, pair.shape, 1)
    zero = jnp.zeros_like(pair)
    return jnp.concatenate(
        [jnp.where(lane < HEAD, pair, zero), jnp.where(lane < HEAD, zero, pair)], axis=0
    )


def mask_keys(scores, last, valid):
    rows = lax.broadcasted_iota(jnp.int32, (BLOCK, scores.shape[1]), 0)
    tail = jnp.where(rows < valid, scores[last * BLOCK :, :], MASKED)
    if last == 0:
        return tail
    return jnp.concatenate([scores[: last * BLOCK, :], tail], axis=0)


def query_mask(meta, scores):
    half = scores.shape[0] // 2
    key = lax.broadcasted_iota(jnp.int32, scores.shape, 0)
    row = lax.broadcasted_iota(jnp.int32, scores.shape, 1) % (2 * half)
    length = jnp.where(key < half, meta[QLEN0], meta[QLEN1])
    keep = ((key < half) == (row < half)) & (key % half < length)
    return jnp.where(keep, scores, MASKED)


def split_turned(pair):
    turned = pair.T
    row = lax.broadcasted_iota(jnp.int32, turned.shape, 0)
    zero = jnp.zeros_like(turned)
    return jnp.concatenate(
        [jnp.where(row < HEAD, turned, zero), jnp.where(row < HEAD, zero, turned)], axis=1
    )


def stack_heads(pair_wide):
    half = pair_wide.shape[1] // 2
    return jnp.concatenate([pair_wide[:, :half], pair_wide[:, half:]], axis=0)


def attend_kernel(meta, q_ref, k_ref, v_ref, *refs):
    out_ref, lse_ref = refs[-2:]

    def scores_of(start, size, keys, masked):
        return masked(dot(keys, split_pair(q_ref[pl.ds(start, size), :]), ((1,), (1,))))

    def finish(start, size, scores, values):
        rows = pl.ds(start, size)
        highest = jnp.max(scores, axis=0, keepdims=True)
        exponent = jnp.exp(scores - highest)
        total = jnp.sum(exponent, axis=0, keepdims=True)
        attended = dot(values, stack_heads(exponent.astype(BF16)))
        recip = 1.0 / total
        row = lax.broadcasted_iota(jnp.int32, attended.shape, 0)
        attended = attended * jnp.where(row < HEAD, recip[:, :size], recip[:, size:])
        out_ref[rows, :] = attended.T.astype(BF16)
        log_norm = highest + jnp.log(total)
        lse_ref[0, 0:1, rows] = log_norm[:, :size]
        lse_ref[0, 1:2, rows] = log_norm[:, size:]

    def run(starts, size, keys, values, masked):
        ahead = scores_of(starts[0], size, keys, masked)
        for at, start in enumerate(starts):
            scores = ahead
            if at + 1 < len(starts):
                ahead = scores_of(starts[at + 1], size, keys, masked)
            finish(start, size, scores, values)

    @pl.loop(0, 2)
    def _(doc):
        start = pl.multiple_of(meta[OFF0 + doc], BLOCK)
        for blocks in range(1, 7):

            @pl.when(meta[CNT0 + doc] == blocks)
            def _():
                whole = pl.ds(start, blocks * BLOCK)
                valid = meta[LEN0 + doc] - (blocks - 1) * BLOCK
                starts = [pl.multiple_of(start + at * TILE, BLOCK) for at in range((blocks + 1) // 2)]
                run(
                    starts, TILE, k_ref[whole, :], split_turned(v_ref[whole, :]),
                    lambda scores: mask_keys(scores, blocks - 1, valid),
                )

    first = pl.multiple_of(meta[OFFQ], BLOCK)
    rows = pl.ds(first, BLOCK)
    run(
        [first], BLOCK, k_ref[rows, :], split_turned(v_ref[rows, :]), functools.partial(query_mask, meta)
    )
    out_ref[pl.ds(first + BLOCK, BLOCK), :] = jnp.zeros((BLOCK, 128), BF16)


def attend(meta, qkv, group, members, before=(), after=()):
    rows, width = qkv.shape[0], qkv.shape[1] // 3
    pairs = width // 128

    def column(part):
        return pl.BlockSpec((rows, 128), lambda h, *_: (0, part * pairs + group * members + h))

    grid_spec = pltpu.PrefetchScalarGridSpec(
        num_scalar_prefetch=1,
        grid=(members,),
        in_specs=[column(0), column(1), column(2)] + anywhere(len(before) + len(after)),
        out_specs=[
            column(0),
            pl.BlockSpec((1, 8, rows), lambda h, *_: (group * members + h, 0, 0)),
        ],
    )
    return pl.pallas_call(
        attend_kernel,
        grid_spec=grid_spec,
        out_shape=[
            jax.ShapeDtypeStruct((rows, width), BF16),
            jax.ShapeDtypeStruct((pairs, 8, rows), F32),
        ],
        input_output_aliases={4 + at: at for at in range(len(before))},
        compiler_params=params(),
        cost_estimate=cost(13),
        name="attend",
    )(meta, qkv, qkv, qkv, *before, *after)


def normalize(summed):
    centered = summed - jnp.mean(summed, axis=-1, keepdims=True)
    recip = lax.rsqrt(jnp.mean(centered * centered, axis=-1, keepdims=True) + EPS_NORM)
    return centered * recip, recip


def forward_kernel(
    meta, counts, att_ref, x_ref, gain_ref, bias_ref, *refs,
):
    outs, scratch = refs[-18:-7], refs[-7:]
    pieces = [refs[0:3], refs[3:8], refs[8:13], refs[13:18]]
    low_ref, z1_ref, r1_ref, saved_ref, z2_ref, r2_ref, sums_ref = outs[:7]
    whole_outs = outs[7:]
    wholes, (sems, out_sems) = scratch[:4], scratch[5:]
    wo_ref, wg_ref, wu_ref, wd_ref = wholes
    tile = pl.program_id(0)
    copies = [
        piece_copies(meta, pieces[at][0].shape[0], pieces[at], wholes[at], sems.at[at])
        for at in range(4)
    ]
    keeps = [
        pltpu.make_async_copy(wholes[at], whole_outs[at], out_sems.at[at]) for at in range(4)
    ]

    @pl.when(tile == 0)
    def _():
        for group in copies:
            for copy in group:
                copy.start()

    def ready(which):
        @pl.when(tile == 0)
        def _():
            for at in which:
                for copy in copies[at]:
                    copy.wait()
                keeps[at].start()

    ready((0,))

    @pl.when(tile < meta[TILES])
    def _():
        z1, r1 = normalize(x_ref[...].astype(F32) + dot(att_ref[...], wo_ref[...]))
        z1_ref[...] = z1.astype(BF16)
        r1_ref[...] = r1
        normed = z1 * gain_ref[...] + bias_ref[...]
        low_ref[...] = normed.astype(BF16)
        scratch[4][...] = normed

    ready((1, 2, 3))

    @pl.when(tile < meta[TILES])
    def _():
        low = low_ref[...]
        total = scratch[4][...]
        inner, chunk = wg_ref.shape[1], SPAN
        chunks = inner // (2 * chunk)

        def products(at):
            columns = slice(at, at + chunk)
            return dot(low, wg_ref[:, columns]), dot(low, wu_ref[:, columns])

        ahead = products(0)
        for at in range(0, inner, chunk):
            columns = slice(at, at + chunk)
            gate, up = ahead
            if at + chunk < inner:
                ahead = products(at + chunk)
            sigmoid = 0.5 * jnp.tanh(0.5 * gate) + 0.5
            silu = gate * sigmoid
            hidden = (silu * up).astype(BF16)
            slope = (up * (sigmoid + silu * (1.0 - sigmoid))).astype(BF16)
            which = at // chunk
            for kind, value in enumerate((hidden, silu.astype(BF16), slope)):
                to = ((which % chunks) * 6 + kind * 2 + which // chunks) * chunk
                saved_ref[:, to : to + chunk] = value
            total = total + dot(hidden, wd_ref[columns, :])
        z2, r2 = normalize(total)
        z2_ref[...] = z2.astype(BF16)
        r2_ref[...] = r2
        half = BLOCK // 2
        inside = lax.broadcasted_iota(jnp.int32, (half, z2.shape[1]), 0)
        for group in range(TILE // half):
            valid = counts[tile * (TILE // half) + group]
            kept = jnp.where(inside < valid, z2[group * half : (group + 1) * half, :], 0.0)
            sums_ref[0, group : group + 1, :] = jnp.sum(kept, axis=0, keepdims=True)

    @pl.when(tile == pl.num_programs(0) - 1)
    def _():
        for keep in keeps:
            keep.wait()


def forward(meta, counts, att, x, pieces, gain, bias, after=()):
    rows, width = x.shape
    inner = pieces[1][0].shape[1]
    wholes = [(width, width), (width, inner), (width, inner), (inner, width)]

    def array(columns, kind):
        return jax.ShapeDtypeStruct((rows, columns), kind)

    grid_spec = pltpu.PrefetchScalarGridSpec(
        num_scalar_prefetch=2,
        grid=(rows // TILE,),
        in_specs=[tiled(width), tiled(width)]
        + [resident(gain.shape), resident(bias.shape)]
        + anywhere(18 + len(after)),
        out_specs=[
            tiled(width), tiled(width), tiled(1), tiled(3 * inner), tiled(width), tiled(1),
            pl.BlockSpec((1, 4, width), lambda i, m, *_: (live(i, m), 0, 0)),
        ]
        + anywhere(4),
        scratch_shapes=[pltpu.VMEM(shape, BF16) for shape in wholes]
        + [
            pltpu.VMEM((TILE, width), F32),
            pltpu.SemaphoreType.DMA((4, 5)),
            pltpu.SemaphoreType.DMA((4,)),
        ],
    )
    return pl.pallas_call(
        forward_kernel,
        grid_spec=grid_spec,
        out_shape=[
            array(width, BF16), array(width, BF16), array(1, F32), array(3 * inner, BF16),
            array(width, BF16), array(1, F32),
            jax.ShapeDtypeStruct((rows // TILE, 4, width), F32),
        ]
        + [jax.ShapeDtypeStruct(shape, BF16) for shape in wholes],
        compiler_params=params(),
        cost_estimate=cost(42),
        name="forward",
    )(meta, counts, att, x, gain, bias, *[p for group in pieces for p in group], *after)


def norm_two_back(counts, owner, tile, z_ref, r_ref, scaled_ref):
    half = BLOCK // 2
    width = z_ref.shape[1]
    inside = lax.broadcasted_iota(jnp.int32, (half, width), 0)
    grads = []
    for group in range(TILE // half):
        at = tile * (TILE // half) + group
        rows = slice(group * half, (group + 1) * half)
        scaled = scaled_ref[pl.ds(owner[at], 1), :]
        z = z_ref[rows, :].astype(F32)
        plain = jnp.mean(scaled, axis=-1, keepdims=True)
        cross = jnp.mean(scaled * z, axis=-1, keepdims=True)
        grad = r_ref[rows, :] * (scaled - plain - z * cross)
        grads.append(jnp.where(inside < counts[at], grad, 0.0))
    return jnp.concatenate(grads, axis=0)


def ffn_back_kernel(starts, meta, counts, owner, *refs):
    @pl.when(pl.program_id(0) < meta[TILES])
    def _():
        ffn_back_tile(starts, meta, counts, owner, *refs)


def ffn_back_tile(
    starts, meta, counts, owner, low_ref, saved_ref, wd0, wd1, wg0, wg1, wu0, wu1, *refs,
):
    tile = pl.program_id(0)
    span = wd0.shape[0]
    acc_g, acc_u, acc_d, wd_turned, wg_turned, wu_turned = refs[-6:]
    keep_ref, send_ref = refs[-8:-6]
    part_out = refs[-9]
    width = low_ref.shape[1]

    @pl.when(tile == 0)
    def _():
        acc_g[...] = jnp.zeros_like(acc_g)
        acc_u[...] = jnp.zeros_like(acc_u)
        acc_d[...] = jnp.zeros_like(acc_d)
        for half, (wd, wg, wu) in enumerate(((wd0, wg0, wu0), (wd1, wg1, wu1))):
            columns = slice(half * span, (half + 1) * span)
            wd_turned[:, columns] = wd[...].T
            wg_turned[columns, :] = wg[...].T
            wu_turned[columns, :] = wu[...].T

    if starts:
        branch = norm_two_back(counts, owner, tile, *refs[:3]).astype(BF16)
        part_out[:, :width] = branch
    else:
        branch = refs[0][...]
    low_t = low_ref[...].T
    branch_t = branch.T
    hiddens = [
        dot(branch, wd_turned[:, half * span : (half + 1) * span]) for half in range(2)
    ]
    total = None
    for half in range(2):
        columns = slice(half * span, (half + 1) * span)
        hid, silu, slope = (
            saved_ref[:, (kind * 2 + half) * span : (kind * 2 + half + 1) * span] for kind in range(3)
        )
        acc_d[:, columns] += dot(branch_t, hid)
        grad_hidden = hiddens[half]
        grad_gate = (grad_hidden * slope.astype(F32)).astype(BF16)
        grad_up = (grad_hidden * silu.astype(F32)).astype(BF16)
        part = dot(grad_gate, wg_turned[columns, :]) + dot(grad_up, wu_turned[columns, :])
        total = part if total is None else total + part
        acc_g[:, columns] += dot(low_t, grad_gate)
        acc_u[:, columns] += dot(low_t, grad_up)
    part_out[:, part_out.shape[1] - width :] = total.astype(BF16)

    @pl.when(tile == meta[TILES] - 1)
    def _():
        rows, quarter = acc_g.shape[0] // 4, acc_g.shape[0] // 4
        side, row, core = meta[SIDE], meta[ROW], meta[CORE]
        for other_core, out in ((0, keep_ref), (1, send_ref)):
            columns = pl.ds(pl.multiple_of((core ^ other_core) * span, span), span)
            inner = pl.ds(
                pl.multiple_of((core ^ other_core) * (span // 2), span // 2), span // 2
            )
            for other_side in range(2):
                for other_row in range(2):
                    at = (side ^ other_side) * 2 + (row ^ other_row)
                    lines = pl.ds(pl.multiple_of(at * quarter, quarter), quarter)
                    out[other_side, other_row, 0] = acc_g[lines, columns].astype(BF16)
                    out[other_side, other_row, 1] = acc_u[lines, columns].astype(BF16)
                    left = pl.multiple_of(
                        (side ^ other_side) * span + (core ^ other_core) * (span // 2), span // 2
                    )
                    for part in range(2):
                        lines = pl.ds(
                            pl.multiple_of((row ^ other_row) * 2 * quarter + part * quarter, quarter),
                            quarter,
                        )
                        out[
                            other_side, other_row, 2, :, part * (span // 2) : (part + 1) * (span // 2)
                        ] = acc_d[lines, pl.ds(left, span // 2)].astype(BF16)


def ffn_back(meta, counts, owner, chunk, low, saved, wd, wg, wu, given, after=()):
    rows, width = low.shape
    inner, span = wg.shape[1], SPAN
    starts = len(given) == 3
    halves = (chunk, chunk + inner // (2 * span))

    def fixed(shape, index):
        return pl.BlockSpec(shape, lambda i, *_: index, pipeline_mode=pl.Buffered(1))

    if starts:
        given_specs = [tiled(width), tiled(1), resident(given[2].shape)]
    else:
        given_specs = [tiled(width)] + anywhere(len(given) - 1)
    grid_spec = pltpu.PrefetchScalarGridSpec(
        num_scalar_prefetch=3,
        grid=(rows // TILE,),
        in_specs=[tiled(width), tiled(6 * span, chunk)]
        + [fixed((span, width), (at, 0)) for at in halves]
        + [fixed((width, span), (0, at)) for _ in range(2) for at in halves]
        + given_specs
        + anywhere(len(after)),
        out_specs=[tiled(2 * width) if starts else tiled(width, len(given) - 1)]
        + [pl.BlockSpec((2, 2, 3, width // 4, span), lambda i, *_: (0, 0, 0, 0, 0))] * 2,
        scratch_shapes=[pltpu.VMEM((width, 2 * span), F32)] * 3
        + [pltpu.VMEM((width, 2 * span), BF16)]
        + [pltpu.VMEM((2 * span, width), BF16)] * 2,
    )
    piece = jax.ShapeDtypeStruct((2, 2, 3, width // 4, span), BF16)
    return pl.pallas_call(
        functools.partial(ffn_back_kernel, starts),
        grid_spec=grid_spec,
        out_shape=[jax.ShapeDtypeStruct((rows, 2 * width), BF16), piece, piece],
        input_output_aliases={12: 0} if len(given) == 2 else {},
        compiler_params=params(),
        cost_estimate=cost(23),
        name="ffn_back",
    )(
        meta, counts, owner, low, saved, wd, wd, wg, wg, wu, wu, *given, *after,
    )


def out_pieces(meta, acc, keep_ref, send_ref):
    part = acc.shape[0] // 8
    side, row, core = meta[SIDE], meta[ROW], meta[CORE]
    for other_core, out in ((0, keep_ref), (1, send_ref)):
        for other_side in range(2):
            for other_row in range(2):
                at = ((side ^ other_side) * 2 + (row ^ other_row)) * 2 + (core ^ other_core)
                lines = pl.ds(pl.multiple_of(at * part, part), part)
                out[other_side, other_row, :, : acc.shape[1]] = acc[lines, :].astype(BF16)


@while_live
def norm_one_back_kernel(
    meta, head_ref, tail_ref, z_ref, r_ref, att_ref, gain_ref, wo_ref, later_ref, *refs,
):
    sum_ref, att_grad_ref, gains_out, keep_ref, send_ref, acc, wo_turned = refs[-7:]
    tile = pl.program_id(0)

    @pl.when(tile == 0)
    def _():
        acc[...] = jnp.zeros_like(acc)
        gains_out[...] = later_ref[...]
        wo_turned[...] = wo_ref[...].T

    width = wo_ref.shape[0]
    first = sum(ref[:, at : at + width].astype(F32) for ref in (head_ref, tail_ref) for at in (0, width))
    z = z_ref[...].astype(F32)
    scaled = first * gain_ref[...]
    plain = jnp.mean(scaled, axis=-1, keepdims=True)
    cross = jnp.mean(scaled * z, axis=-1, keepdims=True)
    grad = r_ref[...] * (scaled - plain - z * cross)
    sum_ref[...] = grad
    low = grad.astype(BF16)
    att_grad_ref[...] = dot(low, wo_turned[...]).astype(BF16)
    acc[...] += dot(att_ref[...].T, low)
    gains_out[0:1, :] += jnp.sum(first * z, axis=0, keepdims=True)
    gains_out[1:2, :] += jnp.sum(first, axis=0, keepdims=True)

    @pl.when(tile == meta[TILES] - 1)
    def _():
        out_pieces(meta, acc, keep_ref, send_ref)


def norm_one_back(meta, terms, z, recip, att, gain, wo, later, after=()):
    rows, width = z.shape
    block = (2, 2, width // 8, width)
    piece = jax.ShapeDtypeStruct(block, BF16)
    grid_spec = pltpu.PrefetchScalarGridSpec(
        num_scalar_prefetch=1,
        grid=(rows // TILE,),
        in_specs=[tiled(2 * width), tiled(2 * width), tiled(width)]
        + [tiled(1), tiled(width)]
        + [resident(gain.shape), resident(wo.shape), resident(later.shape)]
        + anywhere(len(after)),
        out_specs=[tiled(width), tiled(width), pl.BlockSpec((8, width), lambda i, *_: (0, 0))]
        + [pl.BlockSpec(block, lambda i, *_: (0, 0, 0, 0))] * 2,
        scratch_shapes=[pltpu.VMEM((width, width), F32), pltpu.VMEM((width, width), BF16)],
    )
    return pl.pallas_call(
        norm_one_back_kernel,
        grid_spec=grid_spec,
        out_shape=[
            jax.ShapeDtypeStruct((rows, width), F32), jax.ShapeDtypeStruct((rows, width), BF16),
            jax.ShapeDtypeStruct((8, width), F32), piece, piece,
        ],
        compiler_params=params(),
        cost_estimate=cost(12),
        name="norm_one_back",
    )(meta, *terms, z, recip, att, gain, wo, later, *after)


def attend_back_kernel(meta, q_ref, k_ref, v_ref, g_ref, att_ref, lse_ref, cos_ref, sin_ref, *refs):
    out_ref, key_acc, value_acc = refs[-3:]

    def turn_back(grad, table):
        cosine, sine = cos_ref[table, :], sin_ref[table, :]
        return (grad * cosine - swap_halves(grad) * sine).astype(BF16)

    def products(start, size, keys, values, limit, masked):
        rows = pl.ds(start, size)
        queries, grads = split_pair(q_ref[rows, :]), split_pair(g_ref[rows, :])
        log_norm = jnp.concatenate([lse_ref[0, 0:1, rows], lse_ref[0, 1:2, rows]], axis=1)
        if limit is not None:
            column = lax.broadcasted_iota(jnp.int32, log_norm.shape, 1) % size
            log_norm = jnp.where(column < limit, log_norm, -MASKED)
        both = g_ref[rows, :].astype(F32) * att_ref[rows, :].astype(F32)
        head = lax.broadcasted_iota(jnp.int32, (8, 128), 1) // HEAD
        ones = (head == lax.broadcasted_iota(jnp.int32, (8, 128), 0)).astype(F32)
        inner = lax.dot_general(
            ones, both, (((1,), (1,)), ((), ())), precision=lax.Precision.HIGHEST, preferred_element_type=F32
        )
        inner = jnp.concatenate([inner[0:1, :], inner[1:2, :]], axis=1)
        scores = masked(dot(keys, queries, ((1,), (1,))))
        grad_probs = dot(values, grads, ((1,), (1,)))
        return queries, grads, log_norm, inner, scores, grad_probs

    def finish(queries, grads, log_norm, inner, scores, grad_probs, keys_split):
        probs = jnp.exp(scores - log_norm)
        grad_scores = (probs * (grad_probs - inner)).astype(BF16)
        grad_query = (dot(keys_split, stack_heads(grad_scores)) * HEAD**-0.5).T
        return grad_query, dot(grad_scores, queries), dot(probs.astype(BF16), grads)

    @pl.loop(0, 2)
    def _(doc):
        start = pl.multiple_of(meta[OFF0 + doc], BLOCK)
        for blocks in range(1, 7):

            @pl.when(meta[CNT0 + doc] == blocks)
            def _():
                size = blocks * BLOCK
                whole = pl.ds(start, size)
                keys, values = k_ref[whole, :], v_ref[whole, :]
                keys_split = split_turned(keys)
                valid = meta[LEN0 + doc] - (blocks - 1) * BLOCK
                steps = (blocks + 1) // 2

                def ahead_of(step):
                    return products(
                        pl.multiple_of(start + step * TILE, BLOCK), TILE, keys, values,
                        size - step * TILE if size < (step + 1) * TILE else None,
                        lambda scores: mask_keys(scores, blocks - 1, valid),
                    )

                ahead = ahead_of(0)
                for step in range(steps):
                    now = ahead
                    if step + 1 < steps:
                        ahead = ahead_of(step + 1)
                    grad_query, grad_key, grad_value = finish(*now, keys_split)
                    if step > 0:
                        grad_key += key_acc[:size, :]
                        grad_value += value_acc[:size, :]
                    if step + 1 < steps:
                        key_acc[:size, :] = grad_key
                        value_acc[:size, :] = grad_value
                    for sub in range(2):
                        at = pl.multiple_of(start + step * TILE + sub * BLOCK, BLOCK)
                        out_ref[pl.ds(at, BLOCK), 0:128] = turn_back(
                            grad_query[sub * BLOCK : (sub + 1) * BLOCK, :],
                            pl.ds((step * 2 + sub) * BLOCK, BLOCK),
                        )
                out_ref[whole, 128:256] = turn_back(grad_key, pl.ds(0, size))
                out_ref[whole, 256:384] = grad_value.astype(BF16)

    first = pl.multiple_of(meta[OFFQ], BLOCK)
    rows = pl.ds(first, BLOCK)
    keys = k_ref[rows, :]
    grad_query, grad_key, grad_value = finish(
        *products(first, BLOCK, keys, v_ref[rows, :], None, functools.partial(query_mask, meta)),
        split_turned(keys),
    )
    table = pl.ds(cos_ref.shape[0] - BLOCK, BLOCK)
    out_ref[rows, 0:128] = turn_back(grad_query, table)
    out_ref[rows, 128:256] = turn_back(grad_key, table)
    out_ref[rows, 256:384] = grad_value.astype(BF16)
    out_ref[pl.ds(first + BLOCK, BLOCK), :] = jnp.zeros((BLOCK, 384), BF16)


def attend_back(meta, pair, qkv, grad, att, lse, tables, before=(), after=()):
    rows, width = grad.shape
    pairs = width // 128

    def column(part, columns=128):
        return pl.BlockSpec((rows, columns), lambda h, *_: (0, part * pairs + pair))

    grid_spec = pltpu.PrefetchScalarGridSpec(
        num_scalar_prefetch=1,
        grid=(1,),
        in_specs=[
            column(0), column(1), column(2), column(0),
            column(0),
            pl.BlockSpec((1, 8, rows), lambda h, *_: (pair, 0, 0)),
            resident(tables[0].shape), resident(tables[1].shape),
        ]
        + anywhere(len(before) + len(after)),
        out_specs=pl.BlockSpec((rows, 384), lambda h, *_: (0, pair)),
        scratch_shapes=[pltpu.VMEM((6 * BLOCK, 128), F32)] * 2,
    )
    return pl.pallas_call(
        attend_back_kernel,
        grid_spec=grid_spec,
        out_shape=jax.ShapeDtypeStruct((rows, 3 * width), BF16),
        input_output_aliases={9: 0} if before else {},
        compiler_params=params(),
        cost_estimate=cost(11),
        name="attend_back",
    )(meta, qkv, qkv, qkv, grad, att, lse, *tables, *before, *after)


@while_live
def qkv_grad_kernel(meta, x_ref, *refs):
    keep_ref, send_ref, acc = refs[-3:]
    columns = acc.shape[1]
    pairs = columns // 384
    grad_ref, extra = refs[0], refs[1:3]
    tile = pl.program_id(0)

    @pl.when(tile == 0)
    def _():
        acc[...] = jnp.zeros_like(acc)

    grad = jnp.concatenate(
        [
            grad_ref[:, (pair * 3 + part) * 128 : (pair * 3 + part + 1) * 128]
            for part in range(3)
            for pair in range(pairs)
        ],
        axis=1,
    )
    acc[...] += dot(x_ref[...].T, grad)

    @pl.when(tile == meta[TILES] - 1)
    def _():
        out_pieces(meta, acc, keep_ref, send_ref)
        if keep_ref.shape[3] > columns:
            keep_ref[:, :, :, columns:] = extra[0][...]
            send_ref[:, :, :, columns:] = extra[1][...]


def qkv_grad(meta, x, grad, columns, at, extra=(), after=()):
    rows, width = x.shape
    block = (2, 2, width // 8, columns + sum(part.shape[3] for part in extra[:1]))
    piece = jax.ShapeDtypeStruct(block, BF16)
    grid_spec = pltpu.PrefetchScalarGridSpec(
        num_scalar_prefetch=1,
        grid=(rows // TILE,),
        in_specs=[tiled(width)]
        + [tiled(columns, at)]
        + [resident(part.shape) for part in extra]
        + anywhere(len(after)),
        out_specs=[pl.BlockSpec(block, lambda i, *_: (0, 0, 0, 0))] * 2,
        scratch_shapes=[pltpu.VMEM((width, columns), F32)],
    )
    return pl.pallas_call(
        qkv_grad_kernel,
        grid_spec=grid_spec,
        out_shape=[piece, piece],
        compiler_params=params(),
        cost_estimate=cost(9),
        name="qkv_grad",
    )(meta, x, grad, *extra, *after)


def token_grad_kernel(which, meta, *refs):
    sums, grads, weight = refs[0:2], refs[2:4], refs[4]
    step = pl.program_id(0)

    def value():
        total = jnp.concatenate([part[...] for part in sums], axis=0)
        return total + dot(jnp.concatenate([part[...] for part in grads], axis=0), weight[...])

    if which == 0:
        docs_ref = refs[-1]
        length = meta[LEN0] - step * TILE
        store = lambda value: docs_ref.__setitem__(0, value)
    else:
        docs_ref, queries_ref = refs[-2:]
        length = jnp.where(step < 3, meta[LEN1] - step * TILE, TILE)
        store = lambda value: docs_ref.__setitem__(slice(None), value.astype(BF16))

    @pl.when((step < 3) & (length > 0))
    def _():
        total = value()
        inside = lax.broadcasted_iota(jnp.int32, total.shape, 0)
        store(jnp.where(inside < length, total, 0.0))

    @pl.when((step < 3) & (length <= 0))
    def _():
        store(jnp.zeros((TILE, docs_ref.shape[-1]), F32))

    if which == 1:

        @pl.when(step == 3)
        def _():
            total = value()[:BLOCK, :]
            inside = lax.broadcasted_iota(jnp.int32, (BLOCK // 2, total.shape[1]), 0)
            for query in range(2):
                half = total[query * (BLOCK // 2) : (query + 1) * (BLOCK // 2), :]
                queries_ref[query] = jnp.where(inside < meta[QLEN0 + query], half, 0.0)


def token_grad(which, meta, sums, grad, weight, after=()):
    rows, width = sums.shape

    def block_of(step, meta, second):
        last = meta[CNT0 + which] - 1
        in_doc = jnp.minimum(jnp.minimum(step, 2) * 2 + second, last)
        return jnp.where(step < 3, meta[OFF0 + which] // BLOCK + in_doc, meta[OFFQ] // BLOCK)

    def halves(columns):
        return [
            pl.BlockSpec((BLOCK, columns), lambda i, meta, s=s: (block_of(i, meta, s), 0)) for s in range(2)
        ]

    if which == 0:
        out_specs = [pl.BlockSpec((1, TILE, width), lambda i, meta: (1 - meta[SLOT], i, 0))]
        out_shape = [jax.ShapeDtypeStruct((2, 6 * BLOCK, width), F32)]
    else:
        out_specs = [
            pl.BlockSpec((TILE, width), lambda i, meta: (jnp.minimum(i, 2), 0)),
            pl.BlockSpec((2, BLOCK // 2, width), lambda i, meta: (0, 0, 0)),
        ]
        out_shape = [
            jax.ShapeDtypeStruct((6 * BLOCK, width), BF16),
            jax.ShapeDtypeStruct((2, BLOCK // 2, width), F32),
        ]
    grid_spec = pltpu.PrefetchScalarGridSpec(
        num_scalar_prefetch=1,
        grid=(3 + which,),
        in_specs=halves(width) + halves(grad.shape[1]) + [resident(weight.shape)]
        + anywhere(len(after)),
        out_specs=out_specs,
    )
    return pl.pallas_call(
        functools.partial(token_grad_kernel, which),
        grid_spec=grid_spec,
        out_shape=out_shape,
        compiler_params=params(),
        cost_estimate=cost(9),
        name="token_grad",
    )(meta, sums, sums, grad, grad, weight, *after)


def place_moved_kernel(meta, own_ref, other_ref, *refs):
    docs_ref = refs[-1]

    @pl.when(meta[STAY] == 1)
    def _():
        docs_ref[0] = own_ref[...].astype(F32)

    @pl.when(meta[STAY] == 0)
    def _():
        docs_ref[0] = other_ref[...].astype(F32)


def place_moved(meta, docs, own, other, after=()):
    width = docs.shape[2]
    grid_spec = pltpu.PrefetchScalarGridSpec(
        num_scalar_prefetch=1,
        grid=(3,),
        in_specs=[pl.BlockSpec((TILE, width), lambda i, m: (i, 0))] * 2 + anywhere(1 + len(after)),
        out_specs=pl.BlockSpec((1, TILE, width), lambda i, m: (m[SLOT], i, 0)),
    )
    return pl.pallas_call(
        place_moved_kernel,
        grid_spec=grid_spec,
        out_shape=jax.ShapeDtypeStruct(docs.shape, F32),
        input_output_aliases={3: 0},
        compiler_params=pltpu.CompilerParams(vmem_limit_bytes=16 * 1024 * 1024),
        cost_estimate=cost(4),
        name="place_moved",
    )(meta, own, other, docs, *after)


def layout(doc_counts, query_counts, rows, core, side, row, slot, stay):
    blocks = (doc_counts + BLOCK - 1) // BLOCK
    offq = blocks[0] + blocks[1]
    tiles = (offq + 1 + 1) // 2
    meta = jnp.stack(
        [
            jnp.int32(0), blocks[0] * BLOCK, offq * BLOCK, doc_counts[0], doc_counts[1],
            query_counts[0], query_counts[1], blocks[0], blocks[1], tiles, core, side, row,
            slot, stay, jnp.int32(0),
        ]
    ).astype(jnp.int32)
    at = jnp.arange(rows // BLOCK, dtype=jnp.int32)
    in_first, in_second = at < blocks[0], (at >= blocks[0]) & (at < offq)
    table_block = jnp.where(in_first, at, jnp.where(in_second, at - blocks[0], 6))
    half = jnp.arange(rows // (BLOCK // 2), dtype=jnp.int32)
    start = half * (BLOCK // 2)
    first, second = start < blocks[0] * BLOCK, start < offq * BLOCK
    which_query = half - 2 * offq
    counts = jnp.where(
        first,
        doc_counts[0] - start,
        jnp.where(
            second,
            doc_counts[1] - (start - blocks[0] * BLOCK),
            jnp.where(which_query == 0, query_counts[0], jnp.where(which_query == 1, query_counts[1], 0)),
        ),
    )
    owner = jnp.where(first, 0, jnp.where(second, 1, jnp.clip(2 + which_query, 2, 3)))
    return meta, table_block, jnp.clip(counts, 0, BLOCK // 2).astype(jnp.int32), owner.astype(jnp.int32)


def pack_rows(first, second, queries, meta, rows):
    width = first.shape[-1]
    tail = jnp.zeros((rows - first.shape[0], width), first.dtype)
    packed = jnp.concatenate([first, tail], axis=0)
    packed = lax.dynamic_update_slice(packed, second, (meta[OFF1], 0))
    padded = jnp.concatenate(
        [queries.reshape(BLOCK, width), jnp.zeros((BLOCK, width), first.dtype)], axis=0
    )
    return lax.dynamic_update_slice(packed, padded, (meta[OFFQ], 0))


def loss_kernel(ids, message_ref, soft_ref, loss_ref, query_grad_ref, doc_grad_ref):
    rows, half = message_ref.shape[0], message_ref.shape[1] - 128
    pairs = rows // 4
    soft = soft_ref[0:1, 0:1]
    low = message_ref[:, :half]
    extra = message_ref[:, half:].astype(F32)
    row = lax.broadcasted_iota(jnp.int32, (rows, pairs), 0) % 8
    index = (extra[:, 0:1] + 0.5).astype(jnp.int32)
    found = lax.broadcasted_iota(jnp.int32, (rows, pairs), 1) == index
    of_query, of_doc = found & (row % 4 < 2), found & (row % 4 >= 2)

    def units(chosen):
        halves = [
            dot((chosen & (row // 4 == which)).astype(F32).astype(BF16), low, ((0,), (0,))) for which in range(2)
        ]
        return jnp.concatenate(halves, axis=1).astype(BF16)

    units_q, units_d = units(of_query), units(of_doc)
    exact = functools.partial(
        lax.dot_general, precision=lax.Precision.HIGHEST, preferred_element_type=F32
    )
    plain, turned, over_rows = (((1,), (0,)), ((), ())), (((1,), (1,)), ((), ())), (((0,), (0,)), ((), ()))
    extra = exact((of_query & (row < 4)).astype(F32), extra, over_rows)
    weight = extra[:, 2:3] / 16.0 + extra[:, 3:4] / 4096.0 + extra[:, 4:5] / 1048576.0
    similarity = dot(units_q, units_d, ((1,), (1,))) / soft
    columns = lax.broadcasted_iota(jnp.int32, similarity.shape, 1)
    target = (columns == (extra[:, 1:2] + 0.5).astype(jnp.int32)).astype(F32)
    highest = jnp.max(similarity, axis=1, keepdims=True)
    log_norm = highest + jnp.log(jnp.sum(jnp.exp(similarity - highest), axis=1, keepdims=True))
    picked = jnp.sum(target * similarity, axis=1, keepdims=True)
    loss = jnp.sum(weight * (log_norm - picked), axis=0, keepdims=True) / pairs
    loss_ref[...] = jnp.broadcast_to(loss, loss_ref.shape)
    grad = weight * (jnp.exp(similarity - log_norm) - target) / pairs
    line = lax.broadcasted_iota(jnp.int32, (8, pairs), 0)
    column = lax.broadcasted_iota(jnp.int32, (8, pairs), 1)
    my_queries = (column == jnp.where(line == 0, ids[0], ids[1])) & (line < 2)
    my_docs = (column == jnp.where(line == 0, ids[2], ids[3])) & (line < 2)
    query_rows = exact(my_queries.astype(F32), grad, plain)
    doc_rows = exact(my_docs.astype(F32), grad, turned)
    query_grad_ref[...] = exact(query_rows, units_d.astype(F32), plain) / soft
    doc_grad_ref[...] = exact(doc_rows, units_q.astype(F32), plain) / soft


def loss_and_grads(ids, messages, soft, width):
    vmem = pl.BlockSpec(memory_space=pltpu.VMEM)
    return pl.pallas_call(
        loss_kernel,
        in_specs=[pl.BlockSpec(memory_space=pltpu.SMEM), vmem, vmem],
        out_specs=[vmem, vmem, vmem],
        out_shape=[
            jax.ShapeDtypeStruct((8, 128), F32),
            jax.ShapeDtypeStruct((8, width), F32),
            jax.ShapeDtypeStruct((8, width), F32),
        ],
        compiler_params=params(),
        name="loss",
    )(ids, messages, jnp.broadcast_to(soft.reshape(1, 1), (8, 128)))


def wide_unfold_kernel(piece, *refs):
    gate_ref, up_ref, down_ref = refs[-3:]
    gate_ref[...] = piece[0, 0].astype(F32)
    up_ref[...] = piece[0, 1].astype(F32)
    span = piece.shape[3] // 2
    block = jnp.concatenate([piece[0, 2, :, :span], piece[0, 2, :, span:]], axis=0)
    down_ref[...] = block.astype(F32).T


def wide_unfold(chunk, pieces, before, width, inner, after=()):
    quarter, span = pieces.shape[2:]
    chunks = inner // (2 * span)
    place = pl.BlockSpec((quarter, span), lambda i: (i // 2, (i % 2) * chunks + chunk))
    return pl.pallas_call(
        wide_unfold_kernel,
        grid=(4,),
        in_specs=[pl.BlockSpec((1, *pieces.shape[1:]), lambda i: (i, 0, 0, 0))]
        + anywhere(len(before) + len(after)),
        out_specs=[
            place, place,
            pl.BlockSpec((span // 2, 2 * quarter), lambda i: (2 * chunk + i % 2, i // 2)),
        ],
        out_shape=[
            jax.ShapeDtypeStruct((width // 2, inner), F32),
            jax.ShapeDtypeStruct((width // 2, inner), F32),
            jax.ShapeDtypeStruct((inner // 2, width), F32),
        ],
        input_output_aliases={1 + at: at for at in range(len(before))},
        compiler_params=pltpu.CompilerParams(vmem_limit_bytes=16 * 1024 * 1024),
        cost_estimate=cost(3),
        name="wide_unfold",
    )(pieces, *before, *after)


def wide_unfold_parts_kernel(meta, p00, p01, p10, p11, *refs):
    gate_ref, up_ref, down_ref = refs[-3:]
    for other_core in range(2):
        for other_row in range(2):
            piece = ((p00, p01), (p10, p11))[other_core][other_row]

            @pl.when((pl.program_id(0) == other_core) & (pl.program_id(1) == other_row))
            def _():
                gate_ref[...] = piece[0].astype(F32)
                up_ref[...] = piece[1].astype(F32)
                span = piece.shape[2] // 2
                block = jnp.concatenate([piece[2, :, :span], piece[2, :, span:]], axis=0)
                down_ref[...] = block.astype(F32).T


def wide_unfold_parts(meta, chunk, pieces, before, width, inner, after=()):
    quarter, span = pieces[0].shape[1:]
    chunks = inner // (2 * span)
    aliased = [pl.BlockSpec(memory_space=pl.ANY)] * len(before)
    grid_spec = pltpu.PrefetchScalarGridSpec(
        num_scalar_prefetch=1,
        grid=(2, 2),
        in_specs=[resident(p.shape) for p in pieces] + aliased + anywhere(len(after)),
        out_specs=[
            pl.BlockSpec(
                (quarter, span), lambda c, r, m: (m[ROW] ^ r, (m[CORE] ^ c) * chunks + chunk)
            )
            for _ in range(2)
        ]
        + [
            pl.BlockSpec(
                (span // 2, 2 * quarter), lambda c, r, m: (2 * chunk + (m[CORE] ^ c), m[ROW] ^ r)
            )
        ],
    )
    return pl.pallas_call(
        wide_unfold_parts_kernel,
        grid_spec=grid_spec,
        out_shape=[
            jax.ShapeDtypeStruct((width // 2, inner), F32),
            jax.ShapeDtypeStruct((width // 2, inner), F32),
            jax.ShapeDtypeStruct((inner // 2, width), F32),
        ],
        input_output_aliases={5 + at: at for at in range(len(before))},
        compiler_params=pltpu.CompilerParams(vmem_limit_bytes=16 * 1024 * 1024),
        cost_estimate=cost(3),
        name="wide_unfold_parts",
    )(meta, *pieces, *before, *after)


AXES = ("fsdp", "blk")


class Links:
    def __init__(self, sides, blk):
        self.sides, self.blk, self.outer = sides, blk, blk // 4

    def swap(self, value, side=0, mask=0):
        pairs = [
            (f * self.blk + b, (f ^ side) * self.blk + (b ^ mask))
            for f in range(self.sides)
            for b in range(self.blk)
        ]
        return lax.ppermute(value, AXES, pairs)

    def core(self, value):
        return self.swap(value, mask=1)

    def row(self, value):
        return self.swap(value, mask=2)

    def side(self, value):
        return self.swap(value, side=1)

    def shift(self, value, by):
        pairs = [
            (f * self.blk + b, f * self.blk + (b + 4 * by) % self.blk)
            for f in range(self.sides)
            for b in range(self.blk)
        ]
        return lax.ppermute(value, AXES, pairs)

    def step(self, value, moves):
        pairs = [
            (f * self.blk + 4 * start + b, f * self.blk + 4 * end + b)
            for f in range(self.sides)
            for start, end in moves
            for b in range(4)
        ]
        return lax.ppermute(value, AXES, pairs)

    def outer_masks(self):
        mask = 4
        while mask < self.blk:
            yield mask
            mask *= 2

    def gather(self, value):
        both = jnp.concatenate([value, self.core(value)], axis=0)
        plane = jnp.concatenate(
            [both, self.swap(both, 1, 0), self.swap(both, 0, 2), self.swap(both, 1, 2)], axis=0
        )
        return jnp.concatenate(
            [plane] + [self.shift(plane, by) for by in range(1, self.outer)], axis=0
        )

    def stages(self, keep, send, row_first, by_swaps=False):
        add = lambda *terms: sum(term.astype(F32) for term in terms).astype(BF16)
        now = yield
        now = yield (send := tie(send, now))
        received = tie(self.core(send), now)
        if row_first:
            now = yield (away := add(keep[:, 1], received[:, 1]))
            across = tie(self.row(away), now)
            now = yield (away := add(keep[1, 0], received[1, 0], across[1]))
            last = self.side(away)
        else:
            now = yield (away := add(keep[1], received[1]))
            across = tie(self.side(away), now)
            now = yield (away := add(keep[0, 1], received[0, 1], across[1]))
            last = self.row(away)
        mine = add(keep[0, 0], received[0, 0], across[0], tie(last, now))
        if self.outer == 4:
            outer = lax.axis_index("blk") // 4
            now = yield mine
            mine = add(mine, tie(self.step(mine, ((0, 1), (3, 2))), now))
            now = yield mine
            mine = add(mine, tie(self.step(mine, ((1, 2), (2, 1))), now))
            now = yield mine
            result = tie(self.step(mine, ((1, 0), (2, 3))), now)
            mine = jnp.where((outer == 1) | (outer == 2), mine, result)
        else:
            for mask in self.outer_masks():
                now = yield mine
                mine = add(mine, tie(self.swap(mine, mask=mask), now))
        if by_swaps:
            now = yield mine
            other = tie(self.row(mine), now)
            yield other
            return mine, other, self.core(mine), self.core(other)
        groups = [[at + part for part in range(4)] for at in range(0, self.blk, 4)]
        flat = mine.reshape(-1, mine.shape[-1])
        gathered = lax.all_gather(flat, "blk", axis_index_groups=groups, axis=0, tiled=True)
        yield mine
        return gathered

    def stages_small(self, value):
        now = yield
        for side, mask in [(0, 1), (1, 0), (0, 2)] + [(0, mask) for mask in self.outer_masks()]:
            value = tie(value, now)
            now = yield value
            value = value + self.swap(value, side, mask)
        return value


def tie(value, now):
    return lax.optimization_barrier((value, now))[0]


class Flow:
    def __init__(self):
        self.sums, self.done = {}, {}

    def begin(self, name, stages):
        next(stages)
        self.sums[name] = stages

    def forward(self, now, *names):
        sent = []
        for name in names:
            if name in self.done:
                continue
            try:
                sent.append(self.sums[name].send(now))
            except StopIteration as end:
                self.done[name] = end.value
                if name == "s":
                    sent.append(end.value)
        return tuple(sent)

    def result(self, now, name):
        while name not in self.done:
            self.forward(now, name)
        return self.done[name]


def part_of(share, parts, at):
    size = share.shape[0] // parts
    return lax.dynamic_slice_in_dim(share, at * size, size, 0)


def body(
    question_activations,
    passage_activations,
    question_unpadded_counts,
    passage_unpadded_counts,
    correct_passage_index,
    query_weights,
    softness_factor,
    combined_projection_matrix,
    mixing_result_matrix,
    gating_matrix,
    widening_matrix,
    narrowing_matrix,
    initial_layernorm_scale,
    initial_layernorm_shift,
    later_layernorm_scale,
    later_layernorm_shift,
):
    doc_len, width = passage_activations.shape[1:]
    query_len = question_activations.shape[1]
    inner = gating_matrix.shape[1]
    assert passage_activations.shape[0] == 2 and doc_len == 6 * BLOCK and 2 * query_len == BLOCK
    links = Links(lax.axis_size("fsdp"), lax.axis_size("blk"))
    side, blk = lax.axis_index("fsdp"), lax.axis_index("blk")
    core, row = blk % 2, (blk // 2) % 2

    got_qkv = links.side(part_of(combined_projection_matrix, 2, core))
    quarter = row * 2 + core
    part_out = tie(part_of(mixing_result_matrix, 2, core), got_qkv)
    part_gate = tie(part_of(gating_matrix, 4, quarter), got_qkv)
    got_out, got_gate = links.side(part_out), links.side(part_gate)
    vectors = jnp.stack(
        [initial_layernorm_scale, initial_layernorm_shift, later_layernorm_scale, later_layernorm_shift]
    )
    others = links.side(vectors)
    vectors = jnp.concatenate(
        [jnp.where(side == 0, vectors, others), jnp.where(side == 0, others, vectors)], axis=1
    ).astype(F32)
    gain_one, bias_one, gain_two, bias_two = (vectors[at : at + 1] for at in range(4))

    per_chip = passage_unpadded_counts.astype(jnp.int32)
    across = links.core(per_chip)
    four = jnp.where(core == 0, jnp.concatenate([per_chip, across]), jnp.concatenate([across, per_chip]))
    blocks = (four + BLOCK - 1) // BLOCK
    work = blocks * (10 + blocks)
    total = jnp.sum(work)
    loads = jnp.stack([work[0] + work[at] for at in (1, 2, 3)])
    plan = jnp.argmin(jnp.maximum(loads, total - loads)).astype(jnp.int32)
    stay = (plan == 0).astype(jnp.int32)
    slot_of = lambda which: jnp.where(which == 0, 1, jnp.where(plan == 1, 0, 1))
    slot = slot_of(core)
    sent_doc = lax.dynamic_index_in_dim(passage_activations, slot, 0, keepdims=False)
    first_doc = lax.dynamic_index_in_dim(passage_activations, 1 - slot, 0, keepdims=False)
    second_doc = jnp.where(stay == 1, sent_doc, links.core(sent_doc))
    own_counts = per_chip[1 - slot], jnp.where(stay == 1, per_chip[slot], across[slot_of(1 - core)])
    doc_counts, query_counts = jnp.stack(own_counts), question_unpadded_counts
    device = side * links.blk + blk
    ids = jnp.stack(
        [
            2 * device, 2 * device + 1, 2 * device + 1 - slot,
            jnp.where(stay == 1, 2 * device + slot, 2 * (device ^ 1) + slot_of(1 - core)),
        ]
    ).astype(jnp.int32)

    rows = -(-(2 * doc_len + BLOCK) // TILE) * TILE
    meta, table_block, counts, owner = layout(doc_counts, query_counts, rows, core, side, row, slot, stay)
    tables = tuple(jnp.asarray(table) for table in rotary_tables(doc_len, query_len))
    x = pack_rows(first_doc, second_doc, question_activations, meta, rows)

    got_qkv = tie(got_qkv, (x, meta, table_block, counts, owner, gain_one, bias_one, gain_two, bias_two))
    pieces_qkv = (combined_projection_matrix, got_qkv, links.core(got_qkv))
    qkv, wqkv = project(meta, table_block, x, pieces_qkv, tables, (part_out, part_gate))
    got_out, got_gate = tie((got_out, got_gate), qkv)
    part_up = tie(part_of(widening_matrix, 4, quarter), qkv)
    far_out, along_gate, got_up = links.core(got_out), links.row(got_gate), links.side(part_up)
    heads = attend(meta, qkv, 0, 2, (), (got_out, got_gate, part_up))
    along_gate, got_up = tie((along_gate, got_up), heads[1])
    part_down = tie(part_of(narrowing_matrix, 4, quarter), heads[1])
    far_gate = links.core(got_gate), links.core(along_gate)
    along_up, got_down = links.row(got_up), links.side(part_down)
    heads = attend(meta, qkv, 1, 2, heads, (far_out, along_gate, got_up, part_down))
    along_up, got_down = tie((along_up, got_down), heads[1])
    far_up = links.core(got_up), links.core(along_up)
    along_down = links.row(got_down)
    att, lse = attend(meta, qkv, 2, 2, heads, (*far_gate, along_up, got_down))
    along_down = tie(along_down, lse)
    far_down = links.core(got_down), links.core(along_down)
    weights = [
        (mixing_result_matrix, got_out, far_out),
        (gating_matrix, got_gate, along_gate, *far_gate),
        (widening_matrix, got_up, along_up, *far_up),
        (narrowing_matrix, got_down, along_down, *far_down),
    ]
    low, z1, r1, saved, z2, r2, sums, wo, wg, wu, wd = forward(
        meta, counts, att, x, weights, gain_one, bias_one
    )

    groups = rows // (BLOCK // 2)
    used = (jnp.arange(groups) // (2 * TILE // BLOCK))[None, :] < meta[TILES]
    chosen = (owner[None, :] == jnp.arange(4)[:, None]) & used
    z_sums = jnp.sum(jnp.where(chosen[:, :, None], sums.reshape(1, groups, width), 0.0), axis=1)
    lengths = jnp.concatenate([doc_counts, query_counts]).astype(F32)[:, None]
    pooled = z_sums / lengths * gain_two + bias_two
    recip = lax.rsqrt(jnp.sum(pooled * pooled, axis=1, keepdims=True) + EPS_UNIT)
    unit = (pooled * recip).astype(BF16).astype(F32)
    high = jnp.floor(query_weights * 16.0)
    rest = (query_weights * 16.0 - high) * 256.0
    middle = jnp.floor(rest)
    lowest = jnp.floor((rest - middle) * 256.0)
    extra = jnp.stack(
        [ids.astype(BF16)]
        + [jnp.pad(part.astype(BF16), (0, 2)) for part in (correct_passage_index, high, middle, lowest)],
        axis=1,
    )
    extra = jnp.pad(extra, ((0, 0), (0, 123)))
    unit = jnp.concatenate([unit[2:], unit[:2]], axis=0).astype(BF16)
    message = jnp.concatenate(
        [
            jnp.concatenate([unit[:, : width // 2], extra], axis=1),
            jnp.concatenate([unit[:, width // 2 :], extra], axis=1),
        ],
        axis=0,
    )
    messages = links.gather(message)
    loss, grad_q, grad_d = loss_and_grads(ids, messages, softness_factor, width)
    grad_unit = jnp.concatenate([grad_d[:2], grad_q[:2]], axis=0)
    crossed = jnp.sum(grad_unit * pooled, axis=1, keepdims=True)
    grad_rows = (recip * grad_unit - pooled * recip**3 * crossed) / lengths
    grad_gain_two = jnp.sum(grad_rows * z_sums, axis=0)
    grad_bias_two = jnp.sum(grad_rows * lengths, axis=0)

    scaled = jnp.pad(grad_rows * gain_two, ((0, 4), (0, 0)))
    flow = Flow()

    def wide(chunk, given, after):
        out, keep, send = ffn_back(
            meta, counts, owner, chunk, low, saved, wd, wg, wu, given, after
        )
        flow.begin("w%d" % chunk, links.stages(keep, send, chunk == 2, chunk == 2))
        return out, keep

    def score(pair, before, after):
        return attend_back(meta, pair, qkv, grad_att, att, lse, tables, before, after)

    def narrow(group, columns, at, extra, after):
        keep, send = qkv_grad(meta, x, grads, columns, at, extra, after)
        flow.begin("q%d" % group, links.stages(keep, send, group == 0))
        return keep

    head, now = wide(0, (z2, r2, scaled), ())
    tail, now = wide(1, (head,), flow.forward(now, "w0"))
    tail, now = wide(2, (head, tail), flow.forward(now, "w0", "w1"))
    later = jnp.pad(jnp.stack([grad_gain_two, grad_bias_two]), ((2, 4), (0, 0)))
    sum_one, grad_att, now, *mixing = norm_one_back(
        meta, (head, tail), z1, r1, att, gain_one, wo, later, flow.forward(now, "w0", "w1", "w2")
    )
    flow.begin("s", links.stages_small(now))
    grads = score(0, (), flow.forward(now, "w0", "w2"))
    grads = score(1, (grads,), flow.forward(grads, "w0"))
    grads = score(2, (grads,), flow.forward(grads, "w0", "w1"))
    grads = score(3, (grads,), flow.forward(grads, "w0", "w2"))
    now = narrow(0, 1536, 0, mixing, flow.forward(grads, "w1"))
    grads = score(4, (grads,), flow.forward(now, "w1", "w2", "q0"))
    now = grads = score(5, (grads,), flow.forward(grads, "w0", "w1", "w2", "q0"))
    unfold = lambda chunk, before, after: wide_unfold(
        chunk, flow.result(now, "w%d" % chunk).reshape(4, 3, width // 4, -1), before, width, inner, after
    )
    grad_wide = unfold(0, (), ())
    now = narrow(1, 768, 2, (), (*flow.forward(now, "w1", "w2"), grad_wide[0]))
    (grad_docs,) = token_grad(
        0, meta, sum_one, grads, wqkv, flow.forward(now, "w2", "q0", "q1", "s")
    )
    moved, grad_queries = token_grad(
        1, meta, sum_one, grads, wqkv, (grad_docs, *flow.forward(grad_docs, "q0", "q1", "s"))
    )
    other_moved = links.core(moved)
    grad_wide = unfold(1, grad_wide, flow.forward(moved, "w1", "w2", "q0", "q1", "s"))
    now = grad_wide[0]
    grad_docs = place_moved(
        meta, grad_docs, moved, other_moved, (now, *flow.forward(now, "w2", "q0", "q1", "s"))
    )
    after = flow.forward(grad_docs, "q0", "q1", "s")
    grad_wide = wide_unfold_parts(
        meta, 2, flow.result(grad_docs, "w2"), grad_wide, width, inner, (grad_docs, *after)
    )
    while len(flow.done) < 6:
        flow.forward(moved, "q0", "q1", "s")
    first_part, second_part = flow.done["q0"], flow.done["q1"]
    joint = first_part.shape[1] - width
    grad_qkv = jnp.concatenate(
        [
            part.astype(F32)
            for parts in zip(jnp.split(first_part[:, :joint], 3, axis=1), jnp.split(second_part, 3, axis=1))
            for part in parts
        ],
        axis=1,
    )
    grad_out = first_part[:, joint:].astype(F32)
    small = lax.dynamic_slice_in_dim(flow.done["s"], side * (width // 2), width // 2, 1)
    return (
        loss[0, :1],
        grad_queries,
        grad_docs,
        grad_qkv,
        grad_out,
        grad_wide[0],
        grad_wide[1],
        grad_wide[2],
        small[0],
        small[1],
        small[2],
        small[3],
    )


def solution(mesh):
    placed = (
        P(("fsdp", "blk"), None, None),
        P(("fsdp", "blk"), None, None),
        P(("fsdp", "blk")),
        P(("fsdp", "blk")),
        P(("fsdp", "blk")),
        P(("fsdp", "blk")),
        P(),
        P("fsdp", None),
        P("fsdp", None),
        P("fsdp", None),
        P("fsdp", None),
        P("fsdp", None),
        P("fsdp"),
        P("fsdp"),
        P("fsdp"),
        P("fsdp"),
    )
    return jax.shard_map(
        body,
        mesh=mesh,
        in_specs=placed,
        out_specs=(
            P(),
            P(("fsdp", "blk"), None, None),
            P(("fsdp", "blk"), None, None),
            P("fsdp", None),
            P("fsdp", None),
            P("fsdp", None),
            P("fsdp", None),
            P("fsdp", None),
            P("fsdp"),
            P("fsdp"),
            P("fsdp"),
            P("fsdp"),
        ),
        check_vma=False,
    )
```

```python
import functools

import jax
import jax.numpy as jnp
import numpy as np
from jax import lax
from jax.experimental import pallas as pl
from jax.experimental.pallas import tpu as pltpu
from jax.sharding import PartitionSpec as P

HEAD = 64
BLOCK = 128
TILE = 256
EPS_NORM = 1e-05
EPS_UNIT = 1e-06
MASKED = -1e30
F32 = jnp.float32
BF16 = jnp.bfloat16
PACE = 0.5
SPAN = 512
OFF0, OFF1, OFFQ, LEN0, LEN1, QLEN0, QLEN1, CNT0, CNT1, TILES, CORE, SIDE, ROW, SLOT, STAY, IDS = range(16)


def dot(left, right, contract=((1,), (0,))):
    return lax.dot_general(left, right, (contract, ((), ())), preferred_element_type=F32)


def cost(microseconds):
    return pl.CostEstimate(flops=int(microseconds * PACE * 1e9), bytes_accessed=0, transcendentals=0)


def params(mebibytes=60):
    return pltpu.CompilerParams(vmem_limit_bytes=mebibytes * 1024 * 1024)


def rotary_tables(doc_len, query_len):
    frequency = 1000.0 ** (-(np.arange(HEAD // 2, dtype=np.float32) * 2.0 / HEAD))
    positions = np.concatenate([np.arange(doc_len), np.arange(query_len), np.arange(query_len)])
    angles = positions.astype(np.float32)[:, None] * frequency.astype(np.float32)[None, :]
    cosine, sine = np.cos(angles), np.sin(angles)
    return (
        np.concatenate([cosine] * 4, axis=1).astype(np.float32),
        np.concatenate([-sine, sine, -sine, sine], axis=1).astype(np.float32),
    )


def swap_halves(pair):
    lane = lax.broadcasted_iota(jnp.int32, pair.shape, 1)
    return jnp.where(lane % HEAD < HEAD // 2, pltpu.roll(pair, 96, 1), pltpu.roll(pair, 32, 1))


def live(step, meta):
    return jnp.minimum(step, meta[TILES] - 1)


def tiled(columns, at=0):
    return pl.BlockSpec((TILE, columns), lambda i, m, *_: (live(i, m), at))


def while_live(kernel):
    @functools.wraps(kernel)
    def run(meta, *refs):
        @pl.when(pl.program_id(0) < meta[TILES])
        def _():
            kernel(meta, *refs)

    return run


def anywhere(count):
    return [pl.BlockSpec(memory_space=pl.ANY)] * count


def resident(shape):
    return pl.BlockSpec(shape, lambda *_: (0,) * len(shape), pipeline_mode=pl.Buffered(1))


def piece_copies(meta, rows, pieces, whole, sems):
    side, row, core = meta[SIDE], meta[ROW], meta[CORE]
    parts = len(pieces) - 1
    if parts == 2:
        places = [core, 1 - core]
    else:
        places = [row * 2 + core, (1 - row) * 2 + core, row * 2 + 1 - core, (1 - row) * 2 + 1 - core]
    size = rows // parts
    starts = [side * rows] + [(1 - side) * rows + place * size for place in places]
    return [
        pltpu.make_async_copy(
            piece, whole.at[pl.ds(pl.multiple_of(start, 16), piece.shape[0]), :], sems.at[at]
        )
        for at, (piece, start) in enumerate(zip(pieces, starts))
    ]


def qkv_kernel(meta, table_block, x_ref, cos_ref, sin_ref, *refs):
    pieces, (out_ref, turned_out, w_ref, turned, sems, out_sem) = refs[:3], refs[-6:]
    tile = pl.program_id(0)
    keep = pltpu.make_async_copy(turned, turned_out, out_sem)

    @pl.when(tile == 0)
    def _():
        copies = piece_copies(meta, pieces[0].shape[0], pieces, w_ref, sems)
        for copy in copies:
            copy.start()
        for copy in copies:
            copy.wait()

    @pl.when(tile == 1)
    def _():
        width = x_ref.shape[1]
        for pair in range(width // 128):
            for part in range(3):
                at, to = part * width + pair * 128, (pair * 3 + part) * 128
                turned[to : to + 128, :] = w_ref[:, at : at + 128].T
        keep.start()

    @pl.when(tile < meta[TILES])
    def _():
        x = x_ref[...]
        width = x.shape[1]

        def turn(part, acc):
            scale = HEAD**-0.5 if part == 0 else 1.0
            for sub in range(TILE // BLOCK):
                rows = slice(sub * BLOCK, (sub + 1) * BLOCK)
                table = pl.ds(table_block[tile * (TILE // BLOCK) + sub] * BLOCK, BLOCK)
                cosine, sine = cos_ref[table, :] * scale, sin_ref[table, :] * scale
                for group in range(width // 128):
                    pair = acc[rows, group * 128 : (group + 1) * 128]
                    turned_pair = pair * cosine + swap_halves(pair) * sine
                    at = part * width + group * 128
                    out_ref[rows, at : at + 128] = turned_pair.astype(BF16)

        queries = dot(x, w_ref[:, :width])
        keys = dot(x, w_ref[:, width : 2 * width])
        turn(0, queries)
        values = dot(x, w_ref[:, 2 * width :])
        turn(1, keys)
        out_ref[:, 2 * width :] = values.astype(BF16)

    @pl.when(tile == pl.num_programs(0) - 1)
    def _():
        keep.wait()


def project(meta, table_block, x, pieces, tables, after=()):
    rows, width = x.shape
    whole = (width, 3 * width)
    grid_spec = pltpu.PrefetchScalarGridSpec(
        num_scalar_prefetch=2,
        grid=(rows // TILE,),
        in_specs=[tiled(width), resident(tables[0].shape), resident(tables[1].shape)]
        + anywhere(len(pieces) + len(after)),
        out_specs=[tiled(3 * width)] + anywhere(1),
        scratch_shapes=[
            pltpu.VMEM(whole, BF16),
            pltpu.VMEM(whole[::-1], BF16),
            pltpu.SemaphoreType.DMA((len(pieces),)),
            pltpu.SemaphoreType.DMA,
        ],
    )
    return pl.pallas_call(
        qkv_kernel,
        grid_spec=grid_spec,
        out_shape=[
            jax.ShapeDtypeStruct((rows, 3 * width), BF16),
            jax.ShapeDtypeStruct(whole[::-1], BF16),
        ],
        compiler_params=params(36),
        cost_estimate=cost(11),
        name="qkv",
    )(meta, table_block, x, *tables, *pieces, *after)


def split_pair(pair):
    lane = lax.broadcasted_iota(jnp.int32, pair.shape, 1)
    zero = jnp.zeros_like(pair)
    return jnp.concatenate(
        [jnp.where(lane < HEAD, pair, zero), jnp.where(lane < HEAD, zero, pair)], axis=0
    )


def mask_keys(scores, last, valid):
    rows = lax.broadcasted_iota(jnp.int32, (BLOCK, scores.shape[1]), 0)
    tail = jnp.where(rows < valid, scores[last * BLOCK :, :], MASKED)
    if last == 0:
        return tail
    return jnp.concatenate([scores[: last * BLOCK, :], tail], axis=0)


def query_mask(meta, scores):
    half = scores.shape[0] // 2
    key = lax.broadcasted_iota(jnp.int32, scores.shape, 0)
    row = lax.broadcasted_iota(jnp.int32, scores.shape, 1) % (2 * half)
    length = jnp.where(key < half, meta[QLEN0], meta[QLEN1])
    keep = ((key < half) == (row < half)) & (key % half < length)
    return jnp.where(keep, scores, MASKED)


def split_turned(pair):
    turned = pair.T
    row = lax.broadcasted_iota(jnp.int32, turned.shape, 0)
    zero = jnp.zeros_like(turned)
    return jnp.concatenate(
        [jnp.where(row < HEAD, turned, zero), jnp.where(row < HEAD, zero, turned)], axis=1
    )


def stack_heads(pair_wide):
    half = pair_wide.shape[1] // 2
    return jnp.concatenate([pair_wide[:, :half], pair_wide[:, half:]], axis=0)


def attend_kernel(meta, q_ref, k_ref, v_ref, *refs):
    out_ref, lse_ref = refs[-2:]

    def scores_of(start, size, keys, masked):
        return masked(dot(keys, split_pair(q_ref[pl.ds(start, size), :]), ((1,), (1,))))

    def finish(start, size, scores, values):
        rows = pl.ds(start, size)
        highest = jnp.max(scores, axis=0, keepdims=True)
        exponent = jnp.exp(scores - highest)
        total = jnp.sum(exponent, axis=0, keepdims=True)
        attended = dot(values, stack_heads(exponent.astype(BF16)))
        recip = 1.0 / total
        row = lax.broadcasted_iota(jnp.int32, attended.shape, 0)
        attended = attended * jnp.where(row < HEAD, recip[:, :size], recip[:, size:])
        out_ref[rows, :] = attended.T.astype(BF16)
        log_norm = highest + jnp.log(total)
        lse_ref[0, 0:1, rows] = log_norm[:, :size]
        lse_ref[0, 1:2, rows] = log_norm[:, size:]

    def run(starts, size, keys, values, masked):
        ahead = scores_of(starts[0], size, keys, masked)
        for at, start in enumerate(starts):
            scores = ahead
            if at + 1 < len(starts):
                ahead = scores_of(starts[at + 1], size, keys, masked)
            finish(start, size, scores, values)

    @pl.loop(0, 2)
    def _(doc):
        start = pl.multiple_of(meta[OFF0 + doc], BLOCK)
        for blocks in range(1, 7):

            @pl.when(meta[CNT0 + doc] == blocks)
            def _():
                whole = pl.ds(start, blocks * BLOCK)
                valid = meta[LEN0 + doc] - (blocks - 1) * BLOCK
                starts = [pl.multiple_of(start + at * TILE, BLOCK) for at in range((blocks + 1) // 2)]
                run(
                    starts, TILE, k_ref[whole, :], split_turned(v_ref[whole, :]),
                    lambda scores: mask_keys(scores, blocks - 1, valid),
                )

    first = pl.multiple_of(meta[OFFQ], BLOCK)
    rows = pl.ds(first, BLOCK)
    run(
        [first], BLOCK, k_ref[rows, :], split_turned(v_ref[rows, :]), functools.partial(query_mask, meta)
    )
    out_ref[pl.ds(first + BLOCK, BLOCK), :] = jnp.zeros((BLOCK, 128), BF16)


def attend(meta, qkv, group, members, before=(), after=()):
    rows, width = qkv.shape[0], qkv.shape[1] // 3
    pairs = width // 128

    def column(part):
        return pl.BlockSpec((rows, 128), lambda h, *_: (0, part * pairs + group * members + h))

    grid_spec = pltpu.PrefetchScalarGridSpec(
        num_scalar_prefetch=1,
        grid=(members,),
        in_specs=[column(0), column(1), column(2)] + anywhere(len(before) + len(after)),
        out_specs=[
            column(0),
            pl.BlockSpec((1, 8, rows), lambda h, *_: (group * members + h, 0, 0)),
        ],
    )
    return pl.pallas_call(
        attend_kernel,
        grid_spec=grid_spec,
        out_shape=[
            jax.ShapeDtypeStruct((rows, width), BF16),
            jax.ShapeDtypeStruct((pairs, 8, rows), F32),
        ],
        input_output_aliases={4 + at: at for at in range(len(before))},
        compiler_params=params(28),
        cost_estimate=cost(13),
        name="attend",
    )(meta, qkv, qkv, qkv, *before, *after)


def normalize(summed):
    centered = summed - jnp.mean(summed, axis=-1, keepdims=True)
    recip = lax.rsqrt(jnp.mean(centered * centered, axis=-1, keepdims=True) + EPS_NORM)
    return centered * recip, recip


def forward_kernel(
    meta, counts, att_ref, x_ref, gain_ref, bias_ref, *refs,
):
    outs, scratch = refs[-18:-7], refs[-7:]
    pieces = [refs[0:3], refs[3:8], refs[8:13], refs[13:18]]
    low_ref, z1_ref, r1_ref, saved_ref, z2_ref, r2_ref, sums_ref = outs[:7]
    whole_outs = outs[7:]
    wholes, (sems, out_sems) = scratch[:4], scratch[5:]
    wo_ref, wg_ref, wu_ref, wd_ref = wholes
    tile = pl.program_id(0)
    copies = [
        piece_copies(meta, pieces[at][0].shape[0], pieces[at], wholes[at], sems.at[at])
        for at in range(4)
    ]
    keeps = [
        pltpu.make_async_copy(wholes[at], whole_outs[at], out_sems.at[at]) for at in range(4)
    ]

    @pl.when(tile == 0)
    def _():
        for group in copies:
            for copy in group:
                copy.start()

    def ready(which):
        @pl.when(tile == 0)
        def _():
            for at in which:
                for copy in copies[at]:
                    copy.wait()
                keeps[at].start()

    ready((0,))

    @pl.when(tile < meta[TILES])
    def _():
        z1, r1 = normalize(x_ref[...].astype(F32) + dot(att_ref[...], wo_ref[...]))
        z1_ref[...] = z1.astype(BF16)
        r1_ref[...] = r1
        normed = z1 * gain_ref[...] + bias_ref[...]
        low_ref[...] = normed.astype(BF16)
        scratch[4][...] = normed

    ready((1, 2, 3))

    @pl.when(tile < meta[TILES])
    def _():
        low = low_ref[...]
        total = scratch[4][...]
        inner, chunk = wg_ref.shape[1], SPAN
        chunks = inner // (2 * chunk)

        def products(at):
            columns = slice(at, at + chunk)
            return dot(low, wg_ref[:, columns]), dot(low, wu_ref[:, columns])

        ahead = products(0)
        for at in range(0, inner, chunk):
            columns = slice(at, at + chunk)
            gate, up = ahead
            if at + chunk < inner:
                ahead = products(at + chunk)
            sigmoid = 0.5 * jnp.tanh(0.5 * gate) + 0.5
            silu = gate * sigmoid
            hidden = (silu * up).astype(BF16)
            slope = (up * (sigmoid + silu * (1.0 - sigmoid))).astype(BF16)
            which = at // chunk
            for kind, value in enumerate((hidden, silu.astype(BF16), slope)):
                to = ((which % chunks) * 6 + kind * 2 + which // chunks) * chunk
                saved_ref[:, to : to + chunk] = value
            total = total + dot(hidden, wd_ref[columns, :])
        z2, r2 = normalize(total)
        z2_ref[...] = z2.astype(BF16)
        r2_ref[...] = r2
        half = BLOCK // 2
        inside = lax.broadcasted_iota(jnp.int32, (half, z2.shape[1]), 0)
        for group in range(TILE // half):
            valid = counts[tile * (TILE // half) + group]
            kept = jnp.where(inside < valid, z2[group * half : (group + 1) * half, :], 0.0)
            sums_ref[group : group + 1, :] = jnp.sum(kept, axis=0, keepdims=True)
        sums_ref[TILE // half :, :] = jnp.zeros((8 - TILE // half, z2.shape[1]), F32)

    @pl.when(tile == pl.num_programs(0) - 1)
    def _():
        for keep in keeps:
            keep.wait()


def forward(meta, counts, att, x, pieces, gain, bias, after=()):
    rows, width = x.shape
    inner = pieces[1][0].shape[1]
    wholes = [(width, width), (width, inner), (width, inner), (inner, width)]

    def array(columns, kind):
        return jax.ShapeDtypeStruct((rows, columns), kind)

    grid_spec = pltpu.PrefetchScalarGridSpec(
        num_scalar_prefetch=2,
        grid=(rows // TILE,),
        in_specs=[tiled(width), tiled(width)]
        + [resident(gain.shape), resident(bias.shape)]
        + anywhere(18 + len(after)),
        out_specs=[
            tiled(width), tiled(width), tiled(1), tiled(3 * inner), tiled(width), tiled(1),
            pl.BlockSpec((8, width), lambda i, m, *_: (live(i, m), 0)),
        ]
        + anywhere(4),
        scratch_shapes=[pltpu.VMEM(shape, BF16) for shape in wholes]
        + [
            pltpu.VMEM((TILE, width), F32),
            pltpu.SemaphoreType.DMA((4, 5)),
            pltpu.SemaphoreType.DMA((4,)),
        ],
    )
    return pl.pallas_call(
        forward_kernel,
        grid_spec=grid_spec,
        out_shape=[
            array(width, BF16), array(width, BF16), array(1, F32), array(3 * inner, BF16),
            array(width, BF16), array(1, F32),
            jax.ShapeDtypeStruct((rows // TILE * 8, width), F32),
        ]
        + [jax.ShapeDtypeStruct(shape, BF16) for shape in wholes],
        compiler_params=params(52),
        cost_estimate=cost(42),
        name="forward",
    )(meta, counts, att, x, gain, bias, *[p for group in pieces for p in group], *after)


def norm_two_back(counts, owner, tile, z_ref, r_ref, scaled_ref):
    half = BLOCK // 2
    width = z_ref.shape[1]
    inside = lax.broadcasted_iota(jnp.int32, (half, width), 0)
    grads = []
    for group in range(TILE // half):
        at = tile * (TILE // half) + group
        rows = slice(group * half, (group + 1) * half)
        scaled = scaled_ref[pl.ds(owner[at], 1), :]
        z = z_ref[rows, :].astype(F32)
        plain = jnp.mean(scaled, axis=-1, keepdims=True)
        cross = jnp.mean(scaled * z, axis=-1, keepdims=True)
        grad = r_ref[rows, :] * (scaled - plain - z * cross)
        grads.append(jnp.where(inside < counts[at], grad, 0.0))
    return jnp.concatenate(grads, axis=0)


def ffn_back_kernel(starts, meta, counts, owner, *refs):
    @pl.when(pl.program_id(0) < meta[TILES])
    def _():
        ffn_back_tile(starts, meta, counts, owner, *refs)


def ffn_back_tile(
    starts, meta, counts, owner, low_ref, saved_ref, wd0, wd1, wg0, wg1, wu0, wu1, *refs,
):
    tile = pl.program_id(0)
    span = wd0.shape[0]
    acc_g, acc_u, acc_d, wd_turned, wg_turned, wu_turned = refs[-6:]
    keep_ref, send_ref = refs[-8:-6]
    part_out = refs[-9]
    width = low_ref.shape[1]

    @pl.when(tile == 0)
    def _():
        acc_g[...] = jnp.zeros_like(acc_g)
        acc_u[...] = jnp.zeros_like(acc_u)
        acc_d[...] = jnp.zeros_like(acc_d)
        for half, (wd, wg, wu) in enumerate(((wd0, wg0, wu0), (wd1, wg1, wu1))):
            columns = slice(half * span, (half + 1) * span)
            wd_turned[:, columns] = wd[...].T
            wg_turned[columns, :] = wg[...].T
            wu_turned[columns, :] = wu[...].T

    if starts:
        branch = norm_two_back(counts, owner, tile, *refs[:3]).astype(BF16)
        part_out[:, :width] = branch
    else:
        branch = refs[0][...]
    low_t = low_ref[...].T
    branch_t = branch.T
    hiddens = [
        dot(branch, wd_turned[:, half * span : (half + 1) * span]) for half in range(2)
    ]
    total = None
    for half in range(2):
        columns = slice(half * span, (half + 1) * span)
        hid, silu, slope = (
            saved_ref[:, (kind * 2 + half) * span : (kind * 2 + half + 1) * span] for kind in range(3)
        )
        acc_d[:, columns] += dot(branch_t, hid)
        grad_hidden = hiddens[half]
        grad_gate = (grad_hidden * slope.astype(F32)).astype(BF16)
        grad_up = (grad_hidden * silu.astype(F32)).astype(BF16)
        part = dot(grad_gate, wg_turned[columns, :]) + dot(grad_up, wu_turned[columns, :])
        total = part if total is None else total + part
        acc_g[:, columns] += dot(low_t, grad_gate)
        acc_u[:, columns] += dot(low_t, grad_up)
    part_out[:, part_out.shape[1] - width :] = total.astype(BF16)

    @pl.when(tile == meta[TILES] - 1)
    def _():
        rows, quarter = acc_g.shape[0] // 4, acc_g.shape[0] // 4
        side, row, core = meta[SIDE], meta[ROW], meta[CORE]
        for other_core, out in ((0, keep_ref), (1, send_ref)):
            columns = pl.ds(pl.multiple_of((core ^ other_core) * span, span), span)
            inner = pl.ds(
                pl.multiple_of((core ^ other_core) * (span // 2), span // 2), span // 2
            )
            for other_side in range(2):
                for other_row in range(2):
                    at = (side ^ other_side) * 2 + (row ^ other_row)
                    lines = pl.ds(pl.multiple_of(at * quarter, quarter), quarter)
                    out[other_side, other_row, 0] = acc_g[lines, columns].astype(BF16)
                    out[other_side, other_row, 1] = acc_u[lines, columns].astype(BF16)
                    left = pl.multiple_of(
                        (side ^ other_side) * span + (core ^ other_core) * (span // 2), span // 2
                    )
                    for part in range(2):
                        lines = pl.ds(
                            pl.multiple_of((row ^ other_row) * 2 * quarter + part * quarter, quarter),
                            quarter,
                        )
                        out[
                            other_side, other_row, 2, :, part * (span // 2) : (part + 1) * (span // 2)
                        ] = acc_d[lines, pl.ds(left, span // 2)].astype(BF16)


def ffn_back(meta, counts, owner, chunk, low, saved, wd, wg, wu, given, after=()):
    rows, width = low.shape
    inner, span = wg.shape[1], SPAN
    starts = len(given) == 3
    halves = (chunk, chunk + inner // (2 * span))

    def fixed(shape, index):
        return pl.BlockSpec(shape, lambda i, *_: index, pipeline_mode=pl.Buffered(1))

    if starts:
        given_specs = [tiled(width), tiled(1), resident(given[2].shape)]
    else:
        given_specs = [tiled(width)] + anywhere(len(given) - 1)
    grid_spec = pltpu.PrefetchScalarGridSpec(
        num_scalar_prefetch=3,
        grid=(rows // TILE,),
        in_specs=[tiled(width), tiled(6 * span, chunk)]
        + [fixed((span, width), (at, 0)) for at in halves]
        + [fixed((width, span), (0, at)) for _ in range(2) for at in halves]
        + given_specs
        + anywhere(len(after)),
        out_specs=[tiled(2 * width) if starts else tiled(width, len(given) - 1)]
        + [pl.BlockSpec((2, 2, 3, width // 4, span), lambda i, *_: (0, 0, 0, 0, 0))] * 2,
        scratch_shapes=[pltpu.VMEM((width, 2 * span), F32)] * 3
        + [pltpu.VMEM((width, 2 * span), BF16)]
        + [pltpu.VMEM((2 * span, width), BF16)] * 2,
    )
    piece = jax.ShapeDtypeStruct((2, 2, 3, width // 4, span), BF16)
    return pl.pallas_call(
        functools.partial(ffn_back_kernel, starts),
        grid_spec=grid_spec,
        out_shape=[jax.ShapeDtypeStruct((rows, 2 * width), BF16), piece, piece],
        input_output_aliases={12: 0} if len(given) == 2 else {},
        compiler_params=params(44),
        cost_estimate=cost(23),
        name="ffn_back",
    )(
        meta, counts, owner, low, saved, wd, wd, wg, wg, wu, wu, *given, *after,
    )


def out_pieces(meta, acc, keep_ref, send_ref):
    part = acc.shape[0] // 8
    side, row, core = meta[SIDE], meta[ROW], meta[CORE]
    for other_core, out in ((0, keep_ref), (1, send_ref)):
        for other_side in range(2):
            for other_row in range(2):
                at = ((side ^ other_side) * 2 + (row ^ other_row)) * 2 + (core ^ other_core)
                lines = pl.ds(pl.multiple_of(at * part, part), part)
                out[other_side, other_row, :, : acc.shape[1]] = acc[lines, :].astype(BF16)


@while_live
def norm_one_back_kernel(
    meta, head_ref, tail_ref, z_ref, r_ref, att_ref, gain_ref, wo_ref, later_ref, *refs,
):
    sum_ref, att_grad_ref, gains_out, keep_ref, send_ref, acc, wo_turned = refs[-7:]
    tile = pl.program_id(0)

    @pl.when(tile == 0)
    def _():
        acc[...] = jnp.zeros_like(acc)
        gains_out[...] = later_ref[...]
        wo_turned[...] = wo_ref[...].T

    width = wo_ref.shape[0]
    first = sum(ref[:, at : at + width].astype(F32) for ref in (head_ref, tail_ref) for at in (0, width))
    z = z_ref[...].astype(F32)
    scaled = first * gain_ref[...]
    plain = jnp.mean(scaled, axis=-1, keepdims=True)
    cross = jnp.mean(scaled * z, axis=-1, keepdims=True)
    grad = r_ref[...] * (scaled - plain - z * cross)
    sum_ref[...] = grad
    low = grad.astype(BF16)
    att_grad_ref[...] = dot(low, wo_turned[...]).astype(BF16)
    acc[...] += dot(att_ref[...].T, low)
    gains_out[0:1, :] += jnp.sum(first * z, axis=0, keepdims=True)
    gains_out[1:2, :] += jnp.sum(first, axis=0, keepdims=True)

    @pl.when(tile == meta[TILES] - 1)
    def _():
        out_pieces(meta, acc, keep_ref, send_ref)


def norm_one_back(meta, terms, z, recip, att, gain, wo, later, after=()):
    rows, width = z.shape
    block = (2, 2, width // 8, width)
    piece = jax.ShapeDtypeStruct(block, BF16)
    grid_spec = pltpu.PrefetchScalarGridSpec(
        num_scalar_prefetch=1,
        grid=(rows // TILE,),
        in_specs=[tiled(2 * width), tiled(2 * width), tiled(width)]
        + [tiled(1), tiled(width)]
        + [resident(gain.shape), resident(wo.shape), resident(later.shape)]
        + anywhere(len(after)),
        out_specs=[tiled(width), tiled(width), pl.BlockSpec((8, width), lambda i, *_: (0, 0))]
        + [pl.BlockSpec(block, lambda i, *_: (0, 0, 0, 0))] * 2,
        scratch_shapes=[pltpu.VMEM((width, width), F32), pltpu.VMEM((width, width), BF16)],
    )
    return pl.pallas_call(
        norm_one_back_kernel,
        grid_spec=grid_spec,
        out_shape=[
            jax.ShapeDtypeStruct((rows, width), F32), jax.ShapeDtypeStruct((rows, width), BF16),
            jax.ShapeDtypeStruct((8, width), F32), piece, piece,
        ],
        compiler_params=params(28),
        cost_estimate=cost(12),
        name="norm_one_back",
    )(meta, *terms, z, recip, att, gain, wo, later, *after)


def attend_back_kernel(meta, q_ref, k_ref, v_ref, g_ref, att_ref, lse_ref, cos_ref, sin_ref, *refs):
    out_ref, key_acc, value_acc = refs[-3:]

    def turn_back(grad, table):
        cosine, sine = cos_ref[table, :], sin_ref[table, :]
        return (grad * cosine - swap_halves(grad) * sine).astype(BF16)

    def products(start, size, keys, values, limit, masked):
        rows = pl.ds(start, size)
        queries, grads = split_pair(q_ref[rows, :]), split_pair(g_ref[rows, :])
        log_norm = jnp.concatenate([lse_ref[0, 0:1, rows], lse_ref[0, 1:2, rows]], axis=1)
        if limit is not None:
            column = lax.broadcasted_iota(jnp.int32, log_norm.shape, 1) % size
            log_norm = jnp.where(column < limit, log_norm, -MASKED)
        both = g_ref[rows, :].astype(F32) * att_ref[rows, :].astype(F32)
        head = lax.broadcasted_iota(jnp.int32, (8, 128), 1) // HEAD
        ones = (head == lax.broadcasted_iota(jnp.int32, (8, 128), 0)).astype(F32)
        inner = lax.dot_general(
            ones, both, (((1,), (1,)), ((), ())), precision=lax.Precision.HIGHEST, preferred_element_type=F32
        )
        inner = jnp.concatenate([inner[0:1, :], inner[1:2, :]], axis=1)
        scores = masked(dot(keys, queries, ((1,), (1,))))
        grad_probs = dot(values, grads, ((1,), (1,)))
        return queries, grads, log_norm, inner, scores, grad_probs

    def finish(queries, grads, log_norm, inner, scores, grad_probs, keys_split):
        probs = jnp.exp(scores - log_norm)
        grad_scores = (probs * (grad_probs - inner)).astype(BF16)
        grad_query = (dot(keys_split, stack_heads(grad_scores)) * HEAD**-0.5).T
        return grad_query, dot(grad_scores, queries), dot(probs.astype(BF16), grads)

    @pl.loop(0, 2)
    def _(doc):
        start = pl.multiple_of(meta[OFF0 + doc], BLOCK)
        for blocks in range(1, 7):

            @pl.when(meta[CNT0 + doc] == blocks)
            def _():
                size = blocks * BLOCK
                whole = pl.ds(start, size)
                keys, values = k_ref[whole, :], v_ref[whole, :]
                keys_split = split_turned(keys)
                valid = meta[LEN0 + doc] - (blocks - 1) * BLOCK
                steps = (blocks + 1) // 2

                def ahead_of(step):
                    return products(
                        pl.multiple_of(start + step * TILE, BLOCK), TILE, keys, values,
                        size - step * TILE if size < (step + 1) * TILE else None,
                        lambda scores: mask_keys(scores, blocks - 1, valid),
                    )

                ahead = ahead_of(0)
                for step in range(steps):
                    now = ahead
                    if step + 1 < steps:
                        ahead = ahead_of(step + 1)
                    grad_query, grad_key, grad_value = finish(*now, keys_split)
                    if step > 0:
                        grad_key += key_acc[:size, :]
                        grad_value += value_acc[:size, :]
                    if step + 1 < steps:
                        key_acc[:size, :] = grad_key
                        value_acc[:size, :] = grad_value
                    for sub in range(2):
                        at = pl.multiple_of(start + step * TILE + sub * BLOCK, BLOCK)
                        out_ref[pl.ds(at, BLOCK), 0:128] = turn_back(
                            grad_query[sub * BLOCK : (sub + 1) * BLOCK, :],
                            pl.ds((step * 2 + sub) * BLOCK, BLOCK),
                        )
                out_ref[whole, 128:256] = turn_back(grad_key, pl.ds(0, size))
                out_ref[whole, 256:384] = grad_value.astype(BF16)

    first = pl.multiple_of(meta[OFFQ], BLOCK)
    rows = pl.ds(first, BLOCK)
    keys = k_ref[rows, :]
    grad_query, grad_key, grad_value = finish(
        *products(first, BLOCK, keys, v_ref[rows, :], None, functools.partial(query_mask, meta)),
        split_turned(keys),
    )
    table = pl.ds(cos_ref.shape[0] - BLOCK, BLOCK)
    out_ref[rows, 0:128] = turn_back(grad_query, table)
    out_ref[rows, 128:256] = turn_back(grad_key, table)
    out_ref[rows, 256:384] = grad_value.astype(BF16)
    out_ref[pl.ds(first + BLOCK, BLOCK), :] = jnp.zeros((BLOCK, 384), BF16)


def attend_back(meta, pair, qkv, grad, att, lse, tables, before=(), after=()):
    rows, width = grad.shape
    pairs = width // 128

    def column(part, columns=128):
        return pl.BlockSpec((rows, columns), lambda h, *_: (0, part * pairs + pair))

    grid_spec = pltpu.PrefetchScalarGridSpec(
        num_scalar_prefetch=1,
        grid=(1,),
        in_specs=[
            column(0), column(1), column(2), column(0),
            column(0),
            pl.BlockSpec((1, 8, rows), lambda h, *_: (pair, 0, 0)),
            resident(tables[0].shape), resident(tables[1].shape),
        ]
        + anywhere(len(before) + len(after)),
        out_specs=pl.BlockSpec((rows, 384), lambda h, *_: (0, pair)),
        scratch_shapes=[pltpu.VMEM((6 * BLOCK, 128), F32)] * 2,
    )
    return pl.pallas_call(
        attend_back_kernel,
        grid_spec=grid_spec,
        out_shape=jax.ShapeDtypeStruct((rows, 3 * width), BF16),
        input_output_aliases={9: 0} if before else {},
        compiler_params=params(44),
        cost_estimate=cost(11),
        name="attend_back",
    )(meta, qkv, qkv, qkv, grad, att, lse, *tables, *before, *after)


@while_live
def qkv_grad_kernel(meta, x_ref, *refs):
    keep_ref, send_ref, acc = refs[-3:]
    columns = acc.shape[1]
    pairs = columns // 384
    grad_ref, extra = refs[0], refs[1:3]
    tile = pl.program_id(0)

    @pl.when(tile == 0)
    def _():
        acc[...] = jnp.zeros_like(acc)

    grad = jnp.concatenate(
        [
            grad_ref[:, (pair * 3 + part) * 128 : (pair * 3 + part + 1) * 128]
            for part in range(3)
            for pair in range(pairs)
        ],
        axis=1,
    )
    acc[...] += dot(x_ref[...].T, grad)

    @pl.when(tile == meta[TILES] - 1)
    def _():
        out_pieces(meta, acc, keep_ref, send_ref)
        if keep_ref.shape[3] > columns:
            keep_ref[:, :, :, columns:] = extra[0][...]
            send_ref[:, :, :, columns:] = extra[1][...]


def qkv_grad(meta, x, grad, columns, at, extra=(), after=()):
    rows, width = x.shape
    block = (2, 2, width // 8, columns + sum(part.shape[3] for part in extra[:1]))
    piece = jax.ShapeDtypeStruct(block, BF16)
    grid_spec = pltpu.PrefetchScalarGridSpec(
        num_scalar_prefetch=1,
        grid=(rows // TILE,),
        in_specs=[tiled(width)]
        + [tiled(columns, at)]
        + [resident(part.shape) for part in extra]
        + anywhere(len(after)),
        out_specs=[pl.BlockSpec(block, lambda i, *_: (0, 0, 0, 0))] * 2,
        scratch_shapes=[pltpu.VMEM((width, columns), F32)],
    )
    return pl.pallas_call(
        qkv_grad_kernel,
        grid_spec=grid_spec,
        out_shape=[piece, piece],
        compiler_params=params(44),
        cost_estimate=cost(9),
        name="qkv_grad",
    )(meta, x, grad, *extra, *after)


def token_grad_kernel(which, meta, *refs):
    sums, grads, weight = refs[0:2], refs[2:4], refs[4]
    step = pl.program_id(0)

    def value():
        total = jnp.concatenate([part[...] for part in sums], axis=0)
        return total + dot(jnp.concatenate([part[...] for part in grads], axis=0), weight[...])

    if which == 0:
        docs_ref = refs[-1]
        length = meta[LEN0] - step * TILE
        store = lambda value: docs_ref.__setitem__(0, value)
    else:
        docs_ref, queries_ref = refs[-2:]
        length = jnp.where(step < 3, meta[LEN1] - step * TILE, TILE)
        store = lambda value: docs_ref.__setitem__(slice(None), value.astype(BF16))

    @pl.when((step < 3) & (length > 0))
    def _():
        total = value()
        inside = lax.broadcasted_iota(jnp.int32, total.shape, 0)
        store(jnp.where(inside < length, total, 0.0))

    @pl.when((step < 3) & (length <= 0))
    def _():
        store(jnp.zeros((TILE, docs_ref.shape[-1]), F32))

    if which == 1:

        @pl.when(step == 3)
        def _():
            total = value()[:BLOCK, :]
            inside = lax.broadcasted_iota(jnp.int32, (BLOCK // 2, total.shape[1]), 0)
            for query in range(2):
                half = total[query * (BLOCK // 2) : (query + 1) * (BLOCK // 2), :]
                queries_ref[query] = jnp.where(inside < meta[QLEN0 + query], half, 0.0)


def token_grad(which, meta, sums, grad, weight, after=()):
    rows, width = sums.shape

    def block_of(step, meta, second):
        last = meta[CNT0 + which] - 1
        in_doc = jnp.minimum(jnp.minimum(step, 2) * 2 + second, last)
        return jnp.where(step < 3, meta[OFF0 + which] // BLOCK + in_doc, meta[OFFQ] // BLOCK)

    def halves(columns):
        return [
            pl.BlockSpec((BLOCK, columns), lambda i, meta, s=s: (block_of(i, meta, s), 0)) for s in range(2)
        ]

    if which == 0:
        out_specs = [pl.BlockSpec((1, TILE, width), lambda i, meta: (1 - meta[SLOT], i, 0))]
        out_shape = [jax.ShapeDtypeStruct((2, 6 * BLOCK, width), F32)]
    else:
        out_specs = [
            pl.BlockSpec((TILE, width), lambda i, meta: (jnp.minimum(i, 2), 0)),
            pl.BlockSpec((2, BLOCK // 2, width), lambda i, meta: (0, 0, 0)),
        ]
        out_shape = [
            jax.ShapeDtypeStruct((6 * BLOCK, width), BF16),
            jax.ShapeDtypeStruct((2, BLOCK // 2, width), F32),
        ]
    grid_spec = pltpu.PrefetchScalarGridSpec(
        num_scalar_prefetch=1,
        grid=(3 + which,),
        in_specs=halves(width) + halves(grad.shape[1]) + [resident(weight.shape)]
        + anywhere(len(after)),
        out_specs=out_specs,
    )
    return pl.pallas_call(
        functools.partial(token_grad_kernel, which),
        grid_spec=grid_spec,
        out_shape=out_shape,
        compiler_params=params(44),
        cost_estimate=cost(9),
        name="token_grad",
    )(meta, sums, sums, grad, grad, weight, *after)


def place_moved_kernel(meta, own_ref, other_ref, *refs):
    docs_ref = refs[-1]

    @pl.when(meta[STAY] == 1)
    def _():
        docs_ref[0] = own_ref[...].astype(F32)

    @pl.when(meta[STAY] == 0)
    def _():
        docs_ref[0] = other_ref[...].astype(F32)


def place_moved(meta, docs, own, other, after=()):
    width = docs.shape[2]
    grid_spec = pltpu.PrefetchScalarGridSpec(
        num_scalar_prefetch=1,
        grid=(3,),
        in_specs=[pl.BlockSpec((TILE, width), lambda i, m: (i, 0))] * 2 + anywhere(1 + len(after)),
        out_specs=pl.BlockSpec((1, TILE, width), lambda i, m: (m[SLOT], i, 0)),
    )
    return pl.pallas_call(
        place_moved_kernel,
        grid_spec=grid_spec,
        out_shape=jax.ShapeDtypeStruct(docs.shape, F32),
        input_output_aliases={3: 0},
        compiler_params=params(16),
        cost_estimate=cost(4),
        name="place_moved",
    )(meta, own, other, docs, *after)


def plan_kernel(place, own_ref, across_ref, queries_ref, meta, table_block, counts, owner):
    core = place[0]
    half = BLOCK // 2
    number = [
        jnp.where(core == 0, own_ref[at], across_ref[at]) if at < 2
        else jnp.where(core == 0, across_ref[at - 2], own_ref[at - 2])
        for at in range(4)
    ]
    blocks = [(count + BLOCK - 1) // BLOCK for count in number]
    work = [count * (10 + count) for count in blocks]
    total = work[0] + work[1] + work[2] + work[3]
    loads = [jnp.maximum(work[0] + work[at], total - work[0] - work[at]) for at in (1, 2, 3)]
    plan = jnp.where(
        (loads[0] <= loads[1]) & (loads[0] <= loads[2]), 0, jnp.where(loads[1] <= loads[2], 1, 2)
    )
    stay = jnp.where(plan == 0, 1, 0)
    far_slot = jnp.where(plan == 1, 0, 1)
    slot = jnp.where(core == 0, 1, far_slot)
    slot_there = jnp.where(core == 0, far_slot, 1)
    first = jnp.where(slot == 1, own_ref[0], own_ref[1])
    here = jnp.where(slot == 1, own_ref[1], own_ref[0])
    there = jnp.where(slot_there == 1, across_ref[1], across_ref[0])
    second = jnp.where(stay == 1, here, there)
    first_blocks, second_blocks = (first + BLOCK - 1) // BLOCK, (second + BLOCK - 1) // BLOCK
    end = first_blocks + second_blocks
    device = place[3]
    other = jnp.where(core == 0, device + 1, device - 1)
    values = [
        0, first_blocks * BLOCK, end * BLOCK, first, second, queries_ref[0], queries_ref[1],
        first_blocks, second_blocks, (end + 2) // 2, core, place[1], place[2], slot, stay,
        2 * device, 2 * device + 1, 2 * device + 1 - slot,
        jnp.where(stay == 1, 2 * device + slot, 2 * other + slot_there),
    ]
    for at, value in enumerate(values):
        meta[at] = jnp.int32(value)
    for at in range(len(values), meta.shape[0]):
        meta[at] = 0
    for at in range(table_block.shape[0]):
        table_block[at] = jnp.where(
            at < first_blocks, at, jnp.where(at < end, at - first_blocks, 6)
        )
    for at in range(counts.shape[0]):
        in_first, in_second = at < 2 * first_blocks, at < 2 * end
        query = at - 2 * end
        count = jnp.where(
            in_first,
            first - at * half,
            jnp.where(
                in_second,
                second - (at - 2 * first_blocks) * half,
                jnp.where(query == 0, queries_ref[0], jnp.where(query == 1, queries_ref[1], 0)),
            ),
        )
        counts[at] = jnp.clip(count, 0, half)
        owner[at] = jnp.where(in_first, 2, jnp.where(in_second, 3, jnp.clip(query, 0, 1)))


def layout(place, doc_counts, across, query_counts, rows):
    smem = pl.BlockSpec(memory_space=pltpu.SMEM)
    half_blocks = rows // (BLOCK // 2)
    return pl.pallas_call(
        plan_kernel,
        in_specs=[smem] * 4,
        out_specs=[smem] * 4,
        out_shape=[
            jax.ShapeDtypeStruct((length,), jnp.int32)
            for length in (24, rows // BLOCK, half_blocks, half_blocks)
        ],
        cost_estimate=cost(1),
        name="plan",
    )(place, doc_counts, across, query_counts)


def pack_kernel(meta, docs, received, queries, out, sems):
    stay, slot = meta[STAY], meta[SLOT]

    def copies():
        for block in range(docs.shape[1] // BLOCK):
            lines = pl.ds(block * BLOCK, BLOCK)
            to = out.at[pl.ds(pl.multiple_of(meta[OFF1] + block * BLOCK, BLOCK), BLOCK)]
            second = block < meta[CNT1]
            yield block < meta[CNT0], docs.at[1 - slot, lines], out.at[lines], sems.at[0, block]
            yield second & (stay == 1), docs.at[slot, lines], to, sems.at[1, block]
            yield second & (stay == 0), received.at[lines], to, sems.at[2, block]
        end = pl.multiple_of(meta[OFFQ], BLOCK)
        yield None, queries, out.at[pl.ds(end, BLOCK)], sems.at[3, 0]

    out[pl.ds(pl.multiple_of(meta[OFFQ] + BLOCK, BLOCK), BLOCK), :] = jnp.zeros((BLOCK, out.shape[1]), out.dtype)
    for step in ("start", "wait"):
        for needed, source, to, sem in copies():
            copy = pltpu.make_async_copy(source, to, sem)
            if needed is None:
                getattr(copy, step)()
            else:
                pl.when(needed)(getattr(copy, step))


def pack_rows(meta, docs, received, queries, rows):
    width = docs.shape[2]
    return pl.pallas_call(
        pack_kernel,
        in_specs=[pl.BlockSpec(memory_space=pltpu.SMEM)] + anywhere(3),
        out_specs=pl.BlockSpec(memory_space=pltpu.VMEM),
        out_shape=jax.ShapeDtypeStruct((rows, width), docs.dtype),
        scratch_shapes=[pltpu.SemaphoreType.DMA((4, docs.shape[1] // BLOCK))],
        compiler_params=pltpu.CompilerParams(vmem_limit_bytes=16 * 1024 * 1024),
        cost_estimate=cost(2),
        name="pack",
    )(meta, docs, received, queries.reshape(BLOCK, width))


def by_row(shape, values):
    row = lax.broadcasted_iota(jnp.int32, shape, 0) % 4
    first, second, third, fourth = (jnp.full(shape, value) for value in values)
    return jnp.where(row == 0, first, jnp.where(row == 1, second, jnp.where(row == 2, third, fourth)))


def lengths_of(meta):
    lengths = by_row((8, 128), [meta[QLEN0], meta[QLEN1], meta[LEN0], meta[LEN1]])
    return lengths[:, 0:1].astype(F32)


def unit_kernel(meta, owner, index, weights, sums_ref, gain_ref, bias_ref, message_ref, pooled_ref, sums_out, recip_ref):
    rows, width = sums_ref.shape
    shape = (8, 128)
    lane = lax.broadcasted_iota(jnp.int32, shape, 1)
    weight = by_row(shape, [weights[0], weights[1], jnp.float32(0.0), jnp.float32(0.0)])
    high = jnp.floor(weight * 16.0)
    rest = (weight * 16.0 - high) * 256.0
    middle = jnp.floor(rest)
    lowest = jnp.floor((rest - middle) * 256.0)
    number = by_row(shape, [meta[IDS + at] for at in range(4)]).astype(F32)
    partner = by_row(shape, [index[0], index[1], jnp.int32(0), jnp.int32(0)]).astype(F32)
    extra = jnp.zeros(shape, F32)
    for at, value in enumerate((number, partner, high, middle, lowest)):
        extra = jnp.where(lane == at, value, extra)
    per_tile = TILE // (BLOCK // 2)
    line = lax.broadcasted_iota(jnp.int32, (8, rows), 0) % 4
    column = lax.broadcasted_iota(jnp.int32, (8, rows), 1)
    pick = jnp.zeros((8, rows), F32)
    for group in range(rows // 8 * per_tile):
        at = group // per_tile * 8 + group % per_tile
        here = (column == at) & (line == owner[group]) & (group // per_tile < meta[TILES])
        pick = jnp.where(here, 1.0, pick)
    lengths = lengths_of(meta)
    inside = lax.broadcasted_iota(jnp.int32, (rows, width), 0) < 8 * meta[TILES]
    sums = lax.dot_general(
        pick, jnp.where(inside, sums_ref[...], 0.0), (((1,), (0,)), ((), ())),
        precision=lax.Precision.HIGHEST, preferred_element_type=F32,
    )
    pooled = sums / lengths * gain_ref[...] + bias_ref[...]
    recip = lax.rsqrt(jnp.sum(pooled * pooled, axis=1, keepdims=True) + EPS_UNIT)
    unit = (pooled * recip).astype(BF16)
    half = width // 2
    upper = lax.broadcasted_iota(jnp.int32, (8, half), 0) < 4
    message_ref[:, :half] = jnp.where(upper, unit[:, :half].astype(F32), unit[:, half:].astype(F32)).astype(BF16)
    message_ref[:, half:] = extra.astype(BF16)
    pooled_ref[...] = pooled
    sums_out[...] = sums
    recip_ref[...] = jnp.broadcast_to(recip, recip_ref.shape)


def units(meta, owner, index, weights, sums, gain, bias):
    vmem = pl.BlockSpec(memory_space=pltpu.VMEM)
    width = sums.shape[1]
    return pl.pallas_call(
        unit_kernel,
        in_specs=[pl.BlockSpec(memory_space=pltpu.SMEM)] * 4 + [vmem] * 3,
        out_specs=[vmem] * 4,
        out_shape=[
            jax.ShapeDtypeStruct((8, width // 2 + 128), BF16),
            jax.ShapeDtypeStruct((8, width), F32),
            jax.ShapeDtypeStruct((8, width), F32),
            jax.ShapeDtypeStruct((8, 128), F32),
        ],
        compiler_params=pltpu.CompilerParams(vmem_limit_bytes=16 * 1024 * 1024),
        name="unit",
    )(meta, owner, index, weights, sums, gain, bias)


def loss_kernel(meta, softness, gain_ref, pooled_ref, sums_ref, recip_ref, *refs):
    loss_ref, scaled_ref, later_ref = refs[-3:]
    message = jnp.concatenate([ref[...] for ref in refs[:-3]], axis=0)
    rows, half = message.shape[0], message.shape[1] - 128
    pairs = rows // 4
    soft = softness[0]
    low = message[:, :half]
    extra = message[:, half:].astype(F32)
    row = lax.broadcasted_iota(jnp.int32, (rows, pairs), 0) % 8
    index = (extra[:, 0:1] + 0.5).astype(jnp.int32)
    found = lax.broadcasted_iota(jnp.int32, (rows, pairs), 1) == index
    of_query, of_doc = found & (row % 4 < 2), found & (row % 4 >= 2)

    def gathered(chosen):
        halves = [
            dot((chosen & (row // 4 == which)).astype(F32).astype(BF16), low, ((0,), (0,))) for which in range(2)
        ]
        return jnp.concatenate(halves, axis=1).astype(BF16)

    units_q, units_d = gathered(of_query), gathered(of_doc)
    exact = functools.partial(
        lax.dot_general, precision=lax.Precision.HIGHEST, preferred_element_type=F32
    )
    plain, turned, over_rows = (((1,), (0,)), ((), ())), (((1,), (1,)), ((), ())), (((0,), (0,)), ((), ()))
    extra = exact((of_query & (row < 4)).astype(F32), extra, over_rows)
    weight = extra[:, 2:3] / 16.0 + extra[:, 3:4] / 4096.0 + extra[:, 4:5] / 1048576.0
    similarity = dot(units_q, units_d, ((1,), (1,))) / soft
    columns = lax.broadcasted_iota(jnp.int32, similarity.shape, 1)
    target = (columns == (extra[:, 1:2] + 0.5).astype(jnp.int32)).astype(F32)
    highest = jnp.max(similarity, axis=1, keepdims=True)
    log_norm = highest + jnp.log(jnp.sum(jnp.exp(similarity - highest), axis=1, keepdims=True))
    picked = jnp.sum(target * similarity, axis=1, keepdims=True)
    loss = jnp.sum(weight * (log_norm - picked), axis=0, keepdims=True) / pairs
    loss_ref[...] = jnp.broadcast_to(loss, loss_ref.shape)
    grad = weight * (jnp.exp(similarity - log_norm) - target) / pairs
    line = lax.broadcasted_iota(jnp.int32, (8, pairs), 0)
    column = lax.broadcasted_iota(jnp.int32, (8, pairs), 1)
    my_queries = (column == jnp.where(line == 0, meta[IDS], meta[IDS + 1])) & (line < 2)
    my_docs = (column == jnp.where(line == 2, meta[IDS + 2], meta[IDS + 3])) & (line >= 2) & (line < 4)
    query_rows = exact(my_queries.astype(F32), grad, plain)
    doc_rows = exact(my_docs.astype(F32), grad, turned)
    grad_unit = (
        exact(query_rows, units_d.astype(F32), plain) + exact(doc_rows, units_q.astype(F32), plain)
    ) / soft
    pooled, recip, lengths = pooled_ref[...], recip_ref[:, 0:1], lengths_of(meta)
    crossed = jnp.sum(grad_unit * pooled, axis=1, keepdims=True)
    grad_rows = (recip * grad_unit - pooled * (recip * recip * recip) * crossed) / lengths
    first_half = lax.broadcasted_iota(jnp.int32, grad_rows.shape, 0)
    grad_rows = jnp.where(first_half < 4, grad_rows, 0.0)
    scaled_ref[...] = grad_rows * gain_ref[...]
    gain = jnp.sum(grad_rows * sums_ref[...], axis=0, keepdims=True)
    bias = jnp.sum(grad_rows * lengths, axis=0, keepdims=True)
    later_ref[...] = jnp.where(first_half == 2, gain, jnp.where(first_half == 3, bias, 0.0))


def loss_and_grads(meta, softness, gain, pooled, sums, recip, messages):
    width = pooled.shape[1]
    vmem = pl.BlockSpec(memory_space=pltpu.VMEM)
    return pl.pallas_call(
        loss_kernel,
        in_specs=[pl.BlockSpec(memory_space=pltpu.SMEM)] * 2 + [vmem] * (4 + len(messages)),
        out_specs=[vmem, vmem, vmem],
        out_shape=[
            jax.ShapeDtypeStruct((8, 128), F32),
            jax.ShapeDtypeStruct((8, width), F32),
            jax.ShapeDtypeStruct((8, width), F32),
        ],
        compiler_params=pltpu.CompilerParams(vmem_limit_bytes=24 * 1024 * 1024),
        name="loss",
    )(meta, softness, gain, pooled, sums, recip, *messages)


def wide_unfold_kernel(piece, *refs):
    gate_ref, up_ref, down_ref = refs[-3:]
    gate_ref[...] = piece[0, 0].astype(F32)
    up_ref[...] = piece[0, 1].astype(F32)
    span = piece.shape[3] // 2
    block = jnp.concatenate([piece[0, 2, :, :span], piece[0, 2, :, span:]], axis=0)
    down_ref[...] = block.astype(F32).T


def wide_unfold(chunk, pieces, before, width, inner, after=()):
    quarter, span = pieces.shape[2:]
    chunks = inner // (2 * span)
    place = pl.BlockSpec((quarter, span), lambda i: (i // 2, (i % 2) * chunks + chunk))
    return pl.pallas_call(
        wide_unfold_kernel,
        grid=(4,),
        in_specs=[pl.BlockSpec((1, *pieces.shape[1:]), lambda i: (i, 0, 0, 0))]
        + anywhere(len(before) + len(after)),
        out_specs=[
            place, place,
            pl.BlockSpec((span // 2, 2 * quarter), lambda i: (2 * chunk + i % 2, i // 2)),
        ],
        out_shape=[
            jax.ShapeDtypeStruct((width // 2, inner), F32),
            jax.ShapeDtypeStruct((width // 2, inner), F32),
            jax.ShapeDtypeStruct((inner // 2, width), F32),
        ],
        input_output_aliases={1 + at: at for at in range(len(before))},
        compiler_params=params(16),
        cost_estimate=cost(3),
        name="wide_unfold",
    )(pieces, *before, *after)


def wide_unfold_parts_kernel(meta, p00, p01, p10, p11, *refs):
    gate_ref, up_ref, down_ref = refs[-3:]
    for other_core in range(2):
        for other_row in range(2):
            piece = ((p00, p01), (p10, p11))[other_core][other_row]

            @pl.when((pl.program_id(0) == other_core) & (pl.program_id(1) == other_row))
            def _():
                gate_ref[...] = piece[0].astype(F32)
                up_ref[...] = piece[1].astype(F32)
                span = piece.shape[2] // 2
                block = jnp.concatenate([piece[2, :, :span], piece[2, :, span:]], axis=0)
                down_ref[...] = block.astype(F32).T


def wide_unfold_parts(meta, chunk, pieces, before, width, inner, after=()):
    quarter, span = pieces[0].shape[1:]
    chunks = inner // (2 * span)
    aliased = [pl.BlockSpec(memory_space=pl.ANY)] * len(before)
    grid_spec = pltpu.PrefetchScalarGridSpec(
        num_scalar_prefetch=1,
        grid=(2, 2),
        in_specs=[resident(p.shape) for p in pieces] + aliased + anywhere(len(after)),
        out_specs=[
            pl.BlockSpec(
                (quarter, span), lambda c, r, m: (m[ROW] ^ r, (m[CORE] ^ c) * chunks + chunk)
            )
            for _ in range(2)
        ]
        + [
            pl.BlockSpec(
                (span // 2, 2 * quarter), lambda c, r, m: (2 * chunk + (m[CORE] ^ c), m[ROW] ^ r)
            )
        ],
    )
    return pl.pallas_call(
        wide_unfold_parts_kernel,
        grid_spec=grid_spec,
        out_shape=[
            jax.ShapeDtypeStruct((width // 2, inner), F32),
            jax.ShapeDtypeStruct((width // 2, inner), F32),
            jax.ShapeDtypeStruct((inner // 2, width), F32),
        ],
        input_output_aliases={5 + at: at for at in range(len(before))},
        compiler_params=params(16),
        cost_estimate=cost(3),
        name="wide_unfold_parts",
    )(meta, *pieces, *before, *after)


AXES = ("fsdp", "blk")


class Links:
    def __init__(self, sides, blk):
        self.sides, self.blk, self.outer = sides, blk, blk // 4

    def swap(self, value, side=0, mask=0):
        pairs = [
            (f * self.blk + b, (f ^ side) * self.blk + (b ^ mask))
            for f in range(self.sides)
            for b in range(self.blk)
        ]
        return lax.ppermute(value, AXES, pairs)

    def core(self, value):
        return self.swap(value, mask=1)

    def row(self, value):
        return self.swap(value, mask=2)

    def side(self, value):
        return self.swap(value, side=1)

    def shift(self, value, by):
        pairs = [
            (f * self.blk + b, f * self.blk + (b + 4 * by) % self.blk)
            for f in range(self.sides)
            for b in range(self.blk)
        ]
        return lax.ppermute(value, AXES, pairs)

    def step(self, value, moves):
        pairs = [
            (f * self.blk + 4 * start + b, f * self.blk + 4 * end + b)
            for f in range(self.sides)
            for start, end in moves
            for b in range(4)
        ]
        return lax.ppermute(value, AXES, pairs)

    def outer_masks(self):
        mask = 4
        while mask < self.blk:
            yield mask
            mask *= 2

    def gather(self, value):
        both = jnp.concatenate([value, self.core(value)], axis=0)
        plane = jnp.concatenate(
            [both, self.swap(both, 1, 0), self.swap(both, 0, 2), self.swap(both, 1, 2)], axis=0
        )
        return [plane] + [self.shift(plane, by) for by in range(1, self.outer)]

    def stages(self, keep, send, row_first, by_swaps=False):
        add = lambda *terms: sum(term.astype(F32) for term in terms).astype(BF16)
        now = yield
        now = yield (send := tie(send, now))
        received = tie(self.core(send), now)
        if row_first:
            now = yield (away := add(keep[:, 1], received[:, 1]))
            across = tie(self.row(away), now)
            now = yield (away := add(keep[1, 0], received[1, 0], across[1]))
            last = self.side(away)
        else:
            now = yield (away := add(keep[1], received[1]))
            across = tie(self.side(away), now)
            now = yield (away := add(keep[0, 1], received[0, 1], across[1]))
            last = self.row(away)
        mine = add(keep[0, 0], received[0, 0], across[0], tie(last, now))
        if self.outer == 4:
            outer = lax.axis_index("blk") // 4
            now = yield mine
            mine = add(mine, tie(self.step(mine, ((0, 1), (3, 2))), now))
            now = yield mine
            mine = add(mine, tie(self.step(mine, ((1, 2), (2, 1))), now))
            now = yield mine
            result = tie(self.step(mine, ((1, 0), (2, 3))), now)
            mine = jnp.where((outer == 1) | (outer == 2), mine, result)
        else:
            for mask in self.outer_masks():
                now = yield mine
                mine = add(mine, tie(self.swap(mine, mask=mask), now))
        if by_swaps:
            now = yield mine
            other = tie(self.row(mine), now)
            yield other
            return mine, other, self.core(mine), self.core(other)
        groups = [[at + part for part in range(4)] for at in range(0, self.blk, 4)]
        flat = mine.reshape(-1, mine.shape[-1])
        gathered = lax.all_gather(flat, "blk", axis_index_groups=groups, axis=0, tiled=True)
        yield mine
        return gathered

    def stages_small(self, value):
        now = yield
        for side, mask in [(0, 1), (1, 0), (0, 2)] + [(0, mask) for mask in self.outer_masks()]:
            value = tie(value, now)
            now = yield value
            value = value + self.swap(value, side, mask)
        return value


def tie(value, now):
    return lax.optimization_barrier((value, now))[0]


class Flow:
    def __init__(self):
        self.sums, self.done = {}, {}

    def begin(self, name, stages):
        next(stages)
        self.sums[name] = stages

    def forward(self, now, *names):
        sent = []
        for name in names:
            if name in self.done:
                continue
            try:
                sent.append(self.sums[name].send(now))
            except StopIteration as end:
                self.done[name] = end.value
                if name == "s":
                    sent.append(end.value)
        return tuple(sent)

    def result(self, now, name):
        while name not in self.done:
            self.forward(now, name)
        return self.done[name]


def part_of(share, parts, at):
    size = share.shape[0] // parts
    return lax.dynamic_slice_in_dim(share, at * size, size, 0)


def body(
    question_activations,
    passage_activations,
    question_unpadded_counts,
    passage_unpadded_counts,
    correct_passage_index,
    query_weights,
    softness_factor,
    combined_projection_matrix,
    mixing_result_matrix,
    gating_matrix,
    widening_matrix,
    narrowing_matrix,
    initial_layernorm_scale,
    initial_layernorm_shift,
    later_layernorm_scale,
    later_layernorm_shift,
):
    doc_len, width = passage_activations.shape[1:]
    query_len = question_activations.shape[1]
    inner = gating_matrix.shape[1]
    assert passage_activations.shape[0] == 2 and doc_len == 6 * BLOCK and 2 * query_len == BLOCK
    links = Links(lax.axis_size("fsdp"), lax.axis_size("blk"))
    side, blk = lax.axis_index("fsdp"), lax.axis_index("blk")
    core, row = blk % 2, (blk // 2) % 2

    part_qkv = part_of(combined_projection_matrix, 2, core)
    got_qkv = links.side(part_qkv)
    quarter = row * 2 + core
    part_out = tie(part_of(mixing_result_matrix, 2, core), got_qkv)
    part_gate = tie(part_of(gating_matrix, 4, quarter), got_qkv)
    got_out, got_gate = links.side(part_out), links.side(part_gate)
    rows = -(-(2 * doc_len + BLOCK) // TILE) * TILE
    place = jnp.stack([core, side, row, side * links.blk + blk]).astype(jnp.int32)
    per_chip = tie(passage_unpadded_counts.astype(jnp.int32), part_qkv)
    query_counts = question_unpadded_counts.astype(jnp.int32)
    meta, table_block, counts, owner = layout(place, per_chip, links.core(per_chip), query_counts, rows)
    sent_doc = lax.dynamic_index_in_dim(passage_activations, meta[SLOT], 0, keepdims=False)
    tables = tuple(jnp.asarray(table) for table in rotary_tables(doc_len, query_len))
    x = pack_rows(meta, passage_activations, links.core(sent_doc), question_activations, rows)

    got_qkv = tie(got_qkv, x)
    pieces_qkv = (combined_projection_matrix, got_qkv, links.core(got_qkv))
    qkv, wqkv = project(meta, table_block, x, pieces_qkv, tables, (part_out, part_gate))
    got_out, got_gate = tie((got_out, got_gate), qkv)
    own_vectors = tie(
        (initial_layernorm_scale, initial_layernorm_shift, later_layernorm_scale, later_layernorm_shift),
        qkv,
    )
    vectors = jnp.stack(own_vectors)
    others = links.side(vectors)
    vectors = jnp.concatenate(
        [jnp.where(side == 0, vectors, others), jnp.where(side == 0, others, vectors)], axis=1
    ).astype(F32)
    gain_one, bias_one, gain_two, bias_two = (vectors[at : at + 1] for at in range(4))
    part_up = tie(part_of(widening_matrix, 4, quarter), qkv)
    far_out, along_gate, got_up = links.core(got_out), links.row(got_gate), links.side(part_up)
    heads = attend(meta, qkv, 0, 2, (), (got_out, got_gate, part_up))
    along_gate, got_up = tie((along_gate, got_up), heads[1])
    part_down = tie(part_of(narrowing_matrix, 4, quarter), heads[1])
    far_gate = links.core(got_gate), links.core(along_gate)
    along_up, got_down = links.row(got_up), links.side(part_down)
    heads = attend(meta, qkv, 1, 2, heads, (far_out, along_gate, got_up, part_down))
    along_up, got_down = tie((along_up, got_down), heads[1])
    far_up = links.core(got_up), links.core(along_up)
    along_down = links.row(got_down)
    att, lse = attend(
        meta, qkv, 2, 2, heads, (*far_gate, along_up, got_down, vectors)
    )
    along_down = tie(along_down, lse)
    far_down = links.core(got_down), links.core(along_down)
    weights = [
        (mixing_result_matrix, got_out, far_out),
        (gating_matrix, got_gate, along_gate, *far_gate),
        (widening_matrix, got_up, along_up, *far_up),
        (narrowing_matrix, got_down, along_down, *far_down),
    ]
    low, z1, r1, saved, z2, r2, sums, wo, wg, wu, wd = forward(
        meta, counts, att, x, weights, gain_one, bias_one
    )

    message, pooled, z_sums, recip = units(
        meta, owner, correct_passage_index.astype(jnp.int32), query_weights, sums, gain_two, bias_two
    )
    loss, scaled, later = loss_and_grads(
        meta, softness_factor, gain_two, pooled, z_sums, recip, links.gather(message)
    )
    flow = Flow()

    def wide(chunk, given, after):
        out, keep, send = ffn_back(
            meta, counts, owner, chunk, low, saved, wd, wg, wu, given, after
        )
        flow.begin("w%d" % chunk, links.stages(keep, send, chunk == 2, chunk == 2))
        return out, keep

    def score(pair, before, after):
        return attend_back(meta, pair, qkv, grad_att, att, lse, tables, before, after)

    def narrow(group, columns, at, extra, after):
        keep, send = qkv_grad(meta, x, grads, columns, at, extra, after)
        flow.begin("q%d" % group, links.stages(keep, send, group == 0))
        return keep

    head, now = wide(0, (z2, r2, scaled), ())
    tail, now = wide(1, (head,), flow.forward(now, "w0"))
    tail, now = wide(2, (head, tail), flow.forward(now, "w0", "w1"))
    sum_one, grad_att, now, *mixing = norm_one_back(
        meta, (head, tail), z1, r1, att, gain_one, wo, later, flow.forward(now, "w0", "w1", "w2")
    )
    flow.begin("s", links.stages_small(now))
    grads = score(0, (), flow.forward(now, "w0", "w2"))
    grads = score(1, (grads,), flow.forward(grads, "w0"))
    grads = score(2, (grads,), flow.forward(grads, "w0", "w1"))
    grads = score(3, (grads,), flow.forward(grads, "w0", "w2"))
    now = narrow(0, 1536, 0, mixing, flow.forward(grads, "w1"))
    grads = score(4, (grads,), flow.forward(now, "w1", "w2", "q0"))
    now = grads = score(5, (grads,), flow.forward(grads, "w0", "w1", "w2", "q0"))
    unfold = lambda chunk, before, after: wide_unfold(
        chunk, flow.result(now, "w%d" % chunk).reshape(4, 3, width // 4, -1), before, width, inner, after
    )
    grad_wide = unfold(0, (), ())
    now = narrow(1, 768, 2, (), (*flow.forward(now, "w1", "w2"), grad_wide[0]))
    (grad_docs,) = token_grad(
        0, meta, sum_one, grads, wqkv, flow.forward(now, "w2", "q0", "q1", "s")
    )
    moved, grad_queries = token_grad(
        1, meta, sum_one, grads, wqkv, (grad_docs, *flow.forward(grad_docs, "q0", "q1", "s"))
    )
    other_moved = links.core(moved)
    grad_wide = unfold(1, grad_wide, flow.forward(moved, "w1", "w2", "q0", "q1", "s"))
    now = grad_wide[0]
    grad_docs = place_moved(
        meta, grad_docs, moved, other_moved, (now, *flow.forward(now, "w2", "q0", "q1", "s"))
    )
    after = flow.forward(grad_docs, "q0", "q1", "s")
    grad_wide = wide_unfold_parts(
        meta, 2, flow.result(grad_docs, "w2"), grad_wide, width, inner, (grad_docs, *after)
    )
    while len(flow.done) < 6:
        flow.forward(moved, "q0", "q1", "s")
    first_part, second_part = flow.done["q0"], flow.done["q1"]
    joint = first_part.shape[1] - width
    grad_qkv = jnp.concatenate(
        [
            part.astype(F32)
            for parts in zip(jnp.split(first_part[:, :joint], 3, axis=1), jnp.split(second_part, 3, axis=1))
            for part in parts
        ],
        axis=1,
    )
    grad_out = first_part[:, joint:].astype(F32)
    small = lax.dynamic_slice_in_dim(flow.done["s"], side * (width // 2), width // 2, 1)
    return (
        loss[0, :1],
        grad_queries,
        grad_docs,
        grad_qkv,
        grad_out,
        grad_wide[0],
        grad_wide[1],
        grad_wide[2],
        small[0],
        small[1],
        small[2],
        small[3],
    )


def solution(mesh):
    placed = (
        P(("fsdp", "blk"), None, None),
        P(("fsdp", "blk"), None, None),
        P(("fsdp", "blk")),
        P(("fsdp", "blk")),
        P(("fsdp", "blk")),
        P(("fsdp", "blk")),
        P(),
        P("fsdp", None),
        P("fsdp", None),
        P("fsdp", None),
        P("fsdp", None),
        P("fsdp", None),
        P("fsdp"),
        P("fsdp"),
        P("fsdp"),
        P("fsdp"),
    )
    return jax.shard_map(
        body,
        mesh=mesh,
        in_specs=placed,
        out_specs=(
            P(),
            P(("fsdp", "blk"), None, None),
            P(("fsdp", "blk"), None, None),
            P("fsdp", None),
            P("fsdp", None),
            P("fsdp", None),
            P("fsdp", None),
            P("fsdp", None),
            P("fsdp"),
            P("fsdp"),
            P("fsdp"),
            P("fsdp"),
        ),
        check_vma=False,
    )
```

```python
import functools

import jax
import jax.numpy as jnp
import numpy as np
from jax import lax
from jax.experimental import pallas as pl
from jax.experimental.pallas import tpu as pltpu
from jax.sharding import PartitionSpec as P

HEAD = 64
BLOCK = 128
TILE = 256
EPS_NORM = 1e-05
EPS_UNIT = 1e-06
MASKED = -1e30
F32 = jnp.float32
BF16 = jnp.bfloat16
PACE = 0.5
SPAN = 512
OFF0, OFF1, OFFQ, LEN0, LEN1, QLEN0, QLEN1, CNT0, CNT1, TILES, CORE, SIDE, ROW, SLOT, STAY, IDS = range(16)


def dot(left, right, contract=((1,), (0,))):
    return lax.dot_general(left, right, (contract, ((), ())), preferred_element_type=F32)


def cost(microseconds):
    return pl.CostEstimate(flops=int(microseconds * PACE * 1e9), bytes_accessed=0, transcendentals=0)


def params(mebibytes=60):
    return pltpu.CompilerParams(vmem_limit_bytes=mebibytes * 1024 * 1024)


def rotary_tables(doc_len, query_len):
    frequency = 1000.0 ** (-(np.arange(HEAD // 2, dtype=np.float32) * 2.0 / HEAD))
    positions = np.concatenate([np.arange(doc_len), np.arange(query_len), np.arange(query_len)])
    angles = positions.astype(np.float32)[:, None] * frequency.astype(np.float32)[None, :]
    cosine, sine = np.cos(angles), np.sin(angles)
    return (
        np.concatenate([cosine] * 4, axis=1).astype(np.float32),
        np.concatenate([-sine, sine, -sine, sine], axis=1).astype(np.float32),
    )


def swap_halves(pair):
    lane = lax.broadcasted_iota(jnp.int32, pair.shape, 1)
    return jnp.where(lane % HEAD < HEAD // 2, pltpu.roll(pair, 96, 1), pltpu.roll(pair, 32, 1))


def live(step, meta):
    return jnp.minimum(step, meta[TILES] - 1)


def tiled(columns, at=0):
    return pl.BlockSpec((TILE, columns), lambda i, m, *_: (live(i, m), at))


def while_live(kernel):
    @functools.wraps(kernel)
    def run(meta, *refs):
        @pl.when(pl.program_id(0) < meta[TILES])
        def _():
            kernel(meta, *refs)

    return run


def anywhere(count):
    return [pl.BlockSpec(memory_space=pl.ANY)] * count


def resident(shape):
    return pl.BlockSpec(shape, lambda *_: (0,) * len(shape), pipeline_mode=pl.Buffered(1))


def piece_copies(meta, rows, pieces, whole, sems):
    side, row, core = meta[SIDE], meta[ROW], meta[CORE]
    parts = len(pieces) - 1
    if parts == 2:
        places = [core, 1 - core]
    else:
        places = [row * 2 + core, (1 - row) * 2 + core, row * 2 + 1 - core, (1 - row) * 2 + 1 - core]
    size = rows // parts
    starts = [side * rows] + [(1 - side) * rows + place * size for place in places]
    return [
        pltpu.make_async_copy(
            piece, whole.at[pl.ds(pl.multiple_of(start, 16), piece.shape[0]), :], sems.at[at]
        )
        for at, (piece, start) in enumerate(zip(pieces, starts))
    ]


def qkv_kernel(meta, table_block, x_ref, cos_ref, sin_ref, *refs):
    pieces, (out_ref, turned_out, w_ref, turned, sems, out_sem) = refs[:3], refs[-6:]
    tile = pl.program_id(0)
    keep = pltpu.make_async_copy(turned, turned_out, out_sem)

    @pl.when(tile == 0)
    def _():
        copies = piece_copies(meta, pieces[0].shape[0], pieces, w_ref, sems)
        for copy in copies:
            copy.start()
        for copy in copies:
            copy.wait()

    @pl.when(tile == 1)
    def _():
        width = x_ref.shape[1]
        for pair in range(width // 128):
            for part in range(3):
                at, to = part * width + pair * 128, (pair * 3 + part) * 128
                turned[to : to + 128, :] = w_ref[:, at : at + 128].T
        keep.start()

    @pl.when(tile < meta[TILES])
    def _():
        x = x_ref[...]
        width = x.shape[1]

        def turn(part, acc):
            scale = HEAD**-0.5 if part == 0 else 1.0
            for sub in range(TILE // BLOCK):
                rows = slice(sub * BLOCK, (sub + 1) * BLOCK)
                table = pl.ds(table_block[tile * (TILE // BLOCK) + sub] * BLOCK, BLOCK)
                cosine, sine = cos_ref[table, :] * scale, sin_ref[table, :] * scale
                for group in range(width // 128):
                    pair = acc[rows, group * 128 : (group + 1) * 128]
                    turned_pair = pair * cosine + swap_halves(pair) * sine
                    at = part * width + group * 128
                    out_ref[rows, at : at + 128] = turned_pair.astype(BF16)

        queries = dot(x, w_ref[:, :width])
        keys = dot(x, w_ref[:, width : 2 * width])
        turn(0, queries)
        values = dot(x, w_ref[:, 2 * width :])
        turn(1, keys)
        out_ref[:, 2 * width :] = values.astype(BF16)

    @pl.when(tile == pl.num_programs(0) - 1)
    def _():
        keep.wait()


def project(meta, table_block, x, pieces, tables, after=()):
    rows, width = x.shape
    whole = (width, 3 * width)
    grid_spec = pltpu.PrefetchScalarGridSpec(
        num_scalar_prefetch=2,
        grid=(rows // TILE,),
        in_specs=[tiled(width), resident(tables[0].shape), resident(tables[1].shape)]
        + anywhere(len(pieces) + len(after)),
        out_specs=[tiled(3 * width)] + anywhere(1),
        scratch_shapes=[
            pltpu.VMEM(whole, BF16),
            pltpu.VMEM(whole[::-1], BF16),
            pltpu.SemaphoreType.DMA((len(pieces),)),
            pltpu.SemaphoreType.DMA,
        ],
    )
    return pl.pallas_call(
        qkv_kernel,
        grid_spec=grid_spec,
        out_shape=[
            jax.ShapeDtypeStruct((rows, 3 * width), BF16),
            jax.ShapeDtypeStruct(whole[::-1], BF16),
        ],
        compiler_params=params(36),
        cost_estimate=cost(11),
        name="qkv",
    )(meta, table_block, x, *tables, *pieces, *after)


def split_pair(pair):
    lane = lax.broadcasted_iota(jnp.int32, pair.shape, 1)
    zero = jnp.zeros_like(pair)
    return jnp.concatenate(
        [jnp.where(lane < HEAD, pair, zero), jnp.where(lane < HEAD, zero, pair)], axis=0
    )


def mask_keys(scores, last, valid):
    rows = lax.broadcasted_iota(jnp.int32, (BLOCK, scores.shape[1]), 0)
    tail = jnp.where(rows < valid, scores[last * BLOCK :, :], MASKED)
    if last == 0:
        return tail
    return jnp.concatenate([scores[: last * BLOCK, :], tail], axis=0)


def query_mask(meta, scores):
    half = scores.shape[0] // 2
    key = lax.broadcasted_iota(jnp.int32, scores.shape, 0)
    row = lax.broadcasted_iota(jnp.int32, scores.shape, 1) % (2 * half)
    length = jnp.where(key < half, meta[QLEN0], meta[QLEN1])
    keep = ((key < half) == (row < half)) & (key % half < length)
    return jnp.where(keep, scores, MASKED)


def split_turned(pair):
    turned = pair.T
    row = lax.broadcasted_iota(jnp.int32, turned.shape, 0)
    zero = jnp.zeros_like(turned)
    return jnp.concatenate(
        [jnp.where(row < HEAD, turned, zero), jnp.where(row < HEAD, zero, turned)], axis=1
    )


def stack_heads(pair_wide):
    half = pair_wide.shape[1] // 2
    return jnp.concatenate([pair_wide[:, :half], pair_wide[:, half:]], axis=0)


def attend_kernel(meta, q_ref, k_ref, v_ref, *refs):
    out_ref, lse_ref = refs[-2:]

    def scores_of(start, size, keys, masked):
        return masked(dot(keys, split_pair(q_ref[pl.ds(start, size), :]), ((1,), (1,))))

    def finish(start, size, scores, values):
        rows = pl.ds(start, size)
        highest = jnp.max(scores, axis=0, keepdims=True)
        exponent = jnp.exp(scores - highest)
        total = jnp.sum(exponent, axis=0, keepdims=True)
        attended = dot(values, stack_heads(exponent.astype(BF16)))
        recip = 1.0 / total
        row = lax.broadcasted_iota(jnp.int32, attended.shape, 0)
        attended = attended * jnp.where(row < HEAD, recip[:, :size], recip[:, size:])
        out_ref[rows, :] = attended.T.astype(BF16)
        log_norm = highest + jnp.log(total)
        lse_ref[0, 0:1, rows] = log_norm[:, :size]
        lse_ref[0, 1:2, rows] = log_norm[:, size:]

    def run(starts, size, keys, values, masked):
        ahead = scores_of(starts[0], size, keys, masked)
        for at, start in enumerate(starts):
            scores = ahead
            if at + 1 < len(starts):
                ahead = scores_of(starts[at + 1], size, keys, masked)
            finish(start, size, scores, values)

    @pl.loop(0, 2)
    def _(doc):
        start = pl.multiple_of(meta[OFF0 + doc], BLOCK)
        for blocks in range(1, 7):

            @pl.when(meta[CNT0 + doc] == blocks)
            def _():
                whole = pl.ds(start, blocks * BLOCK)
                valid = meta[LEN0 + doc] - (blocks - 1) * BLOCK
                starts = [pl.multiple_of(start + at * TILE, BLOCK) for at in range((blocks + 1) // 2)]
                run(
                    starts, TILE, k_ref[whole, :], split_turned(v_ref[whole, :]),
                    lambda scores: mask_keys(scores, blocks - 1, valid),
                )

    first = pl.multiple_of(meta[OFFQ], BLOCK)
    rows = pl.ds(first, BLOCK)
    run(
        [first], BLOCK, k_ref[rows, :], split_turned(v_ref[rows, :]), functools.partial(query_mask, meta)
    )
    out_ref[pl.ds(first + BLOCK, BLOCK), :] = jnp.zeros((BLOCK, 128), BF16)


def attend(meta, qkv, group, members, before=(), after=()):
    rows, width = qkv.shape[0], qkv.shape[1] // 3
    pairs = width // 128

    def column(part):
        return pl.BlockSpec((rows, 128), lambda h, *_: (0, part * pairs + group * members + h))

    grid_spec = pltpu.PrefetchScalarGridSpec(
        num_scalar_prefetch=1,
        grid=(members,),
        in_specs=[column(0), column(1), column(2)] + anywhere(len(before) + len(after)),
        out_specs=[
            column(0),
            pl.BlockSpec((1, 8, rows), lambda h, *_: (group * members + h, 0, 0)),
        ],
    )
    return pl.pallas_call(
        attend_kernel,
        grid_spec=grid_spec,
        out_shape=[
            jax.ShapeDtypeStruct((rows, width), BF16),
            jax.ShapeDtypeStruct((pairs, 8, rows), F32),
        ],
        input_output_aliases={4 + at: at for at in range(len(before))},
        compiler_params=params(28),
        cost_estimate=cost(13),
        name="attend",
    )(meta, qkv, qkv, qkv, *before, *after)


def normalize(summed):
    centered = summed - jnp.mean(summed, axis=-1, keepdims=True)
    recip = lax.rsqrt(jnp.mean(centered * centered, axis=-1, keepdims=True) + EPS_NORM)
    return centered * recip, recip


def forward_kernel(
    meta, counts, att_ref, x_ref, gain_ref, bias_ref, *refs,
):
    outs, scratch = refs[-18:-7], refs[-7:]
    pieces = [refs[0:3], refs[3:8], refs[8:13], refs[13:16]]
    low_ref, z1_ref, r1_ref, saved_ref, z2_ref, r2_ref, sums_ref = outs[:7]
    whole_outs = outs[7:]
    wholes, (sems, out_sems) = scratch[:4], scratch[5:]
    wo_ref, wg_ref, wu_ref, wd_ref = wholes
    tile = pl.program_id(0)
    copies = [
        piece_copies(meta, pieces[at][0].shape[0], pieces[at], wholes[at], sems.at[at])
        for at in range(4)
    ]
    keeps = [
        pltpu.make_async_copy(wholes[at], whole_outs[at], out_sems.at[at]) for at in range(4)
    ]

    @pl.when(tile == 0)
    def _():
        for group in copies:
            for copy in group:
                copy.start()

    def ready(which):
        @pl.when(tile == 0)
        def _():
            for at in which:
                for copy in copies[at]:
                    copy.wait()
                keeps[at].start()

    ready((0,))

    @pl.when(tile < meta[TILES])
    def _():
        z1, r1 = normalize(x_ref[...].astype(F32) + dot(att_ref[...], wo_ref[...]))
        z1_ref[...] = z1.astype(BF16)
        r1_ref[...] = r1
        normed = z1 * gain_ref[...] + bias_ref[...]
        low_ref[...] = normed.astype(BF16)
        scratch[4][...] = normed

    ready((1, 2, 3))

    @pl.when(tile < meta[TILES])
    def _():
        low = low_ref[...]
        total = scratch[4][...]
        inner, chunk = wg_ref.shape[1], SPAN
        chunks = inner // (2 * chunk)

        def products(at):
            columns = slice(at, at + chunk)
            return dot(low, wg_ref[:, columns]), dot(low, wu_ref[:, columns])

        ahead = products(0)
        for at in range(0, inner, chunk):
            columns = slice(at, at + chunk)
            gate, up = ahead
            if at + chunk < inner:
                ahead = products(at + chunk)
            sigmoid = 0.5 * jnp.tanh(0.5 * gate) + 0.5
            silu = gate * sigmoid
            hidden = (silu * up).astype(BF16)
            slope = (up * (sigmoid + silu * (1.0 - sigmoid))).astype(BF16)
            which = at // chunk
            for kind, value in enumerate((hidden, silu.astype(BF16), slope)):
                to = ((which % chunks) * 6 + kind * 2 + which // chunks) * chunk
                saved_ref[:, to : to + chunk] = value
            total = total + dot(hidden, wd_ref[columns, :])
        z2, r2 = normalize(total)
        z2_ref[...] = z2.astype(BF16)
        r2_ref[...] = r2
        half = BLOCK // 2
        inside = lax.broadcasted_iota(jnp.int32, (half, z2.shape[1]), 0)
        for group in range(TILE // half):
            valid = counts[tile * (TILE // half) + group]
            kept = jnp.where(inside < valid, z2[group * half : (group + 1) * half, :], 0.0)
            sums_ref[group : group + 1, :] = jnp.sum(kept, axis=0, keepdims=True)
        sums_ref[TILE // half :, :] = jnp.zeros((8 - TILE // half, z2.shape[1]), F32)

    @pl.when(tile == pl.num_programs(0) - 1)
    def _():
        for keep in keeps:
            keep.wait()


def forward(meta, counts, att, x, pieces, gain, bias, after=()):
    rows, width = x.shape
    inner = pieces[1][0].shape[1]
    wholes = [(width, width), (width, inner), (width, inner), (inner, width)]

    def array(columns, kind):
        return jax.ShapeDtypeStruct((rows, columns), kind)

    grid_spec = pltpu.PrefetchScalarGridSpec(
        num_scalar_prefetch=2,
        grid=(rows // TILE,),
        in_specs=[tiled(width), tiled(width)]
        + [resident(gain.shape), resident(bias.shape)]
        + anywhere(16 + len(after)),
        out_specs=[
            tiled(width), tiled(width), tiled(1), tiled(3 * inner), tiled(width), tiled(1),
            pl.BlockSpec((8, width), lambda i, m, *_: (live(i, m), 0)),
        ]
        + anywhere(4),
        scratch_shapes=[pltpu.VMEM(shape, BF16) for shape in wholes]
        + [
            pltpu.VMEM((TILE, width), F32),
            pltpu.SemaphoreType.DMA((4, 5)),
            pltpu.SemaphoreType.DMA((4,)),
        ],
    )
    return pl.pallas_call(
        forward_kernel,
        grid_spec=grid_spec,
        out_shape=[
            array(width, BF16), array(width, BF16), array(1, F32), array(3 * inner, BF16),
            array(width, BF16), array(1, F32),
            jax.ShapeDtypeStruct((rows // TILE * 8, width), F32),
        ]
        + [jax.ShapeDtypeStruct(shape, BF16) for shape in wholes],
        compiler_params=params(52),
        cost_estimate=cost(42),
        name="forward",
    )(meta, counts, att, x, gain, bias, *[p for group in pieces for p in group], *after)


def norm_two_back(counts, owner, tile, z_ref, r_ref, scaled_ref):
    half = BLOCK // 2
    width = z_ref.shape[1]
    inside = lax.broadcasted_iota(jnp.int32, (half, width), 0)
    grads = []
    for group in range(TILE // half):
        at = tile * (TILE // half) + group
        rows = slice(group * half, (group + 1) * half)
        scaled = scaled_ref[pl.ds(owner[at], 1), :]
        z = z_ref[rows, :].astype(F32)
        plain = jnp.mean(scaled, axis=-1, keepdims=True)
        cross = jnp.mean(scaled * z, axis=-1, keepdims=True)
        grad = r_ref[rows, :] * (scaled - plain - z * cross)
        grads.append(jnp.where(inside < counts[at], grad, 0.0))
    return jnp.concatenate(grads, axis=0)


def ffn_back_kernel(starts, meta, counts, owner, *refs):
    @pl.when(pl.program_id(0) < meta[TILES])
    def _():
        ffn_back_tile(starts, meta, counts, owner, *refs)


def ffn_back_tile(
    starts, meta, counts, owner, low_ref, saved_ref, wd0, wd1, wg0, wg1, wu0, wu1, *refs,
):
    tile = pl.program_id(0)
    span = wd0.shape[0]
    acc_g, acc_u, acc_d, wd_turned, wg_turned, wu_turned = refs[-6:]
    keep_ref, send_ref = refs[-8:-6]
    part_out = refs[-9]
    width = low_ref.shape[1]

    @pl.when(tile == 0)
    def _():
        acc_g[...] = jnp.zeros_like(acc_g)
        acc_u[...] = jnp.zeros_like(acc_u)
        acc_d[...] = jnp.zeros_like(acc_d)
        for half, (wd, wg, wu) in enumerate(((wd0, wg0, wu0), (wd1, wg1, wu1))):
            columns = slice(half * span, (half + 1) * span)
            wd_turned[:, columns] = wd[...].T
            wg_turned[columns, :] = wg[...].T
            wu_turned[columns, :] = wu[...].T

    if starts:
        branch = norm_two_back(counts, owner, tile, *refs[:3]).astype(BF16)
        part_out[:, :width] = branch
    else:
        branch = refs[0][...]
    low_t = low_ref[...].T
    branch_t = branch.T
    hiddens = [
        dot(branch, wd_turned[:, half * span : (half + 1) * span]) for half in range(2)
    ]
    total = None
    for half in range(2):
        columns = slice(half * span, (half + 1) * span)
        hid, silu, slope = (
            saved_ref[:, (kind * 2 + half) * span : (kind * 2 + half + 1) * span] for kind in range(3)
        )
        acc_d[:, columns] += dot(branch_t, hid)
        grad_hidden = hiddens[half]
        grad_gate = (grad_hidden * slope.astype(F32)).astype(BF16)
        grad_up = (grad_hidden * silu.astype(F32)).astype(BF16)
        part = dot(grad_gate, wg_turned[columns, :]) + dot(grad_up, wu_turned[columns, :])
        total = part if total is None else total + part
        acc_g[:, columns] += dot(low_t, grad_gate)
        acc_u[:, columns] += dot(low_t, grad_up)
    part_out[:, part_out.shape[1] - width :] = total.astype(BF16)

    @pl.when(tile == meta[TILES] - 1)
    def _():
        rows, quarter = acc_g.shape[0] // 4, acc_g.shape[0] // 4
        side, row, core = meta[SIDE], meta[ROW], meta[CORE]
        for other_core, out in ((0, keep_ref), (1, send_ref)):
            columns = pl.ds(pl.multiple_of((core ^ other_core) * span, span), span)
            inner = pl.ds(
                pl.multiple_of((core ^ other_core) * (span // 2), span // 2), span // 2
            )
            for other_side in range(2):
                for other_row in range(2):
                    at = (side ^ other_side) * 2 + (row ^ other_row)
                    lines = pl.ds(pl.multiple_of(at * quarter, quarter), quarter)
                    out[other_side, other_row, 0] = acc_g[lines, columns].astype(BF16)
                    out[other_side, other_row, 1] = acc_u[lines, columns].astype(BF16)
                    left = pl.multiple_of(
                        (side ^ other_side) * span + (core ^ other_core) * (span // 2), span // 2
                    )
                    for part in range(2):
                        lines = pl.ds(
                            pl.multiple_of((row ^ other_row) * 2 * quarter + part * quarter, quarter),
                            quarter,
                        )
                        out[
                            other_side, other_row, 2, :, part * (span // 2) : (part + 1) * (span // 2)
                        ] = acc_d[lines, pl.ds(left, span // 2)].astype(BF16)


def ffn_back(meta, counts, owner, chunk, low, saved, wd, wg, wu, given, after=()):
    rows, width = low.shape
    inner, span = wg.shape[1], SPAN
    starts = len(given) == 3
    halves = (chunk, chunk + inner // (2 * span))

    def fixed(shape, index):
        return pl.BlockSpec(shape, lambda i, *_: index, pipeline_mode=pl.Buffered(1))

    if starts:
        given_specs = [tiled(width), tiled(1), resident(given[2].shape)]
    else:
        given_specs = [tiled(width)] + anywhere(len(given) - 1)
    grid_spec = pltpu.PrefetchScalarGridSpec(
        num_scalar_prefetch=3,
        grid=(rows // TILE,),
        in_specs=[tiled(width), tiled(6 * span, chunk)]
        + [fixed((span, width), (at, 0)) for at in halves]
        + [fixed((width, span), (0, at)) for _ in range(2) for at in halves]
        + given_specs
        + anywhere(len(after)),
        out_specs=[tiled(2 * width) if starts else tiled(width, len(given) - 1)]
        + [pl.BlockSpec((2, 2, 3, width // 4, span), lambda i, *_: (0, 0, 0, 0, 0))] * 2,
        scratch_shapes=[pltpu.VMEM((width, 2 * span), F32)] * 3
        + [pltpu.VMEM((width, 2 * span), BF16)]
        + [pltpu.VMEM((2 * span, width), BF16)] * 2,
    )
    piece = jax.ShapeDtypeStruct((2, 2, 3, width // 4, span), BF16)
    return pl.pallas_call(
        functools.partial(ffn_back_kernel, starts),
        grid_spec=grid_spec,
        out_shape=[jax.ShapeDtypeStruct((rows, 2 * width), BF16), piece, piece],
        input_output_aliases={12: 0} if len(given) == 2 else {},
        compiler_params=params(44),
        cost_estimate=cost(23),
        name="ffn_back",
    )(
        meta, counts, owner, low, saved, wd, wd, wg, wg, wu, wu, *given, *after,
    )


def out_pieces(meta, acc, keep_ref, send_ref):
    part = acc.shape[0] // 8
    side, row, core = meta[SIDE], meta[ROW], meta[CORE]
    for other_core, out in ((0, keep_ref), (1, send_ref)):
        for other_side in range(2):
            for other_row in range(2):
                at = ((side ^ other_side) * 2 + (row ^ other_row)) * 2 + (core ^ other_core)
                lines = pl.ds(pl.multiple_of(at * part, part), part)
                out[other_side, other_row, :, : acc.shape[1]] = acc[lines, :].astype(BF16)


@while_live
def norm_one_back_kernel(
    meta, head_ref, tail_ref, z_ref, r_ref, att_ref, gain_ref, wo_ref, later_ref, *refs,
):
    sum_ref, att_grad_ref, gains_out, keep_ref, send_ref, acc, wo_turned = refs[-7:]
    tile = pl.program_id(0)

    @pl.when(tile == 0)
    def _():
        acc[...] = jnp.zeros_like(acc)
        gains_out[...] = later_ref[...]
        wo_turned[...] = wo_ref[...].T

    width = wo_ref.shape[0]
    first = sum(ref[:, at : at + width].astype(F32) for ref in (head_ref, tail_ref) for at in (0, width))
    z = z_ref[...].astype(F32)
    scaled = first * gain_ref[...]
    plain = jnp.mean(scaled, axis=-1, keepdims=True)
    cross = jnp.mean(scaled * z, axis=-1, keepdims=True)
    grad = r_ref[...] * (scaled - plain - z * cross)
    sum_ref[...] = grad
    low = grad.astype(BF16)
    att_grad_ref[...] = dot(low, wo_turned[...]).astype(BF16)
    acc[...] += dot(att_ref[...].T, low)
    gains_out[0:1, :] += jnp.sum(first * z, axis=0, keepdims=True)
    gains_out[1:2, :] += jnp.sum(first, axis=0, keepdims=True)

    @pl.when(tile == meta[TILES] - 1)
    def _():
        out_pieces(meta, acc, keep_ref, send_ref)


def norm_one_back(meta, terms, z, recip, att, gain, wo, later, after=()):
    rows, width = z.shape
    block = (2, 2, width // 8, width)
    piece = jax.ShapeDtypeStruct(block, BF16)
    grid_spec = pltpu.PrefetchScalarGridSpec(
        num_scalar_prefetch=1,
        grid=(rows // TILE,),
        in_specs=[tiled(2 * width), tiled(2 * width), tiled(width)]
        + [tiled(1), tiled(width)]
        + [resident(gain.shape), resident(wo.shape), resident(later.shape)]
        + anywhere(len(after)),
        out_specs=[tiled(width), tiled(width), pl.BlockSpec((8, width), lambda i, *_: (0, 0))]
        + [pl.BlockSpec(block, lambda i, *_: (0, 0, 0, 0))] * 2,
        scratch_shapes=[pltpu.VMEM((width, width), F32), pltpu.VMEM((width, width), BF16)],
    )
    return pl.pallas_call(
        norm_one_back_kernel,
        grid_spec=grid_spec,
        out_shape=[
            jax.ShapeDtypeStruct((rows, width), F32), jax.ShapeDtypeStruct((rows, width), BF16),
            jax.ShapeDtypeStruct((8, width), F32), piece, piece,
        ],
        compiler_params=params(28),
        cost_estimate=cost(12),
        name="norm_one_back",
    )(meta, *terms, z, recip, att, gain, wo, later, *after)


def attend_back_kernel(meta, q_ref, k_ref, v_ref, g_ref, att_ref, lse_ref, cos_ref, sin_ref, *refs):
    out_ref, key_acc, value_acc = refs[-3:]

    def turn_back(grad, table):
        cosine, sine = cos_ref[table, :], sin_ref[table, :]
        return (grad * cosine - swap_halves(grad) * sine).astype(BF16)

    def products(start, size, keys, values, limit, masked):
        rows = pl.ds(start, size)
        queries, grads = split_pair(q_ref[rows, :]), split_pair(g_ref[rows, :])
        log_norm = jnp.concatenate([lse_ref[0, 0:1, rows], lse_ref[0, 1:2, rows]], axis=1)
        if limit is not None:
            column = lax.broadcasted_iota(jnp.int32, log_norm.shape, 1) % size
            log_norm = jnp.where(column < limit, log_norm, -MASKED)
        both = g_ref[rows, :].astype(F32) * att_ref[rows, :].astype(F32)
        head = lax.broadcasted_iota(jnp.int32, (8, 128), 1) // HEAD
        ones = (head == lax.broadcasted_iota(jnp.int32, (8, 128), 0)).astype(F32)
        inner = lax.dot_general(
            ones, both, (((1,), (1,)), ((), ())), precision=lax.Precision.HIGHEST, preferred_element_type=F32
        )
        inner = jnp.concatenate([inner[0:1, :], inner[1:2, :]], axis=1)
        scores = masked(dot(keys, queries, ((1,), (1,))))
        grad_probs = dot(values, grads, ((1,), (1,)))
        return queries, grads, log_norm, inner, scores, grad_probs

    def finish(queries, grads, log_norm, inner, scores, grad_probs, keys_split):
        probs = jnp.exp(scores - log_norm)
        grad_scores = (probs * (grad_probs - inner)).astype(BF16)
        grad_query = (dot(keys_split, stack_heads(grad_scores)) * HEAD**-0.5).T
        return grad_query, dot(grad_scores, queries), dot(probs.astype(BF16), grads)

    @pl.loop(0, 2)
    def _(doc):
        start = pl.multiple_of(meta[OFF0 + doc], BLOCK)
        for blocks in range(1, 7):

            @pl.when(meta[CNT0 + doc] == blocks)
            def _():
                size = blocks * BLOCK
                whole = pl.ds(start, size)
                keys, values = k_ref[whole, :], v_ref[whole, :]
                keys_split = split_turned(keys)
                valid = meta[LEN0 + doc] - (blocks - 1) * BLOCK
                steps = (blocks + 1) // 2

                def ahead_of(step):
                    return products(
                        pl.multiple_of(start + step * TILE, BLOCK), TILE, keys, values,
                        size - step * TILE if size < (step + 1) * TILE else None,
                        lambda scores: mask_keys(scores, blocks - 1, valid),
                    )

                ahead = ahead_of(0)
                for step in range(steps):
                    now = ahead
                    if step + 1 < steps:
                        ahead = ahead_of(step + 1)
                    grad_query, grad_key, grad_value = finish(*now, keys_split)
                    if step > 0:
                        grad_key += key_acc[:size, :]
                        grad_value += value_acc[:size, :]
                    if step + 1 < steps:
                        key_acc[:size, :] = grad_key
                        value_acc[:size, :] = grad_value
                    for sub in range(2):
                        at = pl.multiple_of(start + step * TILE + sub * BLOCK, BLOCK)
                        out_ref[pl.ds(at, BLOCK), 0:128] = turn_back(
                            grad_query[sub * BLOCK : (sub + 1) * BLOCK, :],
                            pl.ds((step * 2 + sub) * BLOCK, BLOCK),
                        )
                out_ref[whole, 128:256] = turn_back(grad_key, pl.ds(0, size))
                out_ref[whole, 256:384] = grad_value.astype(BF16)

    first = pl.multiple_of(meta[OFFQ], BLOCK)
    rows = pl.ds(first, BLOCK)
    keys = k_ref[rows, :]
    grad_query, grad_key, grad_value = finish(
        *products(first, BLOCK, keys, v_ref[rows, :], None, functools.partial(query_mask, meta)),
        split_turned(keys),
    )
    table = pl.ds(cos_ref.shape[0] - BLOCK, BLOCK)
    out_ref[rows, 0:128] = turn_back(grad_query, table)
    out_ref[rows, 128:256] = turn_back(grad_key, table)
    out_ref[rows, 256:384] = grad_value.astype(BF16)
    out_ref[pl.ds(first + BLOCK, BLOCK), :] = jnp.zeros((BLOCK, 384), BF16)


def attend_back(meta, pair, qkv, grad, att, lse, tables, before=(), after=()):
    rows, width = grad.shape
    pairs = width // 128

    def column(part, columns=128):
        return pl.BlockSpec((rows, columns), lambda h, *_: (0, part * pairs + pair))

    grid_spec = pltpu.PrefetchScalarGridSpec(
        num_scalar_prefetch=1,
        grid=(1,),
        in_specs=[
            column(0), column(1), column(2), column(0),
            column(0),
            pl.BlockSpec((1, 8, rows), lambda h, *_: (pair, 0, 0)),
            resident(tables[0].shape), resident(tables[1].shape),
        ]
        + anywhere(len(before) + len(after)),
        out_specs=pl.BlockSpec((rows, 384), lambda h, *_: (0, pair)),
        scratch_shapes=[pltpu.VMEM((6 * BLOCK, 128), F32)] * 2,
    )
    return pl.pallas_call(
        attend_back_kernel,
        grid_spec=grid_spec,
        out_shape=jax.ShapeDtypeStruct((rows, 3 * width), BF16),
        input_output_aliases={9: 0} if before else {},
        compiler_params=params(44),
        cost_estimate=cost(11),
        name="attend_back",
    )(meta, qkv, qkv, qkv, grad, att, lse, *tables, *before, *after)


@while_live
def qkv_grad_kernel(meta, x_ref, *refs):
    keep_ref, send_ref, acc = refs[-3:]
    columns = acc.shape[1]
    pairs = columns // 384
    grad_ref, extra = refs[0], refs[1:3]
    tile = pl.program_id(0)

    @pl.when(tile == 0)
    def _():
        acc[...] = jnp.zeros_like(acc)

    grad = jnp.concatenate(
        [
            grad_ref[:, (pair * 3 + part) * 128 : (pair * 3 + part + 1) * 128]
            for part in range(3)
            for pair in range(pairs)
        ],
        axis=1,
    )
    acc[...] += dot(x_ref[...].T, grad)

    @pl.when(tile == meta[TILES] - 1)
    def _():
        out_pieces(meta, acc, keep_ref, send_ref)
        if keep_ref.shape[3] > columns:
            keep_ref[:, :, :, columns:] = extra[0][...]
            send_ref[:, :, :, columns:] = extra[1][...]


def qkv_grad(meta, x, grad, columns, at, extra=(), after=()):
    rows, width = x.shape
    block = (2, 2, width // 8, columns + sum(part.shape[3] for part in extra[:1]))
    piece = jax.ShapeDtypeStruct(block, BF16)
    grid_spec = pltpu.PrefetchScalarGridSpec(
        num_scalar_prefetch=1,
        grid=(rows // TILE,),
        in_specs=[tiled(width)]
        + [tiled(columns, at)]
        + [resident(part.shape) for part in extra]
        + anywhere(len(after)),
        out_specs=[pl.BlockSpec(block, lambda i, *_: (0, 0, 0, 0))] * 2,
        scratch_shapes=[pltpu.VMEM((width, columns), F32)],
    )
    return pl.pallas_call(
        qkv_grad_kernel,
        grid_spec=grid_spec,
        out_shape=[piece, piece],
        compiler_params=params(44),
        cost_estimate=cost(9),
        name="qkv_grad",
    )(meta, x, grad, *extra, *after)


def token_grad_kernel(which, meta, *refs):
    sums, grads, weight = refs[0:2], refs[2:4], refs[4]
    step = pl.program_id(0)

    def value():
        total = jnp.concatenate([part[...] for part in sums], axis=0)
        return total + dot(jnp.concatenate([part[...] for part in grads], axis=0), weight[...])

    if which == 0:
        docs_ref = refs[-1]
        length = meta[LEN0] - step * TILE
        store = lambda value: docs_ref.__setitem__(0, value)
    else:
        docs_ref, queries_ref = refs[-2:]
        length = jnp.where(step < 3, meta[LEN1] - step * TILE, TILE)
        store = lambda value: docs_ref.__setitem__(slice(None), value.astype(BF16))

    @pl.when((step < 3) & (length > 0))
    def _():
        total = value()
        inside = lax.broadcasted_iota(jnp.int32, total.shape, 0)
        store(jnp.where(inside < length, total, 0.0))

    @pl.when((step < 3) & (length <= 0))
    def _():
        store(jnp.zeros((TILE, docs_ref.shape[-1]), F32))

    if which == 1:

        @pl.when(step == 3)
        def _():
            total = value()[:BLOCK, :]
            inside = lax.broadcasted_iota(jnp.int32, (BLOCK // 2, total.shape[1]), 0)
            for query in range(2):
                half = total[query * (BLOCK // 2) : (query + 1) * (BLOCK // 2), :]
                queries_ref[query] = jnp.where(inside < meta[QLEN0 + query], half, 0.0)


def token_grad(which, meta, sums, grad, weight, after=()):
    rows, width = sums.shape

    def block_of(step, meta, second):
        last = meta[CNT0 + which] - 1
        in_doc = jnp.minimum(jnp.minimum(step, 2) * 2 + second, last)
        return jnp.where(step < 3, meta[OFF0 + which] // BLOCK + in_doc, meta[OFFQ] // BLOCK)

    def halves(columns):
        return [
            pl.BlockSpec((BLOCK, columns), lambda i, meta, s=s: (block_of(i, meta, s), 0)) for s in range(2)
        ]

    if which == 0:
        out_specs = [pl.BlockSpec((1, TILE, width), lambda i, meta: (1 - meta[SLOT], i, 0))]
        out_shape = [jax.ShapeDtypeStruct((2, 6 * BLOCK, width), F32)]
    else:
        out_specs = [
            pl.BlockSpec((TILE, width), lambda i, meta: (jnp.minimum(i, 2), 0)),
            pl.BlockSpec((2, BLOCK // 2, width), lambda i, meta: (0, 0, 0)),
        ]
        out_shape = [
            jax.ShapeDtypeStruct((6 * BLOCK, width), BF16),
            jax.ShapeDtypeStruct((2, BLOCK // 2, width), F32),
        ]
    grid_spec = pltpu.PrefetchScalarGridSpec(
        num_scalar_prefetch=1,
        grid=(3 + which,),
        in_specs=halves(width) + halves(grad.shape[1]) + [resident(weight.shape)]
        + anywhere(len(after)),
        out_specs=out_specs,
    )
    return pl.pallas_call(
        functools.partial(token_grad_kernel, which),
        grid_spec=grid_spec,
        out_shape=out_shape,
        compiler_params=params(44),
        cost_estimate=cost(9),
        name="token_grad",
    )(meta, sums, sums, grad, grad, weight, *after)


def place_moved_kernel(meta, own_ref, other_ref, *refs):
    docs_ref = refs[-1]

    @pl.when(meta[STAY] == 1)
    def _():
        docs_ref[0] = own_ref[...].astype(F32)

    @pl.when(meta[STAY] == 0)
    def _():
        docs_ref[0] = other_ref[...].astype(F32)


def place_moved(meta, docs, own, other, after=()):
    width = docs.shape[2]
    grid_spec = pltpu.PrefetchScalarGridSpec(
        num_scalar_prefetch=1,
        grid=(3,),
        in_specs=[pl.BlockSpec((TILE, width), lambda i, m: (i, 0))] * 2 + anywhere(1 + len(after)),
        out_specs=pl.BlockSpec((1, TILE, width), lambda i, m: (m[SLOT], i, 0)),
    )
    return pl.pallas_call(
        place_moved_kernel,
        grid_spec=grid_spec,
        out_shape=jax.ShapeDtypeStruct(docs.shape, F32),
        input_output_aliases={3: 0},
        compiler_params=params(16),
        cost_estimate=cost(4),
        name="place_moved",
    )(meta, own, other, docs, *after)


def plan_kernel(place, own_ref, across_ref, queries_ref, meta, table_block, counts, owner):
    core = place[0]
    half = BLOCK // 2
    number = [
        jnp.where(core == 0, own_ref[at], across_ref[at]) if at < 2
        else jnp.where(core == 0, across_ref[at - 2], own_ref[at - 2])
        for at in range(4)
    ]
    blocks = [(count + BLOCK - 1) // BLOCK for count in number]
    work = [count * (10 + count) for count in blocks]
    total = work[0] + work[1] + work[2] + work[3]
    loads = [jnp.maximum(work[0] + work[at], total - work[0] - work[at]) for at in (1, 2, 3)]
    plan = jnp.where(
        (loads[0] <= loads[1]) & (loads[0] <= loads[2]), 0, jnp.where(loads[1] <= loads[2], 1, 2)
    )
    stay = jnp.where(plan == 0, 1, 0)
    far_slot = jnp.where(plan == 1, 0, 1)
    slot = jnp.where(core == 0, 1, far_slot)
    slot_there = jnp.where(core == 0, far_slot, 1)
    first = jnp.where(slot == 1, own_ref[0], own_ref[1])
    here = jnp.where(slot == 1, own_ref[1], own_ref[0])
    there = jnp.where(slot_there == 1, across_ref[1], across_ref[0])
    second = jnp.where(stay == 1, here, there)
    first_blocks, second_blocks = (first + BLOCK - 1) // BLOCK, (second + BLOCK - 1) // BLOCK
    end = first_blocks + second_blocks
    device = place[3]
    other = jnp.where(core == 0, device + 1, device - 1)
    values = [
        0, first_blocks * BLOCK, end * BLOCK, first, second, queries_ref[0], queries_ref[1],
        first_blocks, second_blocks, (end + 2) // 2, core, place[1], place[2], slot, stay,
        2 * device, 2 * device + 1, 2 * device + 1 - slot,
        jnp.where(stay == 1, 2 * device + slot, 2 * other + slot_there),
    ]
    for at, value in enumerate(values):
        meta[at] = jnp.int32(value)
    for at in range(len(values), meta.shape[0]):
        meta[at] = 0
    for at in range(table_block.shape[0]):
        table_block[at] = jnp.where(
            at < first_blocks, at, jnp.where(at < end, at - first_blocks, 6)
        )
    for at in range(counts.shape[0]):
        in_first, in_second = at < 2 * first_blocks, at < 2 * end
        query = at - 2 * end
        count = jnp.where(
            in_first,
            first - at * half,
            jnp.where(
                in_second,
                second - (at - 2 * first_blocks) * half,
                jnp.where(query == 0, queries_ref[0], jnp.where(query == 1, queries_ref[1], 0)),
            ),
        )
        counts[at] = jnp.clip(count, 0, half)
        owner[at] = jnp.where(in_first, 2, jnp.where(in_second, 3, jnp.clip(query, 0, 1)))


def layout(place, doc_counts, across, query_counts, rows):
    smem = pl.BlockSpec(memory_space=pltpu.SMEM)
    half_blocks = rows // (BLOCK // 2)
    return pl.pallas_call(
        plan_kernel,
        in_specs=[smem] * 4,
        out_specs=[smem] * 4,
        out_shape=[
            jax.ShapeDtypeStruct((length,), jnp.int32)
            for length in (24, rows // BLOCK, half_blocks, half_blocks)
        ],
        cost_estimate=cost(1),
        name="plan",
    )(place, doc_counts, across, query_counts)


def pack_kernel(meta, docs, received, queries, out, sems):
    stay, slot = meta[STAY], meta[SLOT]

    def copies():
        for block in range(docs.shape[1] // BLOCK):
            lines = pl.ds(block * BLOCK, BLOCK)
            to = out.at[pl.ds(pl.multiple_of(meta[OFF1] + block * BLOCK, BLOCK), BLOCK)]
            second = block < meta[CNT1]
            yield block < meta[CNT0], docs.at[1 - slot, lines], out.at[lines], sems.at[0, block]
            yield second & (stay == 1), docs.at[slot, lines], to, sems.at[1, block]
            yield second & (stay == 0), received.at[lines], to, sems.at[2, block]
        end = pl.multiple_of(meta[OFFQ], BLOCK)
        yield None, queries, out.at[pl.ds(end, BLOCK)], sems.at[3, 0]

    out[pl.ds(pl.multiple_of(meta[OFFQ] + BLOCK, BLOCK), BLOCK), :] = jnp.zeros((BLOCK, out.shape[1]), out.dtype)
    for step in ("start", "wait"):
        for needed, source, to, sem in copies():
            copy = pltpu.make_async_copy(source, to, sem)
            if needed is None:
                getattr(copy, step)()
            else:
                pl.when(needed)(getattr(copy, step))


def pack_rows(meta, docs, received, queries, rows):
    width = docs.shape[2]
    return pl.pallas_call(
        pack_kernel,
        in_specs=[pl.BlockSpec(memory_space=pltpu.SMEM)] + anywhere(3),
        out_specs=pl.BlockSpec(memory_space=pltpu.VMEM),
        out_shape=jax.ShapeDtypeStruct((rows, width), docs.dtype),
        scratch_shapes=[pltpu.SemaphoreType.DMA((4, docs.shape[1] // BLOCK))],
        compiler_params=pltpu.CompilerParams(vmem_limit_bytes=16 * 1024 * 1024),
        cost_estimate=cost(2),
        name="pack",
    )(meta, docs, received, queries.reshape(BLOCK, width))


def by_row(shape, values):
    row = lax.broadcasted_iota(jnp.int32, shape, 0) % 4
    first, second, third, fourth = (jnp.full(shape, value) for value in values)
    return jnp.where(row == 0, first, jnp.where(row == 1, second, jnp.where(row == 2, third, fourth)))


def lengths_of(meta):
    lengths = by_row((8, 128), [meta[QLEN0], meta[QLEN1], meta[LEN0], meta[LEN1]])
    return lengths[:, 0:1].astype(F32)


def unit_kernel(meta, owner, index, weights, sums_ref, gain_ref, bias_ref, message_ref, pooled_ref, sums_out, recip_ref):
    rows, width = sums_ref.shape
    shape = (8, 128)
    lane = lax.broadcasted_iota(jnp.int32, shape, 1)
    weight = by_row(shape, [weights[0], weights[1], jnp.float32(0.0), jnp.float32(0.0)])
    high = jnp.floor(weight * 16.0)
    rest = (weight * 16.0 - high) * 256.0
    middle = jnp.floor(rest)
    lowest = jnp.floor((rest - middle) * 256.0)
    number = by_row(shape, [meta[IDS + at] for at in range(4)]).astype(F32)
    partner = by_row(shape, [index[0], index[1], jnp.int32(0), jnp.int32(0)]).astype(F32)
    extra = jnp.zeros(shape, F32)
    for at, value in enumerate((number, partner, high, middle, lowest)):
        extra = jnp.where(lane == at, value, extra)
    per_tile = TILE // (BLOCK // 2)
    line = lax.broadcasted_iota(jnp.int32, (8, rows), 0) % 4
    column = lax.broadcasted_iota(jnp.int32, (8, rows), 1)
    pick = jnp.zeros((8, rows), F32)
    for group in range(rows // 8 * per_tile):
        at = group // per_tile * 8 + group % per_tile
        here = (column == at) & (line == owner[group]) & (group // per_tile < meta[TILES])
        pick = jnp.where(here, 1.0, pick)
    lengths = lengths_of(meta)
    inside = lax.broadcasted_iota(jnp.int32, (rows, width), 0) < 8 * meta[TILES]
    sums = lax.dot_general(
        pick, jnp.where(inside, sums_ref[...], 0.0), (((1,), (0,)), ((), ())),
        precision=lax.Precision.HIGHEST, preferred_element_type=F32,
    )
    pooled = sums / lengths * gain_ref[...] + bias_ref[...]
    recip = lax.rsqrt(jnp.sum(pooled * pooled, axis=1, keepdims=True) + EPS_UNIT)
    unit = (pooled * recip).astype(BF16)
    half = width // 2
    upper = lax.broadcasted_iota(jnp.int32, (8, half), 0) < 4
    message_ref[:, :half] = jnp.where(upper, unit[:, :half].astype(F32), unit[:, half:].astype(F32)).astype(BF16)
    message_ref[:, half:] = extra.astype(BF16)
    pooled_ref[...] = pooled
    sums_out[...] = sums
    recip_ref[...] = jnp.broadcast_to(recip, recip_ref.shape)


def units(meta, owner, index, weights, sums, gain, bias):
    vmem = pl.BlockSpec(memory_space=pltpu.VMEM)
    width = sums.shape[1]
    return pl.pallas_call(
        unit_kernel,
        in_specs=[pl.BlockSpec(memory_space=pltpu.SMEM)] * 4 + [vmem] * 3,
        out_specs=[vmem] * 4,
        out_shape=[
            jax.ShapeDtypeStruct((8, width // 2 + 128), BF16),
            jax.ShapeDtypeStruct((8, width), F32),
            jax.ShapeDtypeStruct((8, width), F32),
            jax.ShapeDtypeStruct((8, 128), F32),
        ],
        compiler_params=pltpu.CompilerParams(vmem_limit_bytes=16 * 1024 * 1024),
        name="unit",
    )(meta, owner, index, weights, sums, gain, bias)


def loss_kernel(meta, softness, gain_ref, pooled_ref, sums_ref, recip_ref, *refs):
    loss_ref, scaled_ref, later_ref = refs[-3:]
    message = jnp.concatenate([ref[...] for ref in refs[:-3]], axis=0)
    rows, half = message.shape[0], message.shape[1] - 128
    pairs = rows // 4
    soft = softness[0]
    low = message[:, :half]
    extra = message[:, half:].astype(F32)
    row = lax.broadcasted_iota(jnp.int32, (rows, pairs), 0) % 8
    index = (extra[:, 0:1] + 0.5).astype(jnp.int32)
    found = lax.broadcasted_iota(jnp.int32, (rows, pairs), 1) == index
    of_query, of_doc = found & (row % 4 < 2), found & (row % 4 >= 2)

    def gathered(chosen):
        halves = [
            dot((chosen & (row // 4 == which)).astype(F32).astype(BF16), low, ((0,), (0,))) for which in range(2)
        ]
        return jnp.concatenate(halves, axis=1).astype(BF16)

    units_q, units_d = gathered(of_query), gathered(of_doc)
    exact = functools.partial(
        lax.dot_general, precision=lax.Precision.HIGHEST, preferred_element_type=F32
    )
    plain, turned, over_rows = (((1,), (0,)), ((), ())), (((1,), (1,)), ((), ())), (((0,), (0,)), ((), ()))
    extra = exact((of_query & (row < 4)).astype(F32), extra, over_rows)
    weight = extra[:, 2:3] / 16.0 + extra[:, 3:4] / 4096.0 + extra[:, 4:5] / 1048576.0
    similarity = dot(units_q, units_d, ((1,), (1,))) / soft
    columns = lax.broadcasted_iota(jnp.int32, similarity.shape, 1)
    target = (columns == (extra[:, 1:2] + 0.5).astype(jnp.int32)).astype(F32)
    highest = jnp.max(similarity, axis=1, keepdims=True)
    log_norm = highest + jnp.log(jnp.sum(jnp.exp(similarity - highest), axis=1, keepdims=True))
    picked = jnp.sum(target * similarity, axis=1, keepdims=True)
    loss = jnp.sum(weight * (log_norm - picked), axis=0, keepdims=True) / pairs
    loss_ref[...] = jnp.broadcast_to(loss, loss_ref.shape)
    grad = weight * (jnp.exp(similarity - log_norm) - target) / pairs
    line = lax.broadcasted_iota(jnp.int32, (8, pairs), 0)
    column = lax.broadcasted_iota(jnp.int32, (8, pairs), 1)
    my_queries = (column == jnp.where(line == 0, meta[IDS], meta[IDS + 1])) & (line < 2)
    my_docs = (column == jnp.where(line == 2, meta[IDS + 2], meta[IDS + 3])) & (line >= 2) & (line < 4)
    query_rows = exact(my_queries.astype(F32), grad, plain)
    doc_rows = exact(my_docs.astype(F32), grad, turned)
    grad_unit = (
        exact(query_rows, units_d.astype(F32), plain) + exact(doc_rows, units_q.astype(F32), plain)
    ) / soft
    pooled, recip, lengths = pooled_ref[...], recip_ref[:, 0:1], lengths_of(meta)
    crossed = jnp.sum(grad_unit * pooled, axis=1, keepdims=True)
    grad_rows = (recip * grad_unit - pooled * (recip * recip * recip) * crossed) / lengths
    first_half = lax.broadcasted_iota(jnp.int32, grad_rows.shape, 0)
    grad_rows = jnp.where(first_half < 4, grad_rows, 0.0)
    scaled_ref[...] = grad_rows * gain_ref[...]
    gain = jnp.sum(grad_rows * sums_ref[...], axis=0, keepdims=True)
    bias = jnp.sum(grad_rows * lengths, axis=0, keepdims=True)
    later_ref[...] = jnp.where(first_half == 2, gain, jnp.where(first_half == 3, bias, 0.0))


def loss_and_grads(meta, softness, gain, pooled, sums, recip, messages):
    width = pooled.shape[1]
    vmem = pl.BlockSpec(memory_space=pltpu.VMEM)
    return pl.pallas_call(
        loss_kernel,
        in_specs=[pl.BlockSpec(memory_space=pltpu.SMEM)] * 2 + [vmem] * (4 + len(messages)),
        out_specs=[vmem, vmem, vmem],
        out_shape=[
            jax.ShapeDtypeStruct((8, 128), F32),
            jax.ShapeDtypeStruct((8, width), F32),
            jax.ShapeDtypeStruct((8, width), F32),
        ],
        compiler_params=pltpu.CompilerParams(vmem_limit_bytes=24 * 1024 * 1024),
        name="loss",
    )(meta, softness, gain, pooled, sums, recip, *messages)


def wide_unfold_kernel(piece, *refs):
    gate_ref, up_ref, down_ref = refs[-3:]
    gate_ref[...] = piece[0, 0].astype(F32)
    up_ref[...] = piece[0, 1].astype(F32)
    span = piece.shape[3] // 2
    block = jnp.concatenate([piece[0, 2, :, :span], piece[0, 2, :, span:]], axis=0)
    down_ref[...] = block.astype(F32).T


def wide_unfold(chunk, pieces, before, width, inner, after=()):
    quarter, span = pieces.shape[2:]
    chunks = inner // (2 * span)
    place = pl.BlockSpec((quarter, span), lambda i: (i // 2, (i % 2) * chunks + chunk))
    return pl.pallas_call(
        wide_unfold_kernel,
        grid=(4,),
        in_specs=[pl.BlockSpec((1, *pieces.shape[1:]), lambda i: (i, 0, 0, 0))]
        + anywhere(len(before) + len(after)),
        out_specs=[
            place, place,
            pl.BlockSpec((span // 2, 2 * quarter), lambda i: (2 * chunk + i % 2, i // 2)),
        ],
        out_shape=[
            jax.ShapeDtypeStruct((width // 2, inner), F32),
            jax.ShapeDtypeStruct((width // 2, inner), F32),
            jax.ShapeDtypeStruct((inner // 2, width), F32),
        ],
        input_output_aliases={1 + at: at for at in range(len(before))},
        compiler_params=params(16),
        cost_estimate=cost(3),
        name="wide_unfold",
    )(pieces, *before, *after)


def wide_unfold_parts_kernel(meta, p00, p01, p10, p11, *refs):
    gate_ref, up_ref, down_ref = refs[-3:]
    for other_core in range(2):
        for other_row in range(2):
            piece = ((p00, p01), (p10, p11))[other_core][other_row]

            @pl.when((pl.program_id(0) == other_core) & (pl.program_id(1) == other_row))
            def _():
                gate_ref[...] = piece[0].astype(F32)
                up_ref[...] = piece[1].astype(F32)
                span = piece.shape[2] // 2
                block = jnp.concatenate([piece[2, :, :span], piece[2, :, span:]], axis=0)
                down_ref[...] = block.astype(F32).T


def wide_unfold_parts(meta, chunk, pieces, before, width, inner, after=()):
    quarter, span = pieces[0].shape[1:]
    chunks = inner // (2 * span)
    aliased = [pl.BlockSpec(memory_space=pl.ANY)] * len(before)
    grid_spec = pltpu.PrefetchScalarGridSpec(
        num_scalar_prefetch=1,
        grid=(2, 2),
        in_specs=[resident(p.shape) for p in pieces] + aliased + anywhere(len(after)),
        out_specs=[
            pl.BlockSpec(
                (quarter, span), lambda c, r, m: (m[ROW] ^ r, (m[CORE] ^ c) * chunks + chunk)
            )
            for _ in range(2)
        ]
        + [
            pl.BlockSpec(
                (span // 2, 2 * quarter), lambda c, r, m: (2 * chunk + (m[CORE] ^ c), m[ROW] ^ r)
            )
        ],
    )
    return pl.pallas_call(
        wide_unfold_parts_kernel,
        grid_spec=grid_spec,
        out_shape=[
            jax.ShapeDtypeStruct((width // 2, inner), F32),
            jax.ShapeDtypeStruct((width // 2, inner), F32),
            jax.ShapeDtypeStruct((inner // 2, width), F32),
        ],
        input_output_aliases={5 + at: at for at in range(len(before))},
        compiler_params=params(16),
        cost_estimate=cost(3),
        name="wide_unfold_parts",
    )(meta, *pieces, *before, *after)


AXES = ("fsdp", "blk")


class Links:
    def __init__(self, sides, blk):
        self.sides, self.blk, self.outer = sides, blk, blk // 4

    def swap(self, value, side=0, mask=0):
        pairs = [
            (f * self.blk + b, (f ^ side) * self.blk + (b ^ mask))
            for f in range(self.sides)
            for b in range(self.blk)
        ]
        return lax.ppermute(value, AXES, pairs)

    def core(self, value):
        return self.swap(value, mask=1)

    def row(self, value):
        return self.swap(value, mask=2)

    def side(self, value):
        return self.swap(value, side=1)

    def shift(self, value, by):
        pairs = [
            (f * self.blk + b, f * self.blk + (b + 4 * by) % self.blk)
            for f in range(self.sides)
            for b in range(self.blk)
        ]
        return lax.ppermute(value, AXES, pairs)

    def step(self, value, moves):
        pairs = [
            (f * self.blk + 4 * start + b, f * self.blk + 4 * end + b)
            for f in range(self.sides)
            for start, end in moves
            for b in range(4)
        ]
        return lax.ppermute(value, AXES, pairs)

    def outer_masks(self):
        mask = 4
        while mask < self.blk:
            yield mask
            mask *= 2

    def gather(self, value):
        both = jnp.concatenate([value, self.core(value)], axis=0)
        plane = jnp.concatenate(
            [both, self.swap(both, 1, 0), self.swap(both, 0, 2), self.swap(both, 1, 2)], axis=0
        )
        return [plane] + [self.shift(plane, by) for by in range(1, self.outer)]

    def stages(self, keep, send, row_first, by_swaps=False):
        add = lambda *terms: sum(term.astype(F32) for term in terms).astype(BF16)
        now = yield
        now = yield (send := tie(send, now))
        received = tie(self.core(send), now)
        if row_first:
            now = yield (away := add(keep[:, 1], received[:, 1]))
            across = tie(self.row(away), now)
            now = yield (away := add(keep[1, 0], received[1, 0], across[1]))
            last = self.side(away)
        else:
            now = yield (away := add(keep[1], received[1]))
            across = tie(self.side(away), now)
            now = yield (away := add(keep[0, 1], received[0, 1], across[1]))
            last = self.row(away)
        mine = add(keep[0, 0], received[0, 0], across[0], tie(last, now))
        if self.outer == 4:
            outer = lax.axis_index("blk") // 4
            now = yield mine
            mine = add(mine, tie(self.step(mine, ((0, 1), (3, 2))), now))
            now = yield mine
            mine = add(mine, tie(self.step(mine, ((1, 2), (2, 1))), now))
            now = yield mine
            result = tie(self.step(mine, ((1, 0), (2, 3))), now)
            mine = jnp.where((outer == 1) | (outer == 2), mine, result)
        else:
            for mask in self.outer_masks():
                now = yield mine
                mine = add(mine, tie(self.swap(mine, mask=mask), now))
        if by_swaps:
            now = yield mine
            other = tie(self.row(mine), now)
            yield other
            return mine, other, self.core(mine), self.core(other)
        groups = [[at + part for part in range(4)] for at in range(0, self.blk, 4)]
        flat = mine.reshape(-1, mine.shape[-1])
        gathered = lax.all_gather(flat, "blk", axis_index_groups=groups, axis=0, tiled=True)
        yield mine
        return gathered

    def stages_small(self, value):
        now = yield
        for side, mask in [(0, 1), (1, 0), (0, 2)] + [(0, mask) for mask in self.outer_masks()]:
            value = tie(value, now)
            now = yield value
            value = value + self.swap(value, side, mask)
        return value


def tie(value, now):
    return lax.optimization_barrier((value, now))[0]


class Flow:
    def __init__(self):
        self.sums, self.done = {}, {}

    def begin(self, name, stages):
        next(stages)
        self.sums[name] = stages

    def forward(self, now, *names):
        sent = []
        for name in names:
            if name in self.done:
                continue
            try:
                sent.append(self.sums[name].send(now))
            except StopIteration as end:
                self.done[name] = end.value
                if name == "s":
                    sent.append(end.value)
        return tuple(sent)

    def result(self, now, name):
        while name not in self.done:
            self.forward(now, name)
        return self.done[name]


def part_of(share, parts, at):
    size = share.shape[0] // parts
    return lax.dynamic_slice_in_dim(share, at * size, size, 0)


def body(
    question_activations,
    passage_activations,
    question_unpadded_counts,
    passage_unpadded_counts,
    correct_passage_index,
    query_weights,
    softness_factor,
    combined_projection_matrix,
    mixing_result_matrix,
    gating_matrix,
    widening_matrix,
    narrowing_matrix,
    initial_layernorm_scale,
    initial_layernorm_shift,
    later_layernorm_scale,
    later_layernorm_shift,
):
    doc_len, width = passage_activations.shape[1:]
    query_len = question_activations.shape[1]
    inner = gating_matrix.shape[1]
    assert passage_activations.shape[0] == 2 and doc_len == 6 * BLOCK and 2 * query_len == BLOCK
    links = Links(lax.axis_size("fsdp"), lax.axis_size("blk"))
    side, blk = lax.axis_index("fsdp"), lax.axis_index("blk")
    core, row = blk % 2, (blk // 2) % 2

    part_qkv = part_of(combined_projection_matrix, 2, core)
    got_qkv = links.side(part_qkv)
    quarter = row * 2 + core
    part_out = tie(part_of(mixing_result_matrix, 2, core), got_qkv)
    part_gate = tie(part_of(gating_matrix, 4, quarter), got_qkv)
    got_out, got_gate = links.side(part_out), links.side(part_gate)
    rows = -(-(2 * doc_len + BLOCK) // TILE) * TILE
    place = jnp.stack([core, side, row, side * links.blk + blk]).astype(jnp.int32)
    per_chip = tie(passage_unpadded_counts.astype(jnp.int32), part_qkv)
    query_counts = question_unpadded_counts.astype(jnp.int32)
    meta, table_block, counts, owner = layout(place, per_chip, links.core(per_chip), query_counts, rows)
    sent_doc = lax.dynamic_index_in_dim(passage_activations, meta[SLOT], 0, keepdims=False)
    tables = tuple(jnp.asarray(table) for table in rotary_tables(doc_len, query_len))
    x = pack_rows(meta, passage_activations, links.core(sent_doc), question_activations, rows)

    got_qkv = tie(got_qkv, x)
    pieces_qkv = (combined_projection_matrix, got_qkv, links.core(got_qkv))
    qkv, wqkv = project(meta, table_block, x, pieces_qkv, tables, (part_out, part_gate))
    own_vectors = tie(
        (initial_layernorm_scale, initial_layernorm_shift, later_layernorm_scale, later_layernorm_shift),
        qkv,
    )
    vectors = jnp.stack(own_vectors)
    others = links.side(vectors)
    vectors = jnp.concatenate(
        [jnp.where(side == 0, vectors, others), jnp.where(side == 0, others, vectors)], axis=1
    ).astype(F32)
    gain_one, bias_one, gain_two, bias_two = (vectors[at : at + 1] for at in range(4))
    part_up = tie(part_of(widening_matrix, 4, quarter), qkv)
    got_up = links.side(part_up)
    heads = attend(meta, qkv, 0, 2, (), (part_up,))
    got_out, got_gate = tie((got_out, got_gate), heads[1])
    part_down = tie(part_of(narrowing_matrix, 2, core), heads[1])
    far_out, along_gate, got_down = links.core(got_out), links.row(got_gate), links.side(part_down)
    heads = attend(meta, qkv, 1, 2, heads, (got_out, got_gate, part_down))
    along_gate, got_up = tie((along_gate, got_up), heads[1])
    far_gate = links.core(got_gate), links.core(along_gate)
    along_up = links.row(got_up)
    att, lse = attend(meta, qkv, 2, 2, heads, (far_out, along_gate, got_up, vectors))
    along_up, got_down = tie((along_up, got_down), lse)
    far_up, far_down = (links.core(got_up), links.core(along_up)), links.core(got_down)
    weights = [
        (mixing_result_matrix, got_out, far_out),
        (gating_matrix, got_gate, along_gate, *far_gate),
        (widening_matrix, got_up, along_up, *far_up),
        (narrowing_matrix, got_down, far_down),
    ]
    low, z1, r1, saved, z2, r2, sums, wo, wg, wu, wd = forward(
        meta, counts, att, x, weights, gain_one, bias_one
    )

    message, pooled, z_sums, recip = units(
        meta, owner, correct_passage_index.astype(jnp.int32), query_weights, sums, gain_two, bias_two
    )
    loss, scaled, later = loss_and_grads(
        meta, softness_factor, gain_two, pooled, z_sums, recip, links.gather(message)
    )
    flow = Flow()

    def wide(chunk, given, after):
        out, keep, send = ffn_back(
            meta, counts, owner, chunk, low, saved, wd, wg, wu, given, after
        )
        flow.begin("w%d" % chunk, links.stages(keep, send, chunk == 2, chunk == 2))
        return out, keep

    def score(pair, before, after):
        return attend_back(meta, pair, qkv, grad_att, att, lse, tables, before, after)

    def narrow(group, columns, at, extra, after):
        keep, send = qkv_grad(meta, x, grads, columns, at, extra, after)
        flow.begin("q%d" % group, links.stages(keep, send, group == 0))
        return keep

    head, now = wide(0, (z2, r2, scaled), ())
    tail, now = wide(1, (head,), flow.forward(now, "w0"))
    tail, now = wide(2, (head, tail), flow.forward(now, "w0", "w1"))
    sum_one, grad_att, now, *mixing = norm_one_back(
        meta, (head, tail), z1, r1, att, gain_one, wo, later, flow.forward(now, "w0", "w1", "w2")
    )
    flow.begin("s", links.stages_small(now))
    grads = score(0, (), flow.forward(now, "w0", "w2"))
    grads = score(1, (grads,), flow.forward(grads, "w0"))
    grads = score(2, (grads,), flow.forward(grads, "w0", "w1"))
    grads = score(3, (grads,), flow.forward(grads, "w0", "w2"))
    now = narrow(0, 1536, 0, mixing, flow.forward(grads, "w1"))
    grads = score(4, (grads,), flow.forward(now, "w1", "w2", "q0"))
    now = grads = score(5, (grads,), flow.forward(grads, "w0", "w1", "w2", "q0"))
    unfold = lambda chunk, before, after: wide_unfold(
        chunk, flow.result(now, "w%d" % chunk).reshape(4, 3, width // 4, -1), before, width, inner, after
    )
    grad_wide = unfold(0, (), ())
    now = narrow(1, 768, 2, (), (*flow.forward(now, "w1", "w2"), grad_wide[0]))
    (grad_docs,) = token_grad(
        0, meta, sum_one, grads, wqkv, flow.forward(now, "w2", "q0", "q1", "s")
    )
    moved, grad_queries = token_grad(
        1, meta, sum_one, grads, wqkv, (grad_docs, *flow.forward(grad_docs, "q0", "q1", "s"))
    )
    other_moved = links.core(moved)
    grad_wide = unfold(1, grad_wide, flow.forward(moved, "w1", "w2", "q0", "q1", "s"))
    now = grad_wide[0]
    grad_docs = place_moved(
        meta, grad_docs, moved, other_moved, (now, *flow.forward(now, "w2", "q0", "q1", "s"))
    )
    after = flow.forward(grad_docs, "q0", "q1", "s")
    grad_wide = wide_unfold_parts(
        meta, 2, flow.result(grad_docs, "w2"), grad_wide, width, inner, (grad_docs, *after)
    )
    while len(flow.done) < 6:
        flow.forward(moved, "q0", "q1", "s")
    first_part, second_part = flow.done["q0"], flow.done["q1"]
    joint = first_part.shape[1] - width
    grad_qkv = jnp.concatenate(
        [
            part.astype(F32)
            for parts in zip(jnp.split(first_part[:, :joint], 3, axis=1), jnp.split(second_part, 3, axis=1))
            for part in parts
        ],
        axis=1,
    )
    grad_out = first_part[:, joint:].astype(F32)
    small = lax.dynamic_slice_in_dim(flow.done["s"], side * (width // 2), width // 2, 1)
    return (
        loss[0, :1],
        grad_queries,
        grad_docs,
        grad_qkv,
        grad_out,
        grad_wide[0],
        grad_wide[1],
        grad_wide[2],
        small[0],
        small[1],
        small[2],
        small[3],
    )


def solution(mesh):
    placed = (
        P(("fsdp", "blk"), None, None),
        P(("fsdp", "blk"), None, None),
        P(("fsdp", "blk")),
        P(("fsdp", "blk")),
        P(("fsdp", "blk")),
        P(("fsdp", "blk")),
        P(),
        P("fsdp", None),
        P("fsdp", None),
        P("fsdp", None),
        P("fsdp", None),
        P("fsdp", None),
        P("fsdp"),
        P("fsdp"),
        P("fsdp"),
        P("fsdp"),
    )
    return jax.shard_map(
        body,
        mesh=mesh,
        in_specs=placed,
        out_specs=(
            P(),
            P(("fsdp", "blk"), None, None),
            P(("fsdp", "blk"), None, None),
            P("fsdp", None),
            P("fsdp", None),
            P("fsdp", None),
            P("fsdp", None),
            P("fsdp", None),
            P("fsdp"),
            P("fsdp"),
            P("fsdp"),
            P("fsdp"),
        ),
        check_vma=False,
    )
```
